128 devices in a mesh: pw: 32 (over z_hi, y, x), band: 4 (over z_lo, core).
Axes of the slice: x: 4, y: 4, z: 4 (z_hi: 2, z_lo: 2; z = z_hi * 2 + z_lo), core: 2. Of those that a mesh axis runs over, the one named last changes fastest.
Arguments:
- wave_coef: float32 [2, 4, 524288], P(None, 'band', 'pw'), may hold values from -6 to 6
- projector: float32 [2, 64, 524288], P(None, None, 'pw'), may hold values from -0.109375 to 0.109375
- potential: float32 [256, 256, 256], P('pw'), may hold values from -8 to 8
- grid_slot: int32 [524288], P('pw'), may hold values from 0 to 98303, as said below
- stick_column: int32 [12288], replicated, may hold values from 0 to 65535, as said below
- proj_atom: int32 [64], replicated, may hold values from 0 to 15, never falling along the last dimension, each value on 1 to 8 neighbouring positions
- coupling: float32 [64, 64], replicated, may hold values from -6 to 6
Outputs:
- applied: float32 [2, 4, 524288], P(None, 'band', 'pw')
- subspace_h: float32 [2, 4, 4], P(None, None, 'band')
- correlation: float32 [2, 4, 4], P(None, None, 'band')
The draws below stay inside these ranges and needn't reach their ends.
Inputs may be any that keep to these rules, and one draw needn't show every extreme that they name: `grid_slot`: within each aligned block of 16384 entries (the coefficients of one pw index) the values are distinct. `stick_column`: all values are distinct. `proj_atom`: never falling; each atom has 1 to 8 projectors.
All inputs are finite; a program needn't handle non-finite values.
Results may differ from the reference program's by a relative error of at most 0.000058.
Values sent between devices are 32-bit elements; how exact they have to be, the bound alone decides.
No kernel may reach another device: no remote copies, remote signals or barrier semaphores. Data moves between devices by JAX's collectives and lax.ppermute only.
A program may use at most 192 MiB of HBM per device.

```python
import math
import jax
import jax.numpy as jnp
import numpy as np
from jax import lax

GX = 256
GY = 256
GZ = 256
STICKS_DEV = 384
COEF_DEV = 16384
PROJ = 64
MOST = 8
ATOMS = 16
BANDS = 4
STICKS = 12288
COEFS = 524288


def pick_distinct(key, extent, needed):
    middle = jax.random.permutation(jax.random.fold_in(key, 1), extent - 2) + 1
    chosen = jnp.concatenate([jnp.array([0, extent - 1], jnp.int32), middle[:needed - 2].astype(jnp.int32)])
    shuffle = jax.random.permutation(jax.random.fold_in(key, 2), needed)
    return chosen[shuffle]


def draw_grid_slot(key, part):
    blocks = COEFS // COEF_DEV

    def one_block(position):
        return pick_distinct(jax.random.fold_in(key, position + 7), STICKS_DEV * GZ, COEF_DEV)
    return jax.vmap(one_block)(jnp.arange(blocks, dtype=jnp.int32)).reshape(-1)


def draw_stick_column(key, part):
    return pick_distinct(jax.random.fold_in(key, 3), GX * GY, STICKS)


def steps_of(rng, shape, split, smallest, largest):
    def one(axis_at, shards_of):
        heights = jax.random.uniform(jax.random.fold_in(jax.random.fold_in(rng, 6), axis_at), (shards_of,), jnp.float32, smallest / len(split), largest / len(split))
        return jnp.repeat(jnp.exp(heights), shape[axis_at] // shards_of).reshape((-1,) + (1,) * (len(shape) - axis_at - 1))

    level = one(*split[0])
    for cut in split[1:]:
        level = level * one(*cut)
    return level


def split_up(count, total, bound, slope):
    weights = [(1 << 20) // math.isqrt(standing ** slope) + 1 for standing in range(2, count + 1)]
    spare, holding = total - bound - (count - 1), [1] * (count - 1)
    while spare > 0:
        free = [i for i in range(count - 1) if holding[i] < bound]
        mass, budget = sum([weights[i] for i in free]), spare
        for i in free:
            extra = min(bound - holding[i], max(1, budget * weights[i] // mass), spare)
            holding[i] = holding[i] + extra
            spare = spare - extra
    return np.array([bound] + holding)


def ragged(own_key, amount, total, most, slope):
    if amount == 2:
        one = jax.random.randint(own_key, (), max(1, total - most), min(most, total - 1) + 1)
        return jnp.stack([one, total - one])
    lengths = jnp.asarray(split_up(amount, total, most, slope), jnp.int32)
    twos = (amount - 1) // 2
    source_of, receiver = lengths[1:1 + 2 * twos:2], lengths[2:2 + 2 * twos:2]
    margin = jnp.minimum(source_of - 1, most - receiver)
    moved = jax.random.randint(jax.random.fold_in(own_key, 1), (twos,), 0, 1 << 20) % (margin + 1)
    lengths = lengths.at[1:1 + 2 * twos:2].set(source_of - moved).at[2:2 + 2 * twos:2].set(receiver + moved)
    return lengths[jax.random.permutation(jax.random.fold_in(own_key, 2), amount)]


def scatter_about(stream_key, shape, width, bound, shards=(), kind=jnp.bfloat16):
    values = jax.random.normal(stream_key, shape, jnp.float32) * width
    if len(shards) > 0:
        values = steps_of(stream_key, shape, shards, -0.22, 0.18) * values
    return jnp.clip(values, min=-bound, max=bound).astype(kind)


def setup_inputs(seed: int = 0) -> dict:
    key_list = jax.random.split(jax.random.key(seed), 8)
    return {
        "wave_coef": scatter_about(key_list[0], (2, BANDS, COEFS), 1.0, 6.0, ((1, 4), (2, 32)), jnp.float32),
        "projector": scatter_about(key_list[1], (2, PROJ, COEFS), (0.55 / (PROJ * COEFS) ** 0.25), 0.109375, ((2, 32),), jnp.float32),
        "potential": scatter_about(key_list[2], (GZ, GX, GY), 2.0, 8.0, ((0, 32),), jnp.float32),
        "grid_slot": draw_grid_slot(jax.random.fold_in(key_list[7], 71), 0),
        "stick_column": draw_stick_column(jax.random.fold_in(key_list[7], 71), 0),
        "proj_atom": jnp.searchsorted(jnp.cumsum(ragged(key_list[5], ATOMS, PROJ, MOST, 1)), jnp.arange(PROJ), side="right").astype(jnp.int32),
        "coupling": scatter_about(key_list[6], (PROJ, PROJ), 1.0, 6.0, (), jnp.float32),
    }


KIN_MAX = 2.0
PRECISE = lax.Precision.HIGHEST


def centred(values, length):
    return jnp.where(values < length // 2, values, values - length)


def kinetic_of(x_cell, y_cell, z_cell):
    x_freq = centred(x_cell, GX).astype(jnp.float32) / (GX / 2)
    y_freq = centred(y_cell, GY).astype(jnp.float32) / (GY / 2)
    z_freq = centred(z_cell, GZ).astype(jnp.float32) / (GZ / 2)
    return KIN_MAX * (x_freq * x_freq + y_freq * y_freq + z_freq * z_freq) / 3.0


def contract(left, right):
    return jnp.einsum('ig,bg->ib', left, right, precision=PRECISE)


def expand(coeffs, basis):
    return jnp.einsum('ib,ig->bg', coeffs, basis, precision=PRECISE)


def gram(left, right):
    real_part = jnp.einsum('ig,jg->ij', left[0], right[0], precision=PRECISE) + jnp.einsum('ig,jg->ij', left[1], right[1], precision=PRECISE)
    imag_part = jnp.einsum('ig,jg->ij', left[0], right[1], precision=PRECISE) - jnp.einsum('ig,jg->ij', left[1], right[0], precision=PRECISE)
    return jnp.stack([real_part, imag_part])


def reference(wave_coef, projector, potential, grid_slot, stick_column, proj_atom, coupling):
    device = jnp.arange(COEFS, dtype=jnp.int32) // COEF_DEV
    z_cell = grid_slot // STICKS_DEV
    stick_id = device * STICKS_DEV + grid_slot % STICKS_DEV
    column = stick_column[stick_id]
    x_cell = column // GY
    y_cell = column % GY
    kinetic = kinetic_of(x_cell, y_cell, z_cell)
    flat_cell = (x_cell * GY + y_cell) * GZ + z_cell
    field_xyz = jnp.transpose(potential, (1, 2, 0))

    def one_band(parts):
        complex_coef = parts[0] + 1j * parts[1]
        lattice = jnp.zeros((GX * GY * GZ,), complex_coef.dtype).at[flat_cell].set(complex_coef).reshape(GX, GY, GZ)
        result = jnp.fft.fftn(field_xyz * jnp.fft.ifftn(lattice)).reshape(-1)[flat_cell]
        return jnp.stack([jnp.real(result), jnp.imag(result)])

    local_term = jnp.transpose(lax.map(one_band, jnp.transpose(wave_coef, (1, 0, 2))), (1, 0, 2))
    becp_real = contract(projector[0], wave_coef[0]) + contract(projector[1], wave_coef[1])
    becp_imag = contract(projector[0], wave_coef[1]) - contract(projector[1], wave_coef[0])
    same_atom = proj_atom[:, None] == proj_atom[None, :]
    matrix = jnp.where(same_atom, 0.5 * (coupling + coupling.T), 0.0)
    coupled_real = jnp.dot(matrix, becp_real, precision=PRECISE)
    coupled_imag = jnp.dot(matrix, becp_imag, precision=PRECISE)
    nonlocal_real = expand(coupled_real, projector[0]) - expand(coupled_imag, projector[1])
    nonlocal_imag = expand(coupled_imag, projector[0]) + expand(coupled_real, projector[1])
    nonlocal_term = jnp.stack([nonlocal_real, nonlocal_imag])
    applied = kinetic[None, None, :] * wave_coef + local_term + nonlocal_term
    return applied, gram(wave_coef, applied), gram(wave_coef, wave_coef)
```

```python
import functools

import jax
import jax.numpy as jnp
import ml_dtypes
import numpy as np
from jax import lax
from jax.experimental import pallas as pl
from jax.experimental.pallas import tpu as pltpu
from jax.sharding import PartitionSpec as P

GX = 256
GY = 256
GZ = 256
KIN_MAX = 2.0
PRECISE = lax.Precision.HIGHEST

PW = 32
STICKS = 384
COEFS = 16384
PROJ = 64
PLANES = GZ // PW
ROWS = 2 * PLANES
KC = 1024
TILES = STICKS // 128
BLOCKS = 48
XC = 16
F32 = jnp.float32
BF16 = jnp.bfloat16
NN = (((1,), (0,)), ((), ()))
NT = (((1,), (1,)), ((), ()))


def mm(left, right, dims=NN):
    return lax.dot_general(left, right, dims, preferred_element_type=F32)


def split(value):
    high = value.astype(BF16)
    low = (value - high.astype(F32)).astype(BF16)
    return high, low


def split_table(table):
    high = table.astype(np.float32).astype(ml_dtypes.bfloat16)
    low = (table - high.astype(np.float64)).astype(np.float32).astype(ml_dtypes.bfloat16)
    return high, low


def trig():
    n = np.arange(256)
    angle = 2.0 * np.pi * (np.outer(n, n) % 256) / 256.0
    return np.cos(angle), np.sin(angle)


def plane_tables():
    c, s = trig()
    high, low = split_table(np.concatenate([c, s], axis=0))
    left = np.concatenate([high, low, high], axis=1)
    return left, np.ascontiguousarray(left.T)


def spread_table():
    c, s = trig()
    rows = np.concatenate(
        [np.concatenate([np.concatenate([c[z], -s[z]])[None] if part == 0 else np.concatenate([s[z], c[z]])[None]
                         for z in range(d * PLANES, (d + 1) * PLANES)])
         for d in range(PW) for part in range(2)])
    high, low = split_table(rows)
    return np.concatenate([high, low, high], axis=1)


def collect_table():
    c, s = trig()
    full = np.zeros((512, 512))
    for d in range(PW):
        zs = np.arange(d * PLANES, (d + 1) * PLANES)
        at = d * ROWS
        full[:256, at:at + PLANES] = c[:, zs]
        full[:256, at + PLANES:at + ROWS] = s[:, zs]
        full[256:, at:at + PLANES] = -s[:, zs]
        full[256:, at + PLANES:at + ROWS] = c[:, zs]
    high, low = split_table(full)
    return np.concatenate([high, low, high], axis=1)


def iota(shape, dim):
    return lax.broadcasted_iota(jnp.int32, shape, dim).astype(F32)


def slot_parts(slot):
    slot = slot.astype(F32)
    z = jnp.floor((slot + 0.5) * (1.0 / STICKS))
    return z, slot - z * STICKS


def rank_of(owned):
    wide = jnp.broadcast_to(owned, (128, STICKS))
    down = jnp.transpose(wide)[:, :1]
    rank_row = jnp.sum(jnp.where(down < owned, 1.0, 0.0), axis=0, keepdims=True)
    order = jnp.where(iota((STICKS, STICKS), 0) == rank_row, 1.0, 0.0)
    rank_col = jnp.sum(jnp.where(owned < down, 1.0, 0.0), axis=1, keepdims=True)
    ordered = jnp.sum(jnp.where(iota((STICKS, STICKS), 1) == rank_col, down, 0.0), axis=0, keepdims=True)
    return order, ordered


def spread_kernel(slot_ref, coef_ref, proj_ref, owned_ref, table_ref, out_ref, acc, becp):
    step = pl.program_id(0)

    @pl.when(step == 0)
    def _():
        acc[...] = jnp.zeros_like(acc)
        becp[...] = jnp.zeros_like(becp)

    z, s = slot_parts(slot_ref[...])
    c_re = coef_ref[0]
    c_im = coef_ref[1]
    re_hi, re_lo = split(c_re)
    im_hi, im_lo = split(c_im)
    z_hot = iota((GZ, KC), 0).astype(BF16) == z.astype(BF16)
    none = jnp.zeros((), BF16)
    placed = jnp.concatenate(
        [jnp.where(z_hot, part, none) for part in (re_hi, im_hi, re_lo, im_lo)], axis=0)
    s_hot = jnp.where(
        (iota((STICKS, KC), 0) - 192.0).astype(BF16) == (s - 192.0).astype(BF16), jnp.ones((), BF16), none)
    acc[...] += mm(s_hot, placed, NT)

    p_re = proj_ref[0]
    p_im = proj_ref[1]
    real = p_re * c_re + p_im * c_im
    imag = p_re * c_im - p_im * c_re
    both = jnp.concatenate([real, imag], axis=0)
    total = both[:, :128]
    for at in range(128, KC, 128):
        total = total + both[:, at:at + 128]
    becp[...] += total

    @pl.when(step == pl.num_programs(0) - 1)
    def _():
        order, ordered = rank_of(owned_ref[...].astype(F32))
        sticks = mm(order.astype(BF16), acc[...].astype(BF16)).astype(BF16)
        high = sticks[:, :512]
        low = sticks[:, 512:]
        spread = mm(table_ref[...], jnp.concatenate([high, high, low], axis=1), NT)
        spread = spread.reshape(PW, ROWS, STICKS)
        for t in range(TILES):
            out_ref[:, t * ROWS:(t + 1) * ROWS, :] = spread[:, :, t * 128:(t + 1) * 128]
        line = jnp.sum(jnp.transpose(becp[...]), axis=0, keepdims=True)
        extra = jnp.concatenate(
            [line] + [ordered[:, t * 128:(t + 1) * 128] for t in range(TILES)] + [jnp.zeros((4, 128), F32)], axis=0)
        out_ref[:, TILES * ROWS:, :] = jnp.broadcast_to(extra[None], (PW, 8, 128))


def spread_sticks(slot, coef, proj, owned):
    table = jnp.asarray(spread_table())
    return pl.pallas_call(
        spread_kernel,
        grid=(COEFS // KC,),
        in_specs=[
            pl.BlockSpec((1, KC), lambda i: (0, i)),
            pl.BlockSpec((2, 1, KC), lambda i: (0, 0, i)),
            pl.BlockSpec((2, PROJ, KC), lambda i: (0, 0, i)),
            pl.BlockSpec((1, STICKS), lambda i: (0, 0)),
            pl.BlockSpec((512, 1536), lambda i: (0, 0)),
        ],
        out_specs=pl.BlockSpec((PW, 56, 128), lambda i: (0, 0, 0)),
        out_shape=jax.ShapeDtypeStruct((PW, 56, 128), F32),
        scratch_shapes=[pltpu.VMEM((STICKS, 1024), F32), pltpu.VMEM((128, 128), F32)],
        compiler_params=pltpu.CompilerParams(vmem_limit_bytes=48 << 20),
        name="spread_sticks",
    )(slot, coef, proj, owned, table)


def swap_chunks(parts):
    parts = list(parts)
    chunk = lax.broadcasted_iota(jnp.int32, parts[0].shape, 1) // 16
    for bit in (1, 2, 4):
        here = (chunk & bit) == 0
        for a in range(8):
            if a & bit:
                continue
            one, two = parts[a], parts[a | bit]
            parts[a] = jnp.where(here, one, pltpu.roll(two, 16 * bit, 1))
            parts[a | bit] = jnp.where(here, pltpu.roll(one, 128 - 16 * bit, 1), two)
    return parts


def field_kernel(range_ref, recv_ref, field_ref, left_ref, right_ref, out_ref, sticks, cells, grid, done):
    for t in range(TILES):
        for g in range(4):
            mixed = swap_chunks([recv_ref[g * 8 + i, t * ROWS:(t + 1) * ROWS, :] for i in range(8)])
            for c in range(8):
                sticks[(t * 8 + c) * 2 + g // 2, :, (g % 2) * 128:(g % 2) * 128 + 128] = mixed[c]
    for g in range(4):
        mixed = swap_chunks([recv_ref[g * 8 + i, TILES * ROWS:, :] for i in range(8)])
        for c in range(8):
            for t in range(TILES):
                cells[(t * 8 + c) * 2 + g // 2, :, (g % 2) * 128:(g % 2) * 128 + 128] = jnp.broadcast_to(
                    mixed[c][1 + t:2 + t], (8, 128))

    grid[...] = jnp.zeros_like(grid)

    def cell_of(b):
        cell = cells[b][:1]
        x = jnp.floor(cell * (1.0 / GY))
        y = cell - x * GY
        hot = jnp.where(iota((GY, 256), 0).astype(BF16) == y.astype(BF16), jnp.ones((), BF16), jnp.zeros((), BF16))
        return x, hot

    def place(b, carry):
        x, hot = cell_of(b)
        high, low = split(sticks[b])
        both = jnp.concatenate([high.astype(F32), low.astype(F32)], axis=0)
        wide = jnp.broadcast_to(both[:, None, :], (2 * ROWS, XC, 256)).astype(BF16)

        def one(at, inner):
            first = at * XC
            mine = (iota((XC, 256), 0) + first.astype(F32)).astype(BF16) == x.astype(BF16)
            masked = jnp.where(mine[None], wide, jnp.zeros((), BF16)).reshape(2 * ROWS * XC, 256)
            added = mm(masked, hot, NT).reshape(2, ROWS, XC, 256)
            here = pl.ds(pl.multiple_of(first, XC), XC)
            grid[:, here, :] += added[0] + added[1]
            return inner

        return lax.fori_loop(range_ref[b, 0], range_ref[b, 1] + 1, one, carry)

    lax.fori_loop(0, BLOCKS, place, 0)

    def plane(zz, carry):
        re = grid[zz]
        im = grid[PLANES + zz]

        def along_y(re, im):
            high, low = split(jnp.concatenate([re, im], axis=0))
            return mm(jnp.concatenate([high, high, low], axis=1), right_ref[...])

        def along_x(re, im):
            high, low = split(jnp.concatenate([re, im], axis=1))
            return mm(left_ref[...], jnp.concatenate([high, high, low], axis=0))

        got = along_y(re, im)
        re = got[:256, :256] - got[256:, 256:]
        im = got[:256, 256:] + got[256:, :256]
        got = along_x(re, im)
        re = got[:256, :256] - got[256:, 256:]
        im = got[256:, :256] + got[:256, 256:]
        field = field_ref[zz]
        re = re * field
        im = im * field
        got = along_x(re, im)
        re = got[:256, :256] + got[256:, 256:]
        im = got[:256, 256:] - got[256:, :256]
        got = along_y(re, im)
        re = got[:256, :256] + got[256:, 256:]
        im = got[256:, :256] - got[:256, 256:]
        high, low = split(re)
        done[zz, :, :256] = high
        done[zz, :, 256:] = low
        high, low = split(im)
        done[PLANES + zz, :, :256] = high
        done[PLANES + zz, :, 256:] = low
        return carry

    lax.fori_loop(0, PLANES, plane, 0)

    def pick(b, carry):
        x, hot = cell_of(b)
        hot = jnp.concatenate([hot, hot], axis=0)

        def one(at, total):
            first = at * XC
            mine = (iota((XC, 256), 0) + first.astype(F32)) == x
            here = pl.ds(pl.multiple_of(first, XC), XC)
            lines = done[:, here, :].reshape(ROWS * XC, 512)
            got = mm(lines, hot).reshape(ROWS, XC, 256)
            got = jnp.where(mine[None], got, 0.0)
            return total + got[:, :8] + got[:, 8:]

        total = lax.fori_loop(range_ref[b, 0], range_ref[b, 1] + 1, one, jnp.zeros((ROWS, 8, 256), F32))
        sticks[b] = jnp.sum(total, axis=1)
        return carry

    lax.fori_loop(0, BLOCKS, pick, 0)

    for t in range(TILES):
        for g in range(4):
            mixed = swap_chunks(
                [sticks[(t * 8 + c) * 2 + g // 2, :, (g % 2) * 128:(g % 2) * 128 + 128] for c in range(8)])
            for i in range(8):
                out_ref[g * 8 + i, t * ROWS:(t + 1) * ROWS, :] = mixed[i]


def apply_field(ranges, recv, field):
    left, right = plane_tables()
    vmem = pl.BlockSpec(memory_space=pltpu.VMEM)
    return pl.pallas_call(
        field_kernel,
        in_specs=[pl.BlockSpec(memory_space=pltpu.SMEM), vmem, vmem, vmem, vmem],
        out_specs=vmem,
        out_shape=jax.ShapeDtypeStruct((PW, 48, 128), F32),
        scratch_shapes=[
            pltpu.VMEM((BLOCKS, ROWS, 256), F32),
            pltpu.VMEM((BLOCKS, 8, 256), F32),
            pltpu.VMEM((ROWS, GX, GY), F32),
            pltpu.VMEM((ROWS, GX, 2 * GY), BF16),
        ],
        compiler_params=pltpu.CompilerParams(vmem_limit_bytes=56 << 20),
        name="apply_field",
    )(ranges, recv, field, jnp.asarray(left), jnp.asarray(right))


def centred(values, length):
    return jnp.where(values < length // 2, values, values - length)


def collect_kernel(slot_ref, coef_ref, all_ref, proj_ref, recv_ref, owned_ref, coupled_ref, table_ref,
                   out_ref, sums_ref, values, sums):
    step = pl.program_id(0)

    @pl.when(step == 0)
    def _():
        sums[...] = jnp.zeros_like(sums)
        owned = owned_ref[...].astype(F32)
        order, _ = rank_of(owned)
        order = order.astype(BF16)
        lines = jnp.concatenate(
            [recv_ref[:, t * ROWS:(t + 1) * ROWS, :].reshape(512, 128) for t in range(TILES)], axis=1)
        high, low = split(lines)
        back = mm(table_ref[...], jnp.concatenate([high, high, low], axis=0))
        high, low = split(back)
        values[:512, :STICKS] = mm(high, order).astype(BF16)
        values[:512, STICKS:] = mm(low, order).astype(BF16)
        x = jnp.floor(owned * (1.0 / GY))
        y = centred(owned - x * GY, GY)
        x = centred(x, GX)
        square = x * x + y * y
        upper = jnp.floor(square * (1.0 / 256.0))
        lower = square - upper * 256.0
        pair = jnp.concatenate([upper, lower, jnp.zeros((14, STICKS), F32)], axis=0)
        values[512:, :STICKS] = pair.astype(BF16)
        values[512:, STICKS:] = jnp.zeros((16, STICKS), BF16)

    z, s = slot_parts(slot_ref[...])
    none = jnp.zeros((), BF16)
    s_hot = jnp.where(
        (iota((STICKS, KC), 0) - 192.0).astype(BF16) == (s - 192.0).astype(BF16), jnp.ones((), BF16), none)
    found = mm(values[...], jnp.concatenate([s_hot, s_hot], axis=0))
    z_hot = iota((GZ, KC), 0) == z
    scale = 1.0 / (GX * GY * GZ)
    local_re = jnp.sum(jnp.where(z_hot, found[:256], 0.0), axis=0, keepdims=True) * scale
    local_im = jnp.sum(jnp.where(z_hot, found[256:512], 0.0), axis=0, keepdims=True) * scale
    z = centred(z, GZ)
    square = found[512:513] * 256.0 + found[513:514] + z * z
    kinetic = square * (KIN_MAX / 3.0 / 16384.0)
    c_re = coef_ref[0]
    c_im = coef_ref[1]
    p_re = proj_ref[0]
    p_im = proj_ref[1]
    w_re = coupled_ref[0]
    w_im = coupled_ref[1]
    far_re = jnp.sum(p_re * w_re - p_im * w_im, axis=0, keepdims=True)
    far_im = jnp.sum(p_re * w_im + p_im * w_re, axis=0, keepdims=True)
    h_re = kinetic * c_re + local_re + far_re
    h_im = kinetic * c_im + local_im + far_im
    out_ref[0] = h_re
    out_ref[1] = h_im
    a_re = all_ref[0]
    a_im = all_ref[1]
    sums[0] += a_re * h_re + a_im * h_im
    sums[1] += a_re * h_im - a_im * h_re
    sums[2] += a_re * c_re + a_im * c_im
    sums[3] += a_re * c_im - a_im * c_re

    @pl.when(step == pl.num_programs(0) - 1)
    def _():
        sums_ref[...] = jnp.broadcast_to(jnp.sum(sums[...], axis=2, keepdims=True), (4, 4, 128))


def collect(slot, coef, everyone, proj, recv, owned, coupled):
    table = jnp.asarray(collect_table())
    return pl.pallas_call(
        collect_kernel,
        grid=(COEFS // KC,),
        in_specs=[
            pl.BlockSpec((1, KC), lambda i: (0, i)),
            pl.BlockSpec((2, 1, KC), lambda i: (0, 0, i)),
            pl.BlockSpec((2, 4, KC), lambda i: (0, 0, i)),
            pl.BlockSpec((2, PROJ, KC), lambda i: (0, 0, i)),
            pl.BlockSpec((PW, 48, 128), lambda i: (0, 0, 0)),
            pl.BlockSpec((1, STICKS), lambda i: (0, 0)),
            pl.BlockSpec((2, PROJ, 1), lambda i: (0, 0, 0)),
            pl.BlockSpec((512, 1536), lambda i: (0, 0)),
        ],
        out_specs=[
            pl.BlockSpec((2, 1, KC), lambda i: (0, 0, i)),
            pl.BlockSpec((4, 4, 128), lambda i: (0, 0, 0)),
        ],
        out_shape=[
            jax.ShapeDtypeStruct((2, 1, COEFS), F32),
            jax.ShapeDtypeStruct((4, 4, 128), F32),
        ],
        scratch_shapes=[pltpu.VMEM((528, 2 * STICKS), BF16), pltpu.VMEM((4, 4, KC), F32)],
        compiler_params=pltpu.CompilerParams(vmem_limit_bytes=48 << 20),
        name="collect",
    )(slot, coef, everyone, proj, recv, owned, coupled, table)


def local(wave_coef, projector, potential, grid_slot, stick_column, proj_atom, coupling):
    owned = lax.dynamic_slice_in_dim(stick_column, lax.axis_index("pw") * STICKS, STICKS).reshape(1, STICKS)
    slot = grid_slot.reshape(1, COEFS)
    everyone = lax.all_gather(wave_coef, "band", axis=1, tiled=True)
    sent = spread_sticks(slot, wave_coef, projector, owned)
    recv = lax.all_to_all(sent, "pw", split_axis=0, concat_axis=0, tiled=True)

    rows = recv[:, 49:52, :].reshape(2, 16, TILES, 8, 16)
    rows = jnp.floor(rows * (1.0 / (GY * XC))).astype(jnp.int32)
    first = jnp.min(rows, axis=(1, 4)).transpose(1, 2, 0).reshape(BLOCKS)
    last = jnp.max(rows, axis=(1, 4)).transpose(1, 2, 0).reshape(BLOCKS)
    worked = apply_field(jnp.stack([first, last], axis=1), recv, potential)
    returned = lax.all_to_all(worked, "pw", split_axis=0, concat_axis=0, tiled=True)

    becp = jnp.sum(recv[:, 48, :], axis=0).reshape(2, PROJ)
    same_atom = proj_atom[:, None] == proj_atom[None, :]
    matrix = jnp.where(same_atom, 0.5 * (coupling + coupling.T), 0.0)
    coupled = jnp.sum(matrix[None] * becp[:, None, :], axis=2, keepdims=True)
    applied, sums = collect(slot, wave_coef, everyone, projector, returned, owned, coupled)
    parts = jnp.broadcast_to(sums[:, :, 0].reshape(1, 16), (PW, 16))
    parts = jnp.pad(parts, ((0, 0), (0, 112)))
    total = jnp.sum(lax.all_to_all(parts, "pw", split_axis=0, concat_axis=0, tiled=True), axis=0)[:16]
    total = total.reshape(2, 2, 4, 1)
    return applied, total[0], total[1]


def solution(mesh):
    in_specs = (
        P(None, "band", "pw"),
        P(None, None, "pw"),
        P("pw", None, None),
        P("pw"),
        P(),
        P(),
        P(),
    )
    out_specs = (P(None, "band", "pw"), P(None, None, "band"), P(None, None, "band"))
    return jax.shard_map(local, mesh=mesh, in_specs=in_specs, out_specs=out_specs, check_vma=False)
```

```python
import functools

import jax
import jax.numpy as jnp
import ml_dtypes
import numpy as np
from jax import lax
from jax.experimental import pallas as pl
from jax.experimental.pallas import tpu as pltpu
from jax.sharding import PartitionSpec as P

GX = 256
GY = 256
GZ = 256
KIN_MAX = 2.0
PRECISE = lax.Precision.HIGHEST

PW = 32
STICKS = 384
COEFS = 16384
PROJ = 64
PLANES = GZ // PW
ROWS = 2 * PLANES
KC = 1024
TILES = STICKS // 128
GROUPS = 24
CHUNKS = 16
NQ = 4
NCH = 3
PAIR = 2
F32 = jnp.float32
BF16 = jnp.bfloat16
NN = (((1,), (0,)), ((), ()))
NT = (((1,), (1,)), ((), ()))


def mm(left, right, dims=NN):
    return lax.dot_general(left, right, dims, preferred_element_type=F32)


def split(value):
    high = value.astype(BF16)
    low = (value - high.astype(F32)).astype(BF16)
    return high, low


def split_table(table):
    high = table.astype(np.float32).astype(ml_dtypes.bfloat16)
    low = (table - high.astype(np.float64)).astype(np.float32).astype(ml_dtypes.bfloat16)
    return high, low


def trig():
    n = np.arange(256)
    angle = 2.0 * np.pi * (np.outer(n, n) % 256) / 256.0
    return np.cos(angle), np.sin(angle)


def folded_table():
    c, s = trig()
    return np.concatenate([c[:128], c[128:129], s[1:128]], axis=0)


def plane_tables():
    table = folded_table()
    order = [128 * part + 8 * chunk + i for chunk in range(CHUNKS) for part in range(2) for i in range(8)]
    table_x = table[order]

    def left(values):
        high, low = split_table(values)
        return jnp.asarray(np.concatenate([high, low, high], axis=1))

    def right(values):
        high, low = split_table(values)
        return jnp.asarray(np.concatenate([high, low, high], axis=0))

    return right(table), right(table.T), left(table_x.T), left(table_x)


def spread_table():
    c, s = trig()
    rows = np.concatenate(
        [np.concatenate([np.concatenate([c[z], -s[z]])[None] if part == 0 else np.concatenate([s[z], c[z]])[None]
                         for z in range(d * PLANES, (d + 1) * PLANES)])
         for d in range(PW) for part in range(2)])
    high, low = split_table(rows)
    return np.concatenate([high, low, high], axis=1)


def collect_table():
    c, s = trig()
    full = np.zeros((512, 512))
    for d in range(PW):
        zs = np.arange(d * PLANES, (d + 1) * PLANES)
        at = d * ROWS
        full[:256, at:at + PLANES] = c[:, zs]
        full[:256, at + PLANES:at + ROWS] = s[:, zs]
        full[256:, at:at + PLANES] = -s[:, zs]
        full[256:, at + PLANES:at + ROWS] = c[:, zs]
    high, low = split_table(full)
    return np.concatenate([high, low, high], axis=1)


def iota(shape, dim):
    return lax.broadcasted_iota(jnp.int32, shape, dim).astype(F32)


def slot_parts(slot):
    slot = slot.astype(F32)
    z = jnp.floor((slot + 0.5) * (1.0 / STICKS))
    return z, slot - z * STICKS


def fold(x):
    key = jnp.where(x == 128.0, 0.0, jnp.minimum(x, 256.0 - x))
    even = jnp.where(x == 128.0, -1.0, key)
    odd = jnp.where(x == 0.0, -1.0, key)
    return key, even, odd, jnp.where(x > 128.0, -1.0, 1.0)


def rank_of(owned):
    wide = jnp.broadcast_to(owned, (128, STICKS))
    down = jnp.transpose(wide)[:, :1]

    def sort_key(column):
        return fold(jnp.floor(column * (1.0 / GY)))[0] * 65536.0 + column

    key = sort_key(owned)
    key_down = sort_key(down)
    rank_row = jnp.sum(jnp.where(key_down < key, 1.0, 0.0), axis=0, keepdims=True)
    order = jnp.where(iota((STICKS, STICKS), 0) == rank_row, 1.0, 0.0)
    rank_col = jnp.sum(jnp.where(key < key_down, 1.0, 0.0), axis=1, keepdims=True)
    ordered = jnp.sum(jnp.where(iota((STICKS, STICKS), 1) == rank_col, down, 0.0), axis=0, keepdims=True)
    return order, ordered


def spread_kernel(slot_ref, coef_ref, proj_ref, owned_ref, table_ref, out_ref, acc, becp):
    step = pl.program_id(0)

    @pl.when(step == 0)
    def _():
        acc[...] = jnp.zeros_like(acc)
        becp[...] = jnp.zeros_like(becp)

    z, s = slot_parts(slot_ref[...])
    c_re = coef_ref[0]
    c_im = coef_ref[1]
    re_hi, re_lo = split(c_re)
    im_hi, im_lo = split(c_im)
    z_hot = iota((GZ, KC), 0).astype(BF16) == z.astype(BF16)
    none = jnp.zeros((), BF16)
    placed = jnp.concatenate(
        [jnp.where(z_hot, part, none) for part in (re_hi, im_hi, re_lo, im_lo)], axis=0)
    s_hot = jnp.where(
        (iota((STICKS, KC), 0) - 192.0).astype(BF16) == (s - 192.0).astype(BF16), jnp.ones((), BF16), none)
    acc[...] += mm(s_hot, placed, NT)

    p_re = proj_ref[0]
    p_im = proj_ref[1]
    real = p_re * c_re + p_im * c_im
    imag = p_re * c_im - p_im * c_re
    both = jnp.concatenate([real, imag], axis=0)
    total = both[:, :128]
    for at in range(128, KC, 128):
        total = total + both[:, at:at + 128]
    becp[...] += total

    @pl.when(step == pl.num_programs(0) - 1)
    def _():
        order, ordered = rank_of(owned_ref[...].astype(F32))
        sticks = mm(order.astype(BF16), acc[...].astype(BF16)).astype(BF16)
        high = sticks[:, :512]
        low = sticks[:, 512:]
        spread = mm(table_ref[...], jnp.concatenate([high, high, low], axis=1), NT)
        spread = spread.reshape(PW, ROWS, STICKS)
        for t in range(TILES):
            out_ref[:, t * ROWS:(t + 1) * ROWS, :] = spread[:, :, t * 128:(t + 1) * 128]
        line = jnp.sum(jnp.transpose(becp[...]), axis=0, keepdims=True)
        extra = jnp.concatenate(
            [line] + [ordered[:, t * 128:(t + 1) * 128] for t in range(TILES)] + [jnp.zeros((4, 128), F32)], axis=0)
        out_ref[:, TILES * ROWS:, :] = jnp.broadcast_to(extra[None], (PW, 8, 128))


def spread_sticks(slot, coef, proj, owned):
    table = jnp.asarray(spread_table())
    return pl.pallas_call(
        spread_kernel,
        grid=(COEFS // KC,),
        in_specs=[
            pl.BlockSpec((1, KC), lambda i: (0, i)),
            pl.BlockSpec((2, 1, KC), lambda i: (0, 0, i)),
            pl.BlockSpec((2, PROJ, KC), lambda i: (0, 0, i)),
            pl.BlockSpec((1, STICKS), lambda i: (0, 0)),
            pl.BlockSpec((512, 1536), lambda i: (0, 0)),
        ],
        out_specs=pl.BlockSpec((PW, 56, 128), lambda i: (0, 0, 0)),
        out_shape=jax.ShapeDtypeStruct((PW, 56, 128), F32),
        scratch_shapes=[pltpu.VMEM((STICKS, 1024), F32), pltpu.VMEM((128, 128), F32)],
        compiler_params=pltpu.CompilerParams(vmem_limit_bytes=48 << 20),
        name="spread_sticks",
    )(slot, coef, proj, owned, table)


def swap_chunks(parts):
    parts = list(parts)
    chunk = lax.broadcasted_iota(jnp.int32, parts[0].shape, 1) // 16
    for bit in (1, 2, 4):
        here = (chunk & bit) == 0
        for a in range(8):
            if a & bit:
                continue
            one, two = parts[a], parts[a | bit]
            parts[a] = jnp.where(here, one, pltpu.roll(two, 16 * bit, 1))
            parts[a | bit] = jnp.where(here, pltpu.roll(one, 128 - 16 * bit, 1), two)
    return parts


def field_kernel(range_ref, recv_ref, field_ref, y_in_ref, y_out_ref, x_in_ref, x_out_ref, out_ref,
                 wide, hot, keys, signs, grid, done, sticks):
    cells = []
    for g in range(4):
        mixed = swap_chunks([recv_ref[g * 8 + i, TILES * ROWS:, :] for i in range(8)])
        cells.append(mixed)
    one_hot = iota((128, 512), 0).astype(BF16)
    zero = jnp.zeros((), BF16)
    for t in range(TILES):
        mixed = [swap_chunks([recv_ref[g * 8 + i, t * ROWS:(t + 1) * ROWS, :] for i in range(8)]) for g in range(4)]
        for c in range(8):
            q = t * 8 + c
            values = jnp.concatenate([mixed[g][c] for g in range(4)], axis=1)
            high, low = split(values)
            both = jnp.concatenate([high.astype(F32), low.astype(F32)], axis=0)
            wide[q] = jnp.broadcast_to(both[:, None, :], (2 * ROWS, 16, 512)).astype(BF16)
            column = jnp.concatenate([cells[g][c][1 + t:2 + t] for g in range(4)], axis=1)
            x = jnp.floor(column * (1.0 / GY))
            y = column - x * GY
            _, even, odd, sign = fold(x)
            upper = iota((16, 512), 0) < 8.0
            keys[q] = jnp.where(upper, even, odd).astype(BF16)
            signs[q] = jnp.where(upper, 1.0, sign).astype(BF16)
            _, even, odd, sign = fold(y)
            hot[q, :128, :] = jnp.where(one_hot == even.astype(BF16), jnp.ones((), BF16), zero)
            hot[q, 128:, :] = jnp.where(one_hot == odd.astype(BF16), sign.astype(BF16), zero)
    for q in range(GROUPS, GROUPS + NQ - 1):
        wide[q] = jnp.zeros((2 * ROWS, 16, 512), BF16)
        hot[q] = jnp.zeros((256, 512), BF16)
        keys[q] = jnp.full((16, 512), -1.0, BF16)
        signs[q] = jnp.zeros((16, 512), BF16)
    done[:, GX:, :] = jnp.zeros((ROWS, 16 * (NCH - 1), 512), BF16)

    step_of = iota((16, 512), 0)
    step_of = jnp.where(step_of < 8.0, step_of, step_of - 8.0)

    def place(chunk, carry):
        want = (step_of + (chunk * 8).astype(F32)).astype(BF16)
        here = pl.ds(pl.multiple_of(chunk * 16, 16), 16)
        start = range_ref[0, chunk]

        def product(first):
            masked = []
            for j in range(NQ):
                mine = jnp.where(keys[first + j] == want, signs[first + j], zero)
                masked.append((wide[first + j] * mine[None]).reshape(2 * ROWS * 16, 512))
            got = mm(jnp.concatenate(masked, axis=1),
                     jnp.concatenate([hot[first + j] for j in range(NQ)], axis=1), NT)
            got = got.reshape(2, ROWS, 16, 256)
            return got[0] + got[1]

        grid[:, here, :] = product(start)

        def more(p, inner):
            grid[:, here, :] += product(start + p * NQ)
            return inner

        return lax.fori_loop(1, range_ref[1, chunk], more, carry)

    lax.fori_loop(0, CHUNKS, place, 0)

    row = lax.broadcasted_iota(jnp.int32, (256, 256), 0)
    lane = lax.broadcasted_iota(jnp.int32, (256, 256), 1)
    even_x = ((row & 8) == 0) | (row == 8)
    even_y = lane <= 128

    def along_y(re, im, table):
        high, low = split(jnp.concatenate([re, im], axis=0))
        got = mm(jnp.concatenate([high, high, low], axis=1), table[...])
        return got[:256], got[256:]

    def along_x(re, im, table):
        high, low = split(jnp.concatenate([re, im], axis=1))
        got = mm(table[...], jnp.concatenate([high, high, low], axis=0))
        return got[:, :256], got[:, 256:]

    def plane(zz):
        re = grid[zz]
        im = grid[PLANES + zz]
        re, im = along_y(jnp.where(even_y, re, -im), jnp.where(even_y, im, re), y_in_ref)
        re, im = along_x(jnp.where(even_x, re, -im), jnp.where(even_x, im, re), x_in_ref)
        field = field_ref[zz]
        re, im = along_x(re * field, im * field, x_out_ref)
        re, im = along_y(jnp.where(even_x, re, im), jnp.where(even_x, im, -re), y_out_ref)
        high, low = split(jnp.where(even_y, re, im))
        done[zz, :GX, :256] = high
        done[zz, :GX, 256:] = low
        high, low = split(jnp.where(even_y, im, -re))
        done[PLANES + zz, :GX, :256] = high
        done[PLANES + zz, :GX, 256:] = low

    def planes(pair, carry):
        for at in range(PAIR):
            plane(pair * PAIR + at)
        return carry

    lax.fori_loop(0, PLANES // PAIR, planes, 0)

    def pick(q, carry):
        both = jnp.concatenate([hot[q], hot[q]], axis=0)
        key = keys[q].astype(F32)
        sign = signs[q].astype(F32)
        start = range_ref[2, q]

        def product(first):
            here = pl.ds(pl.multiple_of(first * 16, 16), 16 * NCH)
            lines = done[:, here, :].reshape(ROWS * 16 * NCH, 512)
            got = mm(lines, both).reshape(ROWS, 2 * NCH, 8, 512)
            total = None
            for j in range(NCH):
                want = step_of + ((first + j) * 8).astype(F32)
                mine = jnp.where(key == want, sign, 0.0)
                part = got[:, 2 * j] * mine[None, :8] + got[:, 2 * j + 1] * mine[None, 8:]
                total = part if total is None else total + part
            return jnp.sum(total, axis=1)

        sticks[q] = product(start)

        def more(p, inner):
            sticks[q] += product(start + p * NCH)
            return inner

        return lax.fori_loop(1, range_ref[3, q], more, carry)

    lax.fori_loop(0, GROUPS, pick, 0)

    for t in range(TILES):
        for g in range(4):
            mixed = swap_chunks([sticks[t * 8 + c, :, g * 128:(g + 1) * 128] for c in range(8)])
            for i in range(8):
                out_ref[g * 8 + i, t * ROWS:(t + 1) * ROWS, :] = mixed[i]


def apply_field(ranges, recv, field):
    vmem = pl.BlockSpec(memory_space=pltpu.VMEM)
    return pl.pallas_call(
        field_kernel,
        in_specs=[pl.BlockSpec(memory_space=pltpu.SMEM)] + [vmem] * 6,
        out_specs=vmem,
        out_shape=jax.ShapeDtypeStruct((PW, 48, 128), F32),
        scratch_shapes=[
            pltpu.VMEM((GROUPS + NQ - 1, 2 * ROWS, 16, 512), BF16),
            pltpu.VMEM((GROUPS + NQ - 1, 256, 512), BF16),
            pltpu.VMEM((GROUPS + NQ - 1, 16, 512), BF16),
            pltpu.VMEM((GROUPS + NQ - 1, 16, 512), BF16),
            pltpu.VMEM((ROWS, GX, GY), F32),
            pltpu.VMEM((ROWS, GX + 16 * (NCH - 1), 512), BF16),
            pltpu.VMEM((GROUPS, ROWS, 512), F32),
        ],
        compiler_params=pltpu.CompilerParams(vmem_limit_bytes=56 << 20),
        name="apply_field",
    )(ranges, recv, field, *plane_tables())


def ranges_of(columns):
    chunk = jnp.floor(fold(jnp.floor(columns * (1.0 / GY)))[0] * 0.125).astype(jnp.int32)
    chunk = chunk.reshape(PW, GROUPS, 16)
    first = jnp.min(chunk, axis=(0, 2))
    last = jnp.max(chunk, axis=(0, 2))
    at = jnp.arange(GROUPS, dtype=jnp.int32)[:, None]
    start = jnp.sum(jnp.where(last[None] < at, 1, 0), axis=1)
    end = jnp.sum(jnp.where(first[None] <= at, 1, 0), axis=1)
    start = jnp.minimum(start, GROUPS - 1)
    return jnp.stack([start, (end - start + NQ - 1) // NQ, first, (last - first + NCH) // NCH])


def centred(values, length):
    return jnp.where(values < length // 2, values, values - length)


def collect_kernel(slot_ref, coef_ref, all_ref, proj_ref, recv_ref, owned_ref, coupled_ref, table_ref,
                   out_ref, sums_ref, values, sums):
    step = pl.program_id(0)

    @pl.when(step == 0)
    def _():
        sums[...] = jnp.zeros_like(sums)
        owned = owned_ref[...].astype(F32)
        order, _ = rank_of(owned)
        order = order.astype(BF16)
        lines = jnp.concatenate(
            [recv_ref[:, t * ROWS:(t + 1) * ROWS, :].reshape(512, 128) for t in range(TILES)], axis=1)
        high, low = split(lines)
        back = mm(table_ref[...], jnp.concatenate([high, high, low], axis=0))
        high, low = split(back)
        values[:512, :STICKS] = mm(high, order).astype(BF16)
        values[:512, STICKS:] = mm(low, order).astype(BF16)
        x = jnp.floor(owned * (1.0 / GY))
        y = centred(owned - x * GY, GY)
        x = centred(x, GX)
        square = x * x + y * y
        upper = jnp.floor(square * (1.0 / 256.0))
        lower = square - upper * 256.0
        pair = jnp.concatenate([upper, lower, jnp.zeros((14, STICKS), F32)], axis=0)
        values[512:, :STICKS] = pair.astype(BF16)
        values[512:, STICKS:] = jnp.zeros((16, STICKS), BF16)

    z, s = slot_parts(slot_ref[...])
    none = jnp.zeros((), BF16)
    s_hot = jnp.where(
        (iota((STICKS, KC), 0) - 192.0).astype(BF16) == (s - 192.0).astype(BF16), jnp.ones((), BF16), none)
    found = mm(values[...], jnp.concatenate([s_hot, s_hot], axis=0))
    z_hot = iota((GZ, KC), 0) == z
    scale = 1.0 / (GX * GY * GZ)
    local_re = jnp.sum(jnp.where(z_hot, found[:256], 0.0), axis=0, keepdims=True) * scale
    local_im = jnp.sum(jnp.where(z_hot, found[256:512], 0.0), axis=0, keepdims=True) * scale
    z = centred(z, GZ)
    square = found[512:513] * 256.0 + found[513:514] + z * z
    kinetic = square * (KIN_MAX / 3.0 / 16384.0)
    c_re = coef_ref[0]
    c_im = coef_ref[1]
    p_re = proj_ref[0]
    p_im = proj_ref[1]
    w_re = coupled_ref[0]
    w_im = coupled_ref[1]
    far_re = jnp.sum(p_re * w_re - p_im * w_im, axis=0, keepdims=True)
    far_im = jnp.sum(p_re * w_im + p_im * w_re, axis=0, keepdims=True)
    h_re = kinetic * c_re + local_re + far_re
    h_im = kinetic * c_im + local_im + far_im
    out_ref[0] = h_re
    out_ref[1] = h_im
    a_re = all_ref[0]
    a_im = all_ref[1]
    sums[0] += a_re * h_re + a_im * h_im
    sums[1] += a_re * h_im - a_im * h_re
    sums[2] += a_re * c_re + a_im * c_im
    sums[3] += a_re * c_im - a_im * c_re

    @pl.when(step == pl.num_programs(0) - 1)
    def _():
        sums_ref[...] = jnp.broadcast_to(jnp.sum(sums[...], axis=2, keepdims=True), (4, 4, 128))


def collect(slot, coef, everyone, proj, recv, owned, coupled):
    table = jnp.asarray(collect_table())
    return pl.pallas_call(
        collect_kernel,
        grid=(COEFS // KC,),
        in_specs=[
            pl.BlockSpec((1, KC), lambda i: (0, i)),
            pl.BlockSpec((2, 1, KC), lambda i: (0, 0, i)),
            pl.BlockSpec((2, 4, KC), lambda i: (0, 0, i)),
            pl.BlockSpec((2, PROJ, KC), lambda i: (0, 0, i)),
            pl.BlockSpec((PW, 48, 128), lambda i: (0, 0, 0)),
            pl.BlockSpec((1, STICKS), lambda i: (0, 0)),
            pl.BlockSpec((2, PROJ, 1), lambda i: (0, 0, 0)),
            pl.BlockSpec((512, 1536), lambda i: (0, 0)),
        ],
        out_specs=[
            pl.BlockSpec((2, 1, KC), lambda i: (0, 0, i)),
            pl.BlockSpec((4, 4, 128), lambda i: (0, 0, 0)),
        ],
        out_shape=[
            jax.ShapeDtypeStruct((2, 1, COEFS), F32),
            jax.ShapeDtypeStruct((4, 4, 128), F32),
        ],
        scratch_shapes=[pltpu.VMEM((528, 2 * STICKS), BF16), pltpu.VMEM((4, 4, KC), F32)],
        compiler_params=pltpu.CompilerParams(vmem_limit_bytes=48 << 20),
        name="collect",
    )(slot, coef, everyone, proj, recv, owned, coupled, table)


def local(wave_coef, projector, potential, grid_slot, stick_column, proj_atom, coupling):
    owned = lax.dynamic_slice_in_dim(stick_column, lax.axis_index("pw") * STICKS, STICKS).reshape(1, STICKS)
    slot = grid_slot.reshape(1, COEFS)
    everyone = lax.all_gather(wave_coef, "band", axis=1, tiled=True)
    sent = spread_sticks(slot, wave_coef, projector, owned)
    recv = lax.all_to_all(sent, "pw", split_axis=0, concat_axis=0, tiled=True)

    worked = apply_field(ranges_of(recv[:, 49:52, :].reshape(PW, STICKS)), recv, potential)
    returned = lax.all_to_all(worked, "pw", split_axis=0, concat_axis=0, tiled=True)

    becp = jnp.sum(recv[:, 48, :], axis=0).reshape(2, PROJ)
    same_atom = proj_atom[:, None] == proj_atom[None, :]
    matrix = jnp.where(same_atom, 0.5 * (coupling + coupling.T), 0.0)
    coupled = jnp.sum(matrix[None] * becp[:, None, :], axis=2, keepdims=True)
    applied, sums = collect(slot, wave_coef, everyone, projector, returned, owned, coupled)
    parts = jnp.broadcast_to(sums[:, :, 0].reshape(1, 16), (PW, 16))
    parts = jnp.pad(parts, ((0, 0), (0, 112)))
    total = jnp.sum(lax.all_to_all(parts, "pw", split_axis=0, concat_axis=0, tiled=True), axis=0)[:16]
    total = total.reshape(2, 2, 4, 1)
    return applied, total[0], total[1]


def solution(mesh):
    in_specs = (
        P(None, "band", "pw"),
        P(None, None, "pw"),
        P("pw", None, None),
        P("pw"),
        P(),
        P(),
        P(),
    )
    out_specs = (P(None, "band", "pw"), P(None, None, "band"), P(None, None, "band"))
    return jax.shard_map(local, mesh=mesh, in_specs=in_specs, out_specs=out_specs, check_vma=False)
```

```python
import jax
import jax.numpy as jnp
import ml_dtypes
import numpy as np
from jax import lax
from jax.experimental import pallas as pl
from jax.experimental.pallas import tpu as pltpu
from jax.sharding import PartitionSpec as P

GX = 256
GY = 256
GZ = 256
KIN_MAX = 2.0
PRECISE = lax.Precision.HIGHEST

PW = 32
STICKS = 384
COEFS = 16384
PROJ = 64
PLANES = GZ // PW
ROWS = 2 * PLANES
KC = 2048
WINDOW = 256
SLOT_ROWS = 768
TILES = STICKS // 128
GROUPS = 24
CHUNKS = 16
NQ = 4
NCH = 3
PAIR = 2
PLACE_UNROLL = 2
PICK_UNROLL = 2
GRAM_STEPS = 4
F32 = jnp.float32
BF16 = jnp.bfloat16
NN = (((1,), (0,)), ((), ()))
NT = (((1,), (1,)), ((), ()))


def mm(left, right, dims=NN):
    return lax.dot_general(left, right, dims, preferred_element_type=F32)


def split(value):
    high = value.astype(BF16)
    low = (value - high.astype(F32)).astype(BF16)
    return high, low


def split_table(table):
    high = table.astype(np.float32).astype(ml_dtypes.bfloat16)
    low = (table - high.astype(np.float64)).astype(np.float32).astype(ml_dtypes.bfloat16)
    return high, low


def trig():
    n = np.arange(256)
    angle = 2.0 * np.pi * (np.outer(n, n) % 256) / 256.0
    return np.cos(angle), np.sin(angle)


def folded_table():
    c, s = trig()
    return np.concatenate([c[:128], c[128:129], s[1:128]], axis=0)


def plane_tables():
    table = folded_table()
    order = [128 * part + 8 * chunk + i for chunk in range(CHUNKS) for part in range(2) for i in range(8)]
    table_x = table[order]

    def left(values):
        high, low = split_table(values)
        return jnp.asarray(np.concatenate([high, low, high], axis=1))

    def right(values):
        high, low = split_table(values)
        return jnp.asarray(np.concatenate([high, low, high], axis=0))

    return right(table), right(table.T), left(table_x.T), left(table_x)


def spread_table():
    c, s = trig()
    rows = np.concatenate(
        [np.concatenate([np.concatenate([c[z], -s[z]])[None] if part == 0 else np.concatenate([s[z], c[z]])[None]
                         for z in range(d * PLANES, (d + 1) * PLANES)])
         for d in range(PW) for part in range(2)])
    high, low = split_table(rows)
    return np.concatenate([high, low, high], axis=1)


def collect_table():
    c, s = trig()
    full = np.zeros((512, 512))
    for d in range(PW):
        zs = np.arange(d * PLANES, (d + 1) * PLANES)
        at = d * ROWS
        full[:256, at:at + PLANES] = c[:, zs]
        full[:256, at + PLANES:at + ROWS] = s[:, zs]
        full[256:, at:at + PLANES] = -s[:, zs]
        full[256:, at + PLANES:at + ROWS] = c[:, zs]
    high, low = split_table(full)
    return np.concatenate([high, low, high], axis=1)


def iota(shape, dim):
    return lax.broadcasted_iota(jnp.int32, shape, dim).astype(F32)


def sort_rows(keys, values):
    keys = list(keys)
    values = [list(each) for each in values]
    sub = lax.broadcasted_iota(jnp.int32, (8, 128), 0)
    size = 2
    while size <= 128:
        dist = size // 2
        while dist >= 1:
            if dist < 16:
                for one in range(16):
                    if one & dist:
                        continue
                    two = one | dist
                    swap = keys[one] > keys[two]
                    if size < 16:
                        if one & size:
                            swap = keys[one] < keys[two]
                    elif size < 128:
                        swap = jnp.where((sub & (size // 16)) == 0, keys[one] - keys[two], keys[two] - keys[one]) > 0.0
                    for each in [keys] + values:
                        each[one], each[two] = (jnp.where(swap, each[two], each[one]),
                                                jnp.where(swap, each[one], each[two]))
            else:
                hop = dist // 16
                low = (sub & hop) == 0
                rising = (sub & (size // 16)) == 0 if size < 128 else jnp.full((8, 128), True)
                least = jnp.where(low == rising, 1.0, -1.0)

                def other(x):
                    return jnp.where(low, pltpu.roll(x, 8 - hop, 0), pltpu.roll(x, hop, 0))

                for one in range(16):
                    swap = (keys[one] - other(keys[one])) * least > 0.0
                    for each in [keys] + values:
                        each[one] = jnp.where(swap, other(each[one]), each[one])
            dist //= 2
        size *= 2
    return keys, values


def sorted_row(ref, block):
    at = pl.ds(block // 2, 1)
    half = 8 * (block % 2)
    return jnp.concatenate([ref[half + v, at, :] for v in range(8)], axis=1)


def key_parts(key):
    row = jnp.floor(key * (1.0 / 16384.0))
    rest = key - row * 16384.0
    return row, jnp.floor(rest * (1.0 / 128.0))


def fold(x):
    key = jnp.where(x == 128.0, 0.0, jnp.minimum(x, 256.0 - x))
    even = jnp.where(x == 128.0, -1.0, key)
    odd = jnp.where(x == 0.0, -1.0, key)
    return key, even, odd, jnp.where(x > 128.0, -1.0, 1.0)


def rank_of(owned):
    wide = jnp.broadcast_to(owned, (128, STICKS))
    down = jnp.transpose(wide)[:, :1]

    def sort_key(column):
        return fold(jnp.floor(column * (1.0 / GY)))[0] * 65536.0 + column

    key = sort_key(owned)
    key_down = sort_key(down)
    rank_row = jnp.sum(jnp.where(key_down < key, 1.0, 0.0), axis=0, keepdims=True)
    order = jnp.where(iota((STICKS, STICKS), 0) == rank_row, 1.0, 0.0)
    rank_col = jnp.sum(jnp.where(key < key_down, 1.0, 0.0), axis=1, keepdims=True)
    ordered = jnp.sum(jnp.where(iota((STICKS, STICKS), 1) == rank_col, down, 0.0), axis=0, keepdims=True)
    return order, ordered


def spread_kernel(slot_ref, tile_ref, coef_ref, proj_ref, owned_ref, table_ref, out_ref, key_ref, span_ref,
                  part_re, part_im, acc, becp):
    step = pl.program_id(0)

    @pl.when(step == 0)
    def _():
        slot = slot_ref[...].astype(F32)
        z = jnp.floor((slot + 0.5) * (1.0 / STICKS))
        s = slot - z * STICKS
        tile = jnp.floor(s * (1.0 / 128.0))
        place = (tile * 256.0 + z) * 128.0 + (s - tile * 128.0)
        row = iota((128, 128), 0)
        array = jnp.floor(row * 0.125)
        key = place * 128.0 + (row - array * 8.0) * 16.0 + array

        def rows(x):
            return [x[v * 8:(v + 1) * 8] for v in range(16)]

        keys, (real, imag) = sort_rows(rows(key), [rows(tile_ref[0]), rows(tile_ref[1])])
        for v in range(16):
            key_ref[v] = keys[v]
            part_re[v] = real[v]
            part_im[v] = imag[v]
        for block in range(16):
            half = 8 * (block % 2)
            at = block // 2
            first = jnp.min(key_parts(keys[half][at:at + 1])[0]).astype(jnp.int32)
            last = jnp.max(key_parts(keys[half + 7][at:at + 1])[0]).astype(jnp.int32)
            first = (first >> 4) << 4
            span_ref[0, block] = first
            span_ref[1, block] = ((last - first) >> 8) + 1
        acc[...] = jnp.zeros_like(acc)
        becp[...] = jnp.zeros_like(becp)

    none = jnp.zeros((), BF16)
    lane_of = (iota((128, 1024), 0)).astype(BF16)
    row_of = (iota((WINDOW, 1024), 0) - 128.0).astype(BF16)
    for half in range(2):
        block = step * 2 + half
        at = pl.ds(step, 1)
        key = jnp.concatenate([key_ref[8 * half + v, at, :] for v in range(8)], axis=1)
        real = jnp.concatenate([part_re[8 * half + v, at, :] for v in range(8)], axis=1)
        imag = jnp.concatenate([part_im[8 * half + v, at, :] for v in range(8)], axis=1)
        row, lane = key_parts(key)
        hit = lane_of == lane.astype(BF16)
        re_hi, re_lo = split(real)
        im_hi, im_lo = split(imag)
        placed = jnp.concatenate([jnp.where(hit, part, none) for part in (re_hi, im_hi, re_lo, im_lo)], axis=0)

        def add(first):
            first = pl.multiple_of(first, 16)
            want = row - (first + 128).astype(F32)
            hot = jnp.where(row_of == want.astype(BF16), jnp.ones((), BF16), none)
            acc[pl.ds(first, WINDOW), :] += mm(hot, placed, NT)

        first = span_ref[0, block]
        add(first)

        def more(p, carry):
            add(first + p * WINDOW)
            return carry

        lax.fori_loop(1, span_ref[1, block], more, 0)

    c_re = coef_ref[0]
    c_im = coef_ref[1]
    p_re = proj_ref[0]
    p_im = proj_ref[1]
    real = p_re * c_re + p_im * c_im
    imag = p_re * c_im - p_im * c_re
    both = jnp.concatenate([real, imag], axis=0)
    total = both[:, :128]
    for at in range(128, KC, 128):
        total = total + both[:, at:at + 128]
    becp[...] += total

    @pl.when(step == pl.num_programs(0) - 1)
    def _():
        order, ordered = rank_of(owned_ref[...].astype(F32))
        sticks = jnp.concatenate(
            [jnp.concatenate([acc[t * 256:(t + 1) * 256, part * 128:(part + 1) * 128] for t in range(TILES)], axis=1)
             for part in range(4)], axis=0).astype(BF16)
        sticks = mm(sticks, order.astype(BF16), NT).astype(BF16)
        high = sticks[:512]
        low = sticks[512:]
        spread = mm(table_ref[...], jnp.concatenate([high, high, low], axis=0))
        spread = spread.reshape(PW, ROWS, STICKS)
        for t in range(TILES):
            out_ref[:, t * ROWS:(t + 1) * ROWS, :] = spread[:, :, t * 128:(t + 1) * 128]
        line = jnp.sum(jnp.transpose(becp[...]), axis=0, keepdims=True)
        extra = jnp.concatenate(
            [line] + [ordered[:, t * 128:(t + 1) * 128] for t in range(TILES)] + [jnp.zeros((4, 128), F32)], axis=0)
        out_ref[:, TILES * ROWS:, :] = jnp.broadcast_to(extra[None], (PW, 8, 128))


def spread_sticks(slot, coef, proj, owned):
    table = jnp.asarray(spread_table())
    return pl.pallas_call(
        spread_kernel,
        grid=(COEFS // KC,),
        in_specs=[
            pl.BlockSpec((128, 128), lambda i: (0, 0)),
            pl.BlockSpec((2, 128, 128), lambda i: (0, 0, 0)),
            pl.BlockSpec((2, 1, KC), lambda i: (0, 0, i)),
            pl.BlockSpec((2, PROJ, KC), lambda i: (0, 0, i)),
            pl.BlockSpec((1, STICKS), lambda i: (0, 0)),
            pl.BlockSpec((512, 1536), lambda i: (0, 0)),
        ],
        out_specs=[
            pl.BlockSpec((PW, 56, 128), lambda i: (0, 0, 0)),
            pl.BlockSpec((16, 8, 128), lambda i: (0, 0, 0)),
            pl.BlockSpec(memory_space=pltpu.SMEM),
        ],
        out_shape=[
            jax.ShapeDtypeStruct((PW, 56, 128), F32),
            jax.ShapeDtypeStruct((16, 8, 128), F32),
            jax.ShapeDtypeStruct((2, 16), jnp.int32),
        ],
        scratch_shapes=[
            pltpu.VMEM((16, 8, 128), F32),
            pltpu.VMEM((16, 8, 128), F32),
            pltpu.VMEM((SLOT_ROWS + WINDOW, 512), F32),
            pltpu.VMEM((128, 128), F32),
        ],
        compiler_params=pltpu.CompilerParams(vmem_limit_bytes=48 << 20),
        cost_estimate=pl.CostEstimate(flops=6 * 10 ** 9, bytes_accessed=12 << 20, transcendentals=0),
        name="spread_sticks",
    )(slot, coef.reshape(2, 128, 128), coef, proj, owned, table)


def swap_chunks(parts):
    parts = list(parts)
    chunk = lax.broadcasted_iota(jnp.int32, parts[0].shape, 1) // 16
    for bit in (1, 2, 4):
        here = (chunk & bit) == 0
        for a in range(8):
            if a & bit:
                continue
            one, two = parts[a], parts[a | bit]
            parts[a] = jnp.where(here, one, pltpu.roll(two, 16 * bit, 1))
            parts[a | bit] = jnp.where(here, pltpu.roll(one, 128 - 16 * bit, 1), two)
    return parts


def field_kernel(range_ref, recv_ref, field_ref, y_in_ref, y_out_ref, x_in_ref, x_out_ref, out_ref,
                 wide, hot, keys, signs, grid, done, sticks):
    cells = []
    for g in range(4):
        mixed = swap_chunks([recv_ref[g * 8 + i, TILES * ROWS:, :] for i in range(8)])
        cells.append(mixed)
    one_hot = iota((128, 512), 0).astype(BF16)
    zero = jnp.zeros((), BF16)
    for t in range(TILES):
        mixed = [swap_chunks([recv_ref[g * 8 + i, t * ROWS:(t + 1) * ROWS, :] for i in range(8)]) for g in range(4)]
        for c in range(8):
            q = t * 8 + c
            values = jnp.concatenate([mixed[g][c] for g in range(4)], axis=1)
            high, low = split(values)
            both = jnp.concatenate([high.astype(F32), low.astype(F32)], axis=0)
            wide[q] = jnp.broadcast_to(both[:, None, :], (2 * ROWS, 16, 512)).astype(BF16)
            column = jnp.concatenate([cells[g][c][1 + t:2 + t] for g in range(4)], axis=1)
            x = jnp.floor(column * (1.0 / GY))
            y = column - x * GY
            _, even, odd, sign = fold(x)
            upper = iota((16, 512), 0) < 8.0
            keys[q] = jnp.where(upper, even, odd).astype(BF16)
            signs[q] = jnp.where(upper, 1.0, sign).astype(BF16)
            _, even, odd, sign = fold(y)
            hot[q, :128, :] = jnp.where(one_hot == even.astype(BF16), jnp.ones((), BF16), zero)
            hot[q, 128:, :] = jnp.where(one_hot == odd.astype(BF16), sign.astype(BF16), zero)
    for q in range(GROUPS, GROUPS + NQ - 1):
        wide[q] = jnp.zeros((2 * ROWS, 16, 512), BF16)
        hot[q] = jnp.zeros((256, 512), BF16)
        keys[q] = jnp.full((16, 512), -1.0, BF16)
        signs[q] = jnp.zeros((16, 512), BF16)
    done[:, GX:, :] = jnp.zeros((ROWS, 16 * (NCH - 1), 512), BF16)

    step_of = iota((16, 512), 0)
    step_of = jnp.where(step_of < 8.0, step_of, step_of - 8.0)

    def place(chunk, first, groups):
        want = (step_of + (chunk * 8).astype(F32)).astype(BF16)
        masked = []
        for j in range(groups):
            mine = jnp.where(keys[first + j] == want, signs[first + j], zero)
            masked.append((wide[first + j] * mine[None]).reshape(2 * ROWS * 16, 512))
        got = mm(jnp.concatenate(masked, axis=1),
                 jnp.concatenate([hot[first + j] for j in range(groups)], axis=1), NT)
        got = got.reshape(2, ROWS, 16, 256)
        return got[0] + got[1]

    def rows_of(chunk):
        return pl.ds(pl.multiple_of(chunk * 16, 16), 16)

    def place_first(step, carry):
        for at in range(PLACE_UNROLL):
            chunk = step * PLACE_UNROLL + at
            grid[:, rows_of(chunk), :] = place(chunk, range_ref[0, chunk], NQ)
        return carry

    def place_rest(chunk, carry):
        def more(p, inner):
            grid[:, rows_of(chunk), :] += place(chunk, range_ref[0, chunk] + p, 1)
            return inner

        return lax.fori_loop(NQ, range_ref[1, chunk], more, carry)

    lax.fori_loop(0, CHUNKS // PLACE_UNROLL, place_first, 0)
    lax.fori_loop(0, CHUNKS, place_rest, 0)

    row = lax.broadcasted_iota(jnp.int32, (256, 256), 0)
    lane = lax.broadcasted_iota(jnp.int32, (256, 256), 1)
    even_x = ((row & 8) == 0) | (row == 8)
    even_y = lane <= 128

    def along_y(re, im, table):
        high, low = split(jnp.concatenate([re, im], axis=0))
        got = mm(jnp.concatenate([high, high, low], axis=1), table[...])
        return got[:256], got[256:]

    def along_x(re, im, table):
        high, low = split(jnp.concatenate([re, im], axis=1))
        got = mm(table[...], jnp.concatenate([high, high, low], axis=0))
        return got[:, :256], got[:, 256:]

    def plane(zz):
        re = grid[zz]
        im = grid[PLANES + zz]
        re, im = along_y(jnp.where(even_y, re, -im), jnp.where(even_y, im, re), y_in_ref)
        re, im = along_x(jnp.where(even_x, re, -im), jnp.where(even_x, im, re), x_in_ref)
        field = field_ref[zz]
        re, im = along_x(re * field, im * field, x_out_ref)
        re, im = along_y(jnp.where(even_x, re, im), jnp.where(even_x, im, -re), y_out_ref)
        high, low = split(jnp.where(even_y, re, im))
        done[zz, :GX, :256] = high
        done[zz, :GX, 256:] = low
        high, low = split(jnp.where(even_y, im, -re))
        done[PLANES + zz, :GX, :256] = high
        done[PLANES + zz, :GX, 256:] = low

    def planes(pair, carry):
        for at in range(PAIR):
            plane(pair * PAIR + at)
        return carry

    lax.fori_loop(0, PLANES // PAIR, planes, 0)

    def pick(q, first, chunks):
        both = jnp.concatenate([hot[q], hot[q]], axis=0)
        key = keys[q].astype(F32)
        sign = signs[q].astype(F32)
        here = pl.ds(pl.multiple_of(first * 16, 16), 16 * chunks)
        lines = done[:, here, :].reshape(ROWS * 16 * chunks, 512)
        got = mm(lines, both).reshape(ROWS, 2 * chunks, 8, 512)
        total = None
        for j in range(chunks):
            want = step_of + ((first + j) * 8).astype(F32)
            mine = jnp.where(key == want, sign, 0.0)
            part = got[:, 2 * j] * mine[None, :8] + got[:, 2 * j + 1] * mine[None, 8:]
            total = part if total is None else total + part
        return jnp.sum(total, axis=1)

    def pick_first(step, carry):
        for at in range(PICK_UNROLL):
            q = step * PICK_UNROLL + at
            sticks[q] = pick(q, range_ref[2, q], NCH)
        return carry

    def pick_rest(q, carry):
        def more(p, inner):
            sticks[q] += pick(q, range_ref[2, q] + p, 1)
            return inner

        return lax.fori_loop(NCH, range_ref[3, q], more, carry)

    lax.fori_loop(0, GROUPS // PICK_UNROLL, pick_first, 0)
    lax.fori_loop(0, GROUPS, pick_rest, 0)

    for t in range(TILES):
        for g in range(4):
            mixed = swap_chunks([sticks[t * 8 + c, :, g * 128:(g + 1) * 128] for c in range(8)])
            for i in range(8):
                out_ref[g * 8 + i, t * ROWS:(t + 1) * ROWS, :] = mixed[i]


def apply_field(ranges, recv, field):
    vmem = pl.BlockSpec(memory_space=pltpu.VMEM)
    return pl.pallas_call(
        field_kernel,
        in_specs=[pl.BlockSpec(memory_space=pltpu.SMEM)] + [vmem] * 6,
        out_specs=vmem,
        out_shape=jax.ShapeDtypeStruct((PW, 48, 128), F32),
        scratch_shapes=[
            pltpu.VMEM((GROUPS + NQ - 1, 2 * ROWS, 16, 512), BF16),
            pltpu.VMEM((GROUPS + NQ - 1, 256, 512), BF16),
            pltpu.VMEM((GROUPS + NQ - 1, 16, 512), BF16),
            pltpu.VMEM((GROUPS + NQ - 1, 16, 512), BF16),
            pltpu.VMEM((ROWS, GX, GY), F32),
            pltpu.VMEM((ROWS, GX + 16 * (NCH - 1), 512), BF16),
            pltpu.VMEM((GROUPS, ROWS, 512), F32),
        ],
        compiler_params=pltpu.CompilerParams(vmem_limit_bytes=56 << 20),
        cost_estimate=pl.CostEstimate(flops=35 * 10 ** 9, bytes_accessed=8 << 20, transcendentals=0),
        name="apply_field",
    )(ranges, recv, field, *plane_tables())


def ranges_of(columns):
    chunk = jnp.floor(fold(jnp.floor(columns * (1.0 / GY)))[0] * 0.125).astype(jnp.int32)
    chunk = chunk.reshape(PW, GROUPS, 16)
    first = jnp.min(chunk, axis=(0, 2))
    last = jnp.max(chunk, axis=(0, 2))
    at = jnp.arange(GROUPS, dtype=jnp.int32)[:, None]
    start = jnp.sum(jnp.where(last[None] < at, 1, 0), axis=1)
    end = jnp.sum(jnp.where(first[None] <= at, 1, 0), axis=1)
    start = jnp.minimum(start, GROUPS - 1)
    return jnp.stack([start, end - start, first, last - first + 1])


def centred(values, length):
    return jnp.where(values < length // 2, values, values - length)


def kinetic_kernel(slot_ref, coef_ref, all_ref, owned_ref, kinetic_ref, sums_ref):
    slot = slot_ref[...].astype(F32)
    z = jnp.floor((slot + 0.5) * (1.0 / STICKS))
    s = slot - z * STICKS
    tile = jnp.floor(s * (1.0 / 128.0))
    lane = (s - tile * 128.0).astype(jnp.int32)
    owned = owned_ref[...].astype(F32)
    x = jnp.floor(owned * (1.0 / GY))
    y = centred(owned - x * GY, GY)
    x = centred(x, GX)
    flat = x * x + y * y
    square = jnp.zeros((128, 128), F32)
    for t in range(TILES):
        line = jnp.broadcast_to(flat[:, t * 128:(t + 1) * 128], (128, 128))
        square = jnp.where(tile == t, jnp.take_along_axis(line, lane, axis=1), square)
    z = centred(z, GZ)
    kinetic = (square + z * z) * (KIN_MAX / 3.0 / 16384.0)
    kinetic_ref[...] = kinetic
    c_re = coef_ref[0]
    c_im = coef_ref[1]
    for a in range(4):
        real = all_ref[a, 0] * c_re + all_ref[a, 1] * c_im
        imag = all_ref[a, 0] * c_im - all_ref[a, 1] * c_re
        for at, value in ((a, real * kinetic), (4 + a, imag * kinetic), (8 + a, real), (12 + a, imag)):
            sums_ref[at:at + 1, :] = jnp.sum(value, axis=0, keepdims=True)


def kinetic_part(slot, coef, everyone, owned):
    vmem = pl.BlockSpec(memory_space=pltpu.VMEM)
    return pl.pallas_call(
        kinetic_kernel,
        in_specs=[vmem] * 4,
        out_specs=[vmem, vmem],
        out_shape=[jax.ShapeDtypeStruct((128, 128), F32), jax.ShapeDtypeStruct((16, 128), F32)],
        cost_estimate=pl.CostEstimate(flops=10 ** 6, bytes_accessed=1 << 20, transcendentals=0),
        name="kinetic_part",
    )(slot, coef, everyone, owned)


def gram_kernel(sums_ref, all_ref, worked_ref, out_ref, total):
    step = pl.program_id(0)

    @pl.when(step == 0)
    def _():
        total[...] = jnp.zeros_like(total)

    span = PW // GRAM_STEPS
    here = pl.ds(pl.multiple_of(step * span, span), span)
    worked = worked_ref[here].reshape(span * TILES, 2, PLANES, 128)
    out_ref[here, :TILES * ROWS, :] = worked_ref[here]
    w_re = worked[:, 0]
    w_im = worked[:, 1]
    for a in range(4):
        lines = all_ref[a, :, :TILES * ROWS, :].reshape(span * TILES, 2, PLANES, 128)
        a_re = lines[:, 0]
        a_im = lines[:, 1]
        total[a] += jnp.sum(a_re * w_re + a_im * w_im, axis=0)
        total[4 + a] += jnp.sum(a_re * w_im - a_im * w_re, axis=0)

    @pl.when(step == pl.num_programs(0) - 1)
    def _():
        scale = 1.0 / (GX * GY * GZ)
        local_sums = jnp.concatenate(
            [jnp.sum(total[a], axis=0, keepdims=True) for a in range(8)] + [jnp.zeros((8, 128), F32)], axis=0) * scale
        lines = jnp.concatenate([local_sums + sums_ref[...], jnp.zeros((112, 128), F32)], axis=0)
        line = jnp.sum(jnp.transpose(lines), axis=0, keepdims=True)
        out_ref[:, TILES * ROWS:, :] = jnp.broadcast_to(line[None], (PW, 8, 128))


def gram_part(sums, everyone, worked):
    span = PW // GRAM_STEPS
    return pl.pallas_call(
        gram_kernel,
        grid=(GRAM_STEPS,),
        in_specs=[
            pl.BlockSpec((16, 128), lambda i: (0, 0)),
            pl.BlockSpec((4, span, 56, 128), lambda i: (0, i, 0, 0)),
            pl.BlockSpec((PW, 48, 128), lambda i: (0, 0, 0)),
        ],
        out_specs=pl.BlockSpec((PW, 56, 128), lambda i: (0, 0, 0)),
        out_shape=jax.ShapeDtypeStruct((PW, 56, 128), F32),
        scratch_shapes=[pltpu.VMEM((8, PLANES, 128), F32)],
        compiler_params=pltpu.CompilerParams(vmem_limit_bytes=32 << 20),
        cost_estimate=pl.CostEstimate(flops=10 ** 7, bytes_accessed=6 << 20, transcendentals=0),
        name="gram_part",
    )(sums, everyone, worked)


def base_kernel(kinetic_ref, coef_ref, proj_ref, coupled_ref, out_ref):
    kinetic = kinetic_ref[...]
    p_re = proj_ref[0]
    p_im = proj_ref[1]
    w_re = coupled_ref[0]
    w_im = coupled_ref[1]
    far_re = jnp.sum(p_re * w_re - p_im * w_im, axis=0, keepdims=True)
    far_im = jnp.sum(p_re * w_im + p_im * w_re, axis=0, keepdims=True)
    out_ref[0] = kinetic * coef_ref[0] + far_re
    out_ref[1] = kinetic * coef_ref[1] + far_im


def base_part(kinetic, coef, proj, coupled):
    return pl.pallas_call(
        base_kernel,
        grid=(COEFS // KC,),
        in_specs=[
            pl.BlockSpec((1, KC), lambda i: (0, i)),
            pl.BlockSpec((2, 1, KC), lambda i: (0, 0, i)),
            pl.BlockSpec((2, PROJ, KC), lambda i: (0, 0, i)),
            pl.BlockSpec((2, PROJ, 1), lambda i: (0, 0, 0)),
        ],
        out_specs=pl.BlockSpec((2, 1, KC), lambda i: (0, 0, i)),
        out_shape=jax.ShapeDtypeStruct((2, 1, COEFS), F32),
        compiler_params=pltpu.CompilerParams(vmem_limit_bytes=32 << 20),
        cost_estimate=pl.CostEstimate(flops=10 ** 7, bytes_accessed=10 << 20, transcendentals=0),
        name="base_part",
    )(kinetic, coef, proj, coupled)


def collect_kernel(span_ref, key_ref, recv_ref, owned_ref, table_ref, base_ref, far_ref, out_ref, sums_ref,
                   values, found_re, found_im):
    sums_ref[...] = jnp.sum(recv_ref[:, TILES * ROWS:, :], axis=0) + far_ref[...]
    order, _ = rank_of(owned_ref[...].astype(F32))
    order = order.astype(BF16)
    lines = jnp.concatenate(
        [recv_ref[:, t * ROWS:(t + 1) * ROWS, :].reshape(512, 128) for t in range(TILES)], axis=1)
    high, low = split(lines)
    back = mm(table_ref[...], jnp.concatenate([high, high, low], axis=0))
    for at, part in enumerate(split(back)):
        part = mm(part, order).astype(BF16)
        for ri in range(2):
            for t in range(TILES):
                values[ri, t * 256:(t + 1) * 256, at * 128:(at + 1) * 128] = part[
                    ri * 256:(ri + 1) * 256, t * 128:(t + 1) * 128]
    values[:, SLOT_ROWS:, :] = jnp.zeros((2, WINDOW, 256), BF16)

    lane_of = iota((128, 1024), 0).astype(BF16)
    row_of = iota((WINDOW, 1024), 0)

    def one(step, carry):
        at = pl.ds(step, 1)
        for half in range(2):
            block = step * 2 + half
            key = jnp.concatenate([key_ref[8 * half + v, at, :] for v in range(8)], axis=1)
            row, lane = key_parts(key)
            hit = jnp.where(lane_of == lane.astype(BF16), jnp.ones((), BF16), jnp.zeros((), BF16))
            hit = jnp.concatenate([hit, hit], axis=0)

            def fetch(first):
                first = pl.multiple_of(first, 16)
                here = pl.ds(first, WINDOW)
                got = mm(jnp.concatenate([values[0, here, :], values[1, here, :]], axis=0), hit)
                mine = row_of == row - first.astype(F32)
                return (jnp.sum(jnp.where(mine, got[:WINDOW], 0.0), axis=0, keepdims=True),
                        jnp.sum(jnp.where(mine, got[WINDOW:], 0.0), axis=0, keepdims=True))

            first = span_ref[0, block]

            def put(pair):
                for v in range(8):
                    found_re[8 * half + v, at, :] = pair[0][:, v * 128:(v + 1) * 128]
                    found_im[8 * half + v, at, :] = pair[1][:, v * 128:(v + 1) * 128]

            def more(p, inner):
                pair = fetch(first + p * WINDOW)
                for v in range(8):
                    found_re[8 * half + v, at, :] += pair[0][:, v * 128:(v + 1) * 128]
                    found_im[8 * half + v, at, :] += pair[1][:, v * 128:(v + 1) * 128]
                return inner

            put(fetch(first))
            lax.fori_loop(1, span_ref[1, block], more, 0)
        return carry

    lax.fori_loop(0, 8, one, 0)
    scale = 1.0 / (GX * GY * GZ)
    home = []
    for v in range(16):
        key = key_ref[v]
        home.append(key - jnp.floor(key * (1.0 / 128.0)) * 128.0)
    _, (real, imag) = sort_rows(home, [[found_re[v] for v in range(16)], [found_im[v] for v in range(16)]])
    for v in range(16):
        here = slice(v * 8, (v + 1) * 8)
        out_ref[0, here, :] = base_ref[0, here, :] + real[v] * scale
        out_ref[1, here, :] = base_ref[1, here, :] + imag[v] * scale


def collect(span, key, recv, owned, base, far):
    vmem = pl.BlockSpec(memory_space=pltpu.VMEM)
    return pl.pallas_call(
        collect_kernel,
        in_specs=[pl.BlockSpec(memory_space=pltpu.SMEM)] + [vmem] * 6,
        out_specs=[vmem, vmem],
        out_shape=[jax.ShapeDtypeStruct((2, 128, 128), F32), jax.ShapeDtypeStruct((8, 128), F32)],
        scratch_shapes=[
            pltpu.VMEM((2, SLOT_ROWS + WINDOW, 256), BF16),
            pltpu.VMEM((16, 8, 128), F32),
            pltpu.VMEM((16, 8, 128), F32),
        ],
        compiler_params=pltpu.CompilerParams(vmem_limit_bytes=48 << 20),
        cost_estimate=pl.CostEstimate(flops=6 * 10 ** 9, bytes_accessed=4 << 20, transcendentals=0),
        name="collect",
    )(span, key, recv, owned, jnp.asarray(collect_table()), base, far)


def local(wave_coef, projector, potential, grid_slot, stick_column, proj_atom, coupling):
    owned = lax.dynamic_slice_in_dim(stick_column, lax.axis_index("pw") * STICKS, STICKS).reshape(1, STICKS)
    slot = grid_slot.reshape(128, 128)
    coef = wave_coef.reshape(2, 128, 128)
    everyone = lax.all_gather(wave_coef.reshape(1, 2 * COEFS), "band", axis=0, tiled=True)
    sent, key, span = spread_sticks(slot, wave_coef, projector, owned)
    recv = lax.all_to_all(sent, "pw", split_axis=0, concat_axis=0, tiled=True)
    kinetic, sums = kinetic_part(slot, coef, everyone.reshape(4, 2, 128, 128), owned)

    every_stick = lax.all_gather(recv, "band", axis=0)
    worked = apply_field(ranges_of(recv[:, 49:52, :].reshape(PW, STICKS)), recv, potential)
    payload = gram_part(sums, every_stick, worked)
    returned = lax.all_to_all(payload, "pw", split_axis=0, concat_axis=0, tiled=True)

    becp = jnp.sum(recv[:, 48, :], axis=0).reshape(2, PROJ)
    same_atom = proj_atom[:, None] == proj_atom[None, :]
    matrix = jnp.where(same_atom, 0.5 * (coupling + coupling.T), 0.0)
    coupled = jnp.sum(matrix[None] * becp[:, None, :], axis=2, keepdims=True)
    base = base_part(kinetic.reshape(1, COEFS), wave_coef, projector, coupled)
    every_becp = jnp.sum(every_stick[:, :, 48, :], axis=1).reshape(4, 2, PROJ)
    line = coupled.reshape(1, 2, PROJ)
    far_re = jnp.sum(every_becp * line, axis=(1, 2))
    far_im = jnp.sum(every_becp[:, 0] * line[:, 1] - every_becp[:, 1] * line[:, 0], axis=1)
    far = jnp.concatenate([far_re, far_im, jnp.zeros((120,), F32)]).reshape(1, 128)
    applied, total = collect(span, key, returned, owned, base.reshape(2, 128, 128), far)
    total = total[0, :16].reshape(2, 2, 4, 1)
    return applied.reshape(2, 1, COEFS), total[0], total[1]


def solution(mesh):
    in_specs = (
        P(None, "band", "pw"),
        P(None, None, "pw"),
        P("pw", None, None),
        P("pw"),
        P(),
        P(),
        P(),
    )
    out_specs = (P(None, "band", "pw"), P(None, None, "band"), P(None, None, "band"))
    return jax.shard_map(local, mesh=mesh, in_specs=in_specs, out_specs=out_specs, check_vma=False)
```

```python
import jax
import jax.numpy as jnp
import ml_dtypes
import numpy as np
from jax import lax
from jax.experimental import pallas as pl
from jax.experimental.pallas import tpu as pltpu
from jax.sharding import PartitionSpec as P

GX = 256
GY = 256
GZ = 256
KIN_MAX = 2.0
PRECISE = lax.Precision.HIGHEST

PW = 32
STICKS = 384
COEFS = 16384
PROJ = 64
PLANES = GZ // PW
ROWS = 2 * PLANES
KC = 2048
WINDOW = 256
SLOT_ROWS = 768
TILES = STICKS // 128
GROUPS = 24
CHUNKS = 16
NQ = 4
NCH = 3
PAIR = 2
PLACE_UNROLL = 4
PICK_UNROLL = 4
GRAM_STEPS = 4
F32 = jnp.float32
BF16 = jnp.bfloat16
NN = (((1,), (0,)), ((), ()))
NT = (((1,), (1,)), ((), ()))


def mm(left, right, dims=NN):
    return lax.dot_general(left, right, dims, preferred_element_type=F32)


def split(value):
    high = value.astype(BF16)
    low = (value - high.astype(F32)).astype(BF16)
    return high, low


def split_table(table):
    high = table.astype(np.float32).astype(ml_dtypes.bfloat16)
    low = (table - high.astype(np.float64)).astype(np.float32).astype(ml_dtypes.bfloat16)
    return high, low


def trig():
    n = np.arange(256)
    angle = 2.0 * np.pi * (np.outer(n, n) % 256) / 256.0
    return np.cos(angle), np.sin(angle)


def folded_table():
    c, s = trig()
    return np.concatenate([c[:128], c[128:129], s[1:128]], axis=0)


def plane_tables():
    table = folded_table()
    order = [128 * part + 8 * chunk + i for chunk in range(CHUNKS) for part in range(2) for i in range(8)]
    table_x = table[order]

    def left(values):
        high, low = split_table(values)
        return jnp.asarray(np.concatenate([high, low, high], axis=1))

    def right(values):
        high, low = split_table(values)
        return jnp.asarray(np.concatenate([high, low, high], axis=0))

    return right(table), right(table.T), left(table_x.T), left(table_x)


def spread_table():
    c, s = trig()
    rows = np.concatenate(
        [np.concatenate([np.concatenate([c[z], -s[z]])[None] if part == 0 else np.concatenate([s[z], c[z]])[None]
                         for z in range(d * PLANES, (d + 1) * PLANES)])
         for d in range(PW) for part in range(2)])
    high, low = split_table(rows)
    return np.concatenate([high, low, high], axis=1)


def collect_table():
    c, s = trig()
    full = np.zeros((512, 512))
    for d in range(PW):
        zs = np.arange(d * PLANES, (d + 1) * PLANES)
        at = d * ROWS
        full[:256, at:at + PLANES] = c[:, zs]
        full[:256, at + PLANES:at + ROWS] = s[:, zs]
        full[256:, at:at + PLANES] = -s[:, zs]
        full[256:, at + PLANES:at + ROWS] = c[:, zs]
    high, low = split_table(full)
    return np.concatenate([high, low, high], axis=1)


def iota(shape, dim):
    return lax.broadcasted_iota(jnp.int32, shape, dim).astype(F32)


def sort_rows(keys, values):
    keys = list(keys)
    values = [list(each) for each in values]
    sub = lax.broadcasted_iota(jnp.int32, (8, 128), 0)
    size = 2
    while size <= 128:
        dist = size // 2
        while dist >= 1:
            if dist < 16:
                for one in range(16):
                    if one & dist:
                        continue
                    two = one | dist
                    swap = keys[one] > keys[two]
                    if size < 16:
                        if one & size:
                            swap = keys[one] < keys[two]
                    elif size < 128:
                        swap = jnp.where((sub & (size // 16)) == 0, keys[one] - keys[two], keys[two] - keys[one]) > 0.0
                    for each in [keys] + values:
                        each[one], each[two] = (jnp.where(swap, each[two], each[one]),
                                                jnp.where(swap, each[one], each[two]))
            else:
                hop = dist // 16
                low = (sub & hop) == 0
                rising = (sub & (size // 16)) == 0 if size < 128 else jnp.full((8, 128), True)
                least = jnp.where(low == rising, 1.0, -1.0)

                def other(x):
                    return jnp.where(low, pltpu.roll(x, 8 - hop, 0), pltpu.roll(x, hop, 0))

                for one in range(16):
                    swap = (keys[one] - other(keys[one])) * least > 0.0
                    for each in [keys] + values:
                        each[one] = jnp.where(swap, other(each[one]), each[one])
            dist //= 2
        size *= 2
    return keys, values


def sorted_row(ref, block):
    at = pl.ds(block // 2, 1)
    half = 8 * (block % 2)
    return jnp.concatenate([ref[half + v, at, :] for v in range(8)], axis=1)


def key_parts(key):
    row = jnp.floor(key * (1.0 / 16384.0))
    rest = key - row * 16384.0
    return row, jnp.floor(rest * (1.0 / 128.0))


def fold(x):
    key = jnp.where(x == 128.0, 0.0, jnp.minimum(x, 256.0 - x))
    even = jnp.where(x == 128.0, -1.0, key)
    odd = jnp.where(x == 0.0, -1.0, key)
    return key, even, odd, jnp.where(x > 128.0, -1.0, 1.0)


def rank_of(owned):
    wide = jnp.broadcast_to(owned, (128, STICKS))
    down = jnp.transpose(wide)[:, :1]

    def sort_key(column):
        return fold(jnp.floor(column * (1.0 / GY)))[0] * 65536.0 + column

    key = sort_key(owned)
    key_down = sort_key(down)
    rank_row = jnp.sum(jnp.where(key_down < key, 1.0, 0.0), axis=0, keepdims=True)
    order = jnp.where(iota((STICKS, STICKS), 0) == rank_row, 1.0, 0.0)
    rank_col = jnp.sum(jnp.where(key < key_down, 1.0, 0.0), axis=1, keepdims=True)
    ordered = jnp.sum(jnp.where(iota((STICKS, STICKS), 1) == rank_col, down, 0.0), axis=0, keepdims=True)
    return order, ordered


def centred(values, length):
    return jnp.where(values < length // 2, values, values - length)


def owned_row(stick_ref):
    first = lax.axis_index("pw") * TILES
    return jnp.concatenate([stick_ref[pl.ds(first + t, 1), :] for t in range(TILES)], axis=1).astype(F32)


def kinetic_of(z, tile, lane, owned):
    x = jnp.floor(owned * (1.0 / GY))
    y = centred(owned - x * GY, GY)
    x = centred(x, GX)
    flat = x * x + y * y
    square = jnp.zeros((128, 128), F32)
    for t in range(TILES):
        line = jnp.broadcast_to(flat[:, t * 128:(t + 1) * 128], (128, 128))
        square = jnp.where(tile == t, jnp.take_along_axis(line, lane.astype(jnp.int32), axis=1), square)
    z = centred(z, GZ)
    return (square + z * z) * (KIN_MAX / 3.0 / 16384.0)


def spread_kernel(slot_ref, tile_ref, coef_ref, proj_ref, stick_ref, table_ref, out_ref, key_ref, kinetic_ref,
                  span_ref, part_re, part_im, acc, becp):
    step = pl.program_id(0)

    @pl.when(step == 0)
    def _():
        slot = slot_ref[...].astype(F32)
        z = jnp.floor((slot + 0.5) * (1.0 / STICKS))
        s = slot - z * STICKS
        tile = jnp.floor(s * (1.0 / 128.0))
        lane = s - tile * 128.0
        place = (tile * 256.0 + z) * 128.0 + lane
        kinetic = kinetic_of(z, tile, lane, owned_row(stick_ref))
        kinetic_ref[...] = kinetic
        for d in range(PW):
            here = slice(d * 4, d * 4 + 4)
            out_ref[d, 52:56, :] = kinetic[here]
            out_ref[d, 56:60, :] = tile_ref[0, here, :]
            out_ref[d, 60:64, :] = tile_ref[1, here, :]
        row = iota((128, 128), 0)
        array = jnp.floor(row * 0.125)
        key = place * 128.0 + (row - array * 8.0) * 16.0 + array

        def rows(x):
            return [x[v * 8:(v + 1) * 8] for v in range(16)]

        keys, (real, imag) = sort_rows(rows(key), [rows(tile_ref[0]), rows(tile_ref[1])])
        for v in range(16):
            key_ref[v] = keys[v]
            part_re[v] = real[v]
            part_im[v] = imag[v]
        for block in range(16):
            half = 8 * (block % 2)
            at = block // 2
            first = jnp.min(key_parts(keys[half][at:at + 1])[0]).astype(jnp.int32)
            last = jnp.max(key_parts(keys[half + 7][at:at + 1])[0]).astype(jnp.int32)
            first = (first >> 4) << 4
            span_ref[0, block] = first
            span_ref[1, block] = ((last - first) >> 8) + 1
        acc[...] = jnp.zeros_like(acc)
        becp[...] = jnp.zeros_like(becp)

    none = jnp.zeros((), BF16)
    lane_of = (iota((128, 1024), 0)).astype(BF16)
    row_of = (iota((WINDOW, 1024), 0) - 128.0).astype(BF16)
    for half in range(2):
        block = step * 2 + half
        at = pl.ds(step, 1)
        key = jnp.concatenate([key_ref[8 * half + v, at, :] for v in range(8)], axis=1)
        real = jnp.concatenate([part_re[8 * half + v, at, :] for v in range(8)], axis=1)
        imag = jnp.concatenate([part_im[8 * half + v, at, :] for v in range(8)], axis=1)
        row, lane = key_parts(key)
        hit = lane_of == lane.astype(BF16)
        re_hi, re_lo = split(real)
        im_hi, im_lo = split(imag)
        placed = jnp.concatenate([jnp.where(hit, part, none) for part in (re_hi, im_hi, re_lo, im_lo)], axis=0)

        def add(first):
            first = pl.multiple_of(first, 16)
            want = row - (first + 128).astype(F32)
            hot = jnp.where(row_of == want.astype(BF16), jnp.ones((), BF16), none)
            acc[pl.ds(first, WINDOW), :] += mm(hot, placed, NT)

        first = span_ref[0, block]
        add(first)

        def more(p, carry):
            add(first + p * WINDOW)
            return carry

        lax.fori_loop(1, span_ref[1, block], more, 0)

    c_re = coef_ref[0]
    c_im = coef_ref[1]
    p_re = proj_ref[0]
    p_im = proj_ref[1]
    real = p_re * c_re + p_im * c_im
    imag = p_re * c_im - p_im * c_re
    both = jnp.concatenate([real, imag], axis=0)
    total = both[:, :128]
    for at in range(128, KC, 128):
        total = total + both[:, at:at + 128]
    becp[...] += total

    @pl.when(step == pl.num_programs(0) - 1)
    def _():
        order, ordered = rank_of(owned_row(stick_ref))
        sticks = jnp.concatenate(
            [jnp.concatenate([acc[t * 256:(t + 1) * 256, part * 128:(part + 1) * 128] for t in range(TILES)], axis=1)
             for part in range(4)], axis=0).astype(BF16)
        sticks = mm(sticks, order.astype(BF16), NT).astype(BF16)
        high = sticks[:512]
        low = sticks[512:]
        spread = mm(table_ref[...], jnp.concatenate([high, high, low], axis=0))
        spread = spread.reshape(PW, ROWS, STICKS)
        for t in range(TILES):
            out_ref[:, t * ROWS:(t + 1) * ROWS, :] = spread[:, :, t * 128:(t + 1) * 128]
        line = jnp.sum(jnp.transpose(becp[...]), axis=0, keepdims=True)
        extra = jnp.concatenate(
            [line] + [ordered[:, t * 128:(t + 1) * 128] for t in range(TILES)], axis=0)
        out_ref[:, TILES * ROWS:TILES * ROWS + 4, :] = jnp.broadcast_to(extra[None], (PW, 4, 128))


def spread_sticks(slot, coef, proj, stick):
    table = jnp.asarray(spread_table())
    return pl.pallas_call(
        spread_kernel,
        grid=(COEFS // KC,),
        in_specs=[
            pl.BlockSpec((128, 128), lambda i: (0, 0)),
            pl.BlockSpec((2, 128, 128), lambda i: (0, 0, 0)),
            pl.BlockSpec((2, 1, KC), lambda i: (0, 0, i)),
            pl.BlockSpec((2, PROJ, KC), lambda i: (0, 0, i)),
            pl.BlockSpec((PW * TILES, 128), lambda i: (0, 0)),
            pl.BlockSpec((512, 1536), lambda i: (0, 0)),
        ],
        out_specs=[
            pl.BlockSpec((PW, 64, 128), lambda i: (0, 0, 0)),
            pl.BlockSpec((16, 8, 128), lambda i: (0, 0, 0)),
            pl.BlockSpec((128, 128), lambda i: (0, 0)),
            pl.BlockSpec(memory_space=pltpu.SMEM),
        ],
        out_shape=[
            jax.ShapeDtypeStruct((PW, 64, 128), F32),
            jax.ShapeDtypeStruct((16, 8, 128), F32),
            jax.ShapeDtypeStruct((128, 128), F32),
            jax.ShapeDtypeStruct((2, 16), jnp.int32),
        ],
        scratch_shapes=[
            pltpu.VMEM((16, 8, 128), F32),
            pltpu.VMEM((16, 8, 128), F32),
            pltpu.VMEM((SLOT_ROWS + WINDOW, 512), F32),
            pltpu.VMEM((128, 128), F32),
        ],
        compiler_params=pltpu.CompilerParams(vmem_limit_bytes=60 << 20),
        cost_estimate=pl.CostEstimate(flops=6 * 10 ** 9, bytes_accessed=12 << 20, transcendentals=0),
        name="spread_sticks",
    )(slot, coef.reshape(2, 128, 128), coef, proj, stick, table)


def swap_chunks(parts):
    parts = list(parts)
    chunk = lax.broadcasted_iota(jnp.int32, parts[0].shape, 1) // 16
    for bit in (1, 2, 4):
        here = (chunk & bit) == 0
        for a in range(8):
            if a & bit:
                continue
            one, two = parts[a], parts[a | bit]
            parts[a] = jnp.where(here, one, pltpu.roll(two, 16 * bit, 1))
            parts[a | bit] = jnp.where(here, pltpu.roll(one, 128 - 16 * bit, 1), two)
    return parts


def write_bounds(columns, bounds):
    firsts, lasts = [], []
    for column in columns:
        chunk = jnp.floor(fold(jnp.floor(column * (1.0 / GY)))[0] * 0.125)
        firsts.append(jnp.min(chunk, axis=1, keepdims=True))
        lasts.append(jnp.max(chunk, axis=1, keepdims=True))
    first = jnp.broadcast_to(jnp.concatenate(firsts, axis=0), (GROUPS, 128))
    last = jnp.broadcast_to(jnp.concatenate(lasts, axis=0), (GROUPS, 128))
    lane = iota((GROUPS, 128), 1)
    start = jnp.sum(jnp.where(last < lane, 1.0, 0.0), axis=0, keepdims=True)
    end = jnp.sum(jnp.where(first <= lane, 1.0, 0.0), axis=0, keepdims=True)
    more = jnp.zeros((128 - GROUPS, 128), F32)
    first = jnp.transpose(jnp.concatenate([first, more], axis=0))[:1]
    last = jnp.transpose(jnp.concatenate([last, more], axis=0))[:1]
    lines = [jnp.minimum(start, GROUPS - 1.0), end - start, first, last - first + 1.0, jnp.zeros((4, 128), F32)]
    bounds[...] = jnp.concatenate(lines, axis=0).astype(jnp.int32)


def field_kernel(recv_ref, field_hbm, y_in_ref, y_out_ref, x_in_ref, x_out_ref, out_ref,
                 wide, hot, keys, signs, grid, done, sticks, field_ref, bounds, range_ref, field_sem, range_sem):
    field_copy = pltpu.make_async_copy(field_hbm, field_ref, field_sem)
    field_copy.start()
    cells = []
    for g in range(4):
        mixed = swap_chunks([recv_ref[g * 8 + i, TILES * ROWS:TILES * ROWS + 8, :] for i in range(8)])
        cells.append(mixed)
    columns = [jnp.concatenate([cells[g][q % 8][1 + q // 8:2 + q // 8] for g in range(4)], axis=1)
               for q in range(GROUPS)]
    write_bounds(columns, bounds)
    range_copy = pltpu.make_async_copy(bounds, range_ref, range_sem)
    range_copy.start()
    one_hot = iota((128, 512), 0).astype(BF16)
    zero = jnp.zeros((), BF16)
    for t in range(TILES):
        mixed = [swap_chunks([recv_ref[g * 8 + i, t * ROWS:(t + 1) * ROWS, :] for i in range(8)]) for g in range(4)]
        for c in range(8):
            q = t * 8 + c
            values = jnp.concatenate([mixed[g][c] for g in range(4)], axis=1)
            high, low = split(values)
            both = jnp.concatenate([high.astype(F32), low.astype(F32)], axis=0)
            wide[q] = jnp.broadcast_to(both[:, None, :], (2 * ROWS, 16, 512)).astype(BF16)
            column = columns[q]
            x = jnp.floor(column * (1.0 / GY))
            y = column - x * GY
            _, even, odd, sign = fold(x)
            upper = iota((16, 512), 0) < 8.0
            keys[q] = jnp.where(upper, even, odd).astype(BF16)
            signs[q] = jnp.where(upper, 1.0, sign).astype(BF16)
            _, even, odd, sign = fold(y)
            hot[q, :128, :] = jnp.where(one_hot == even.astype(BF16), jnp.ones((), BF16), zero)
            hot[q, 128:, :] = jnp.where(one_hot == odd.astype(BF16), sign.astype(BF16), zero)
    for q in range(GROUPS, GROUPS + NQ - 1):
        wide[q] = jnp.zeros((2 * ROWS, 16, 512), BF16)
        hot[q] = jnp.zeros((256, 512), BF16)
        keys[q] = jnp.full((16, 512), -1.0, BF16)
        signs[q] = jnp.zeros((16, 512), BF16)
    done[:, GX:, :] = jnp.zeros((ROWS, 16 * (NCH - 1), 512), BF16)

    step_of = iota((16, 512), 0)
    step_of = jnp.where(step_of < 8.0, step_of, step_of - 8.0)

    def place(chunk, first, groups):
        want = (step_of + (chunk * 8).astype(F32)).astype(BF16)
        masked = []
        for j in range(groups):
            mine = jnp.where(keys[first + j] == want, signs[first + j], zero)
            masked.append((wide[first + j] * mine[None]).reshape(2 * ROWS * 16, 512))
        got = mm(jnp.concatenate(masked, axis=1),
                 jnp.concatenate([hot[first + j] for j in range(groups)], axis=1), NT)
        got = got.reshape(2, ROWS, 16, 256)
        return got[0] + got[1]

    def rows_of(chunk):
        return pl.ds(pl.multiple_of(chunk * 16, 16), 16)

    def place_first(step, carry):
        for at in range(PLACE_UNROLL):
            chunk = step * PLACE_UNROLL + at
            grid[:, rows_of(chunk), :] = place(chunk, range_ref[0, chunk], NQ)
        return carry

    def place_rest(chunk, carry):
        def more(p, inner):
            grid[:, rows_of(chunk), :] += place(chunk, range_ref[0, chunk] + p, 1)
            return inner

        return lax.fori_loop(NQ, range_ref[1, chunk], more, carry)

    range_copy.wait()
    lax.fori_loop(0, CHUNKS // PLACE_UNROLL, place_first, 0)
    lax.fori_loop(0, CHUNKS, place_rest, 0)

    row = lax.broadcasted_iota(jnp.int32, (256, 256), 0)
    lane = lax.broadcasted_iota(jnp.int32, (256, 256), 1)
    even_x = ((row & 8) == 0) | (row == 8)
    even_y = lane <= 128

    def along_y(re, im, table):
        high, low = split(jnp.concatenate([re, im], axis=0))
        got = mm(jnp.concatenate([high, high, low], axis=1), table[...])
        return got[:256], got[256:]

    def along_x(re, im, table):
        high, low = split(jnp.concatenate([re, im], axis=1))
        got = mm(table[...], jnp.concatenate([high, high, low], axis=0))
        return got[:, :256], got[:, 256:]

    def plane(zz):
        re = grid[zz]
        im = grid[PLANES + zz]
        re, im = along_y(jnp.where(even_y, re, -im), jnp.where(even_y, im, re), y_in_ref)
        re, im = along_x(jnp.where(even_x, re, -im), jnp.where(even_x, im, re), x_in_ref)
        field = field_ref[zz]
        re, im = along_x(re * field, im * field, x_out_ref)
        re, im = along_y(jnp.where(even_x, re, im), jnp.where(even_x, im, -re), y_out_ref)
        high, low = split(jnp.where(even_y, re, im))
        done[zz, :GX, :256] = high
        done[zz, :GX, 256:] = low
        high, low = split(jnp.where(even_y, im, -re))
        done[PLANES + zz, :GX, :256] = high
        done[PLANES + zz, :GX, 256:] = low

    def planes(pair, carry):
        for at in range(PAIR):
            plane(pair * PAIR + at)
        return carry

    field_copy.wait()
    lax.fori_loop(0, PLANES // PAIR, planes, 0)

    def pick(q, first, chunks):
        both = jnp.concatenate([hot[q], hot[q]], axis=0)
        key = keys[q].astype(F32)
        sign = signs[q].astype(F32)
        here = pl.ds(pl.multiple_of(first * 16, 16), 16 * chunks)
        lines = done[:, here, :].reshape(ROWS * 16 * chunks, 512)
        got = mm(lines, both).reshape(ROWS, 2 * chunks, 8, 512)
        total = None
        for j in range(chunks):
            want = step_of + ((first + j) * 8).astype(F32)
            mine = jnp.where(key == want, sign, 0.0)
            part = got[:, 2 * j] * mine[None, :8] + got[:, 2 * j + 1] * mine[None, 8:]
            total = part if total is None else total + part
        return jnp.sum(total, axis=1)

    def pick_first(step, carry):
        for at in range(PICK_UNROLL):
            q = step * PICK_UNROLL + at
            sticks[q] = pick(q, range_ref[2, q], NCH)
        return carry

    def pick_rest(q, carry):
        def more(p, inner):
            sticks[q] += pick(q, range_ref[2, q] + p, 1)
            return inner

        return lax.fori_loop(NCH, range_ref[3, q], more, carry)

    lax.fori_loop(0, GROUPS // PICK_UNROLL, pick_first, 0)
    lax.fori_loop(0, GROUPS, pick_rest, 0)

    for t in range(TILES):
        for g in range(4):
            mixed = swap_chunks([sticks[t * 8 + c, :, g * 128:(g + 1) * 128] for c in range(8)])
            for i in range(8):
                out_ref[g * 8 + i, t * ROWS:(t + 1) * ROWS, :] = mixed[i]


def apply_field(recv, field):
    vmem = pl.BlockSpec(memory_space=pltpu.VMEM)
    return pl.pallas_call(
        field_kernel,
        in_specs=[vmem, pl.BlockSpec(memory_space=pl.ANY)] + [vmem] * 4,
        out_specs=vmem,
        out_shape=jax.ShapeDtypeStruct((PW, 48, 128), F32),
        scratch_shapes=[
            pltpu.VMEM((GROUPS + NQ - 1, 2 * ROWS, 16, 512), BF16),
            pltpu.VMEM((GROUPS + NQ - 1, 256, 512), BF16),
            pltpu.VMEM((GROUPS + NQ - 1, 16, 512), BF16),
            pltpu.VMEM((GROUPS + NQ - 1, 16, 512), BF16),
            pltpu.VMEM((ROWS, GX, GY), F32),
            pltpu.VMEM((ROWS, GX + 16 * (NCH - 1), 512), BF16),
            pltpu.VMEM((GROUPS, ROWS, 512), F32),
            pltpu.VMEM((PLANES, GX, GY), F32),
            pltpu.VMEM((8, 128), jnp.int32),
            pltpu.SMEM((8, 128), jnp.int32),
            pltpu.SemaphoreType.DMA,
            pltpu.SemaphoreType.DMA,
        ],
        compiler_params=pltpu.CompilerParams(vmem_limit_bytes=60 << 20),
        cost_estimate=pl.CostEstimate(flops=35 * 10 ** 9, bytes_accessed=8 << 20, transcendentals=0),
        name="apply_field",
    )(recv, field, *plane_tables())


def gram_kernel(own_ref, one_ref, two_ref, three_ref, worked_ref, out_ref, becp_ref, total, small):
    step = pl.program_id(0)

    @pl.when(step == 0)
    def _():
        total[...] = jnp.zeros_like(total)
        small[...] = jnp.zeros_like(small)
        becp_ref[...] = jnp.zeros_like(becp_ref)

    span = PW // GRAM_STEPS
    here = pl.ds(pl.multiple_of(step * span, span), span)
    worked = worked_ref[...].reshape(span * TILES, 2, PLANES, 128)
    out_ref[here, :TILES * ROWS, :] = worked_ref[...]
    w_re = worked[:, 0]
    w_im = worked[:, 1]
    upper = lax.broadcasted_iota(jnp.int32, (span * 8, 128), 0) % 8 < 4
    mine = own_ref[:, 56:, :].reshape(span * 8, 128)
    weight = own_ref[:, 48:56, :].reshape(span * 8, 128)

    def halves(x):
        return pltpu.roll(x.reshape(span, 8, 128), 4, 1).reshape(span * 8, 128)

    turned = jnp.where(upper, halves(mine), -halves(mine))
    weight = jnp.where(upper, halves(weight), weight)
    for a, ref in enumerate((own_ref, one_ref, two_ref, three_ref)):
        lines = ref[:, :TILES * ROWS, :].reshape(span * TILES, 2, PLANES, 128)
        a_re = lines[:, 0]
        a_im = lines[:, 1]
        total[a] += jnp.sum(a_re * w_re + a_im * w_im, axis=0)
        total[4 + a] += jnp.sum(a_re * w_im - a_im * w_re, axis=0)
        becp_ref[a] += jnp.sum(ref[:, 48:56, :], axis=0)
        coef = ref[:, 56:, :].reshape(span * 8, 128)
        real = coef * mine
        imag = coef * turned
        for at, value in ((a, real * weight), (4 + a, imag * weight), (8 + a, real), (12 + a, imag)):
            small[at] += jnp.sum(value.reshape(span, 8, 128), axis=0)

    @pl.when(step == pl.num_programs(0) - 1)
    def _():
        scale = 1.0 / (GX * GY * GZ)
        lines = [jnp.sum(small[at] + total[at] * scale, axis=0, keepdims=True) for at in range(8)]
        lines += [jnp.sum(small[at], axis=0, keepdims=True) for at in range(8, 16)]
        lines = jnp.concatenate(lines + [jnp.zeros((112, 128), F32)], axis=0)
        line = jnp.sum(jnp.transpose(lines), axis=0, keepdims=True)
        out_ref[:, TILES * ROWS:, :] = jnp.broadcast_to(line[None], (PW, 8, 128))


def gram_part(recv, others, worked):
    span = PW // GRAM_STEPS
    return pl.pallas_call(
        gram_kernel,
        grid=(GRAM_STEPS,),
        in_specs=[pl.BlockSpec((span, 64, 128), lambda i: (i, 0, 0))] * 4 + [
            pl.BlockSpec((span, 48, 128), lambda i: (i, 0, 0)),
        ],
        out_specs=[pl.BlockSpec((PW, 56, 128), lambda i: (0, 0, 0)), pl.BlockSpec((4, 8, 128), lambda i: (0, 0, 0))],
        out_shape=[jax.ShapeDtypeStruct((PW, 56, 128), F32), jax.ShapeDtypeStruct((4, 8, 128), F32)],
        scratch_shapes=[pltpu.VMEM((8, PLANES, 128), F32), pltpu.VMEM((16, 8, 128), F32)],
        compiler_params=pltpu.CompilerParams(vmem_limit_bytes=60 << 20),
        cost_estimate=pl.CostEstimate(flops=10 ** 7, bytes_accessed=6 << 20, transcendentals=0),
        name="gram_part",
    )(recv, *others, worked)


def base_kernel(kinetic_ref, coef_ref, proj_ref, coupled_ref, out_ref):
    kinetic = kinetic_ref[...]
    p_re = proj_ref[0]
    p_im = proj_ref[1]
    w_re = coupled_ref[0]
    w_im = coupled_ref[1]
    far_re = jnp.sum(p_re * w_re - p_im * w_im, axis=0, keepdims=True)
    far_im = jnp.sum(p_re * w_im + p_im * w_re, axis=0, keepdims=True)
    out_ref[0] = kinetic * coef_ref[0] + far_re
    out_ref[1] = kinetic * coef_ref[1] + far_im


def base_part(kinetic, coef, proj, coupled):
    return pl.pallas_call(
        base_kernel,
        grid=(COEFS // KC,),
        in_specs=[
            pl.BlockSpec((1, KC), lambda i: (0, i)),
            pl.BlockSpec((2, 1, KC), lambda i: (0, 0, i)),
            pl.BlockSpec((2, PROJ, KC), lambda i: (0, 0, i)),
            pl.BlockSpec((2, PROJ, 1), lambda i: (0, 0, 0)),
        ],
        out_specs=pl.BlockSpec((2, 1, KC), lambda i: (0, 0, i)),
        out_shape=jax.ShapeDtypeStruct((2, 1, COEFS), F32),
        compiler_params=pltpu.CompilerParams(vmem_limit_bytes=60 << 20),
        cost_estimate=pl.CostEstimate(flops=10 ** 7, bytes_accessed=10 << 20, transcendentals=0),
        name="base_part",
    )(kinetic, coef, proj, coupled)


def collect_kernel(span_ref, key_ref, recv_ref, stick_ref, table_ref, base_ref, far_ref, out_ref, sums_ref,
                   values, found_re, found_im):
    sums_ref[...] = jnp.sum(recv_ref[:, TILES * ROWS:, :], axis=0) + far_ref[...]
    order, _ = rank_of(owned_row(stick_ref))
    order = order.astype(BF16)
    lines = jnp.concatenate(
        [recv_ref[:, t * ROWS:(t + 1) * ROWS, :].reshape(512, 128) for t in range(TILES)], axis=1)
    high, low = split(lines)
    back = mm(table_ref[...], jnp.concatenate([high, high, low], axis=0))
    for at, part in enumerate(split(back)):
        part = mm(part, order).astype(BF16)
        for ri in range(2):
            for t in range(TILES):
                values[ri, t * 256:(t + 1) * 256, at * 128:(at + 1) * 128] = part[
                    ri * 256:(ri + 1) * 256, t * 128:(t + 1) * 128]
    values[:, SLOT_ROWS:, :] = jnp.zeros((2, WINDOW, 256), BF16)

    lane_of = iota((128, 1024), 0).astype(BF16)
    row_of = iota((WINDOW, 1024), 0)

    def one(step, carry):
        at = pl.ds(step, 1)
        for half in range(2):
            block = step * 2 + half
            key = jnp.concatenate([key_ref[8 * half + v, at, :] for v in range(8)], axis=1)
            row, lane = key_parts(key)
            hit = jnp.where(lane_of == lane.astype(BF16), jnp.ones((), BF16), jnp.zeros((), BF16))
            hit = jnp.concatenate([hit, hit], axis=0)

            def fetch(first):
                first = pl.multiple_of(first, 16)
                here = pl.ds(first, WINDOW)
                got = mm(jnp.concatenate([values[0, here, :], values[1, here, :]], axis=0), hit)
                mine = row_of == row - first.astype(F32)
                return (jnp.sum(jnp.where(mine, got[:WINDOW], 0.0), axis=0, keepdims=True),
                        jnp.sum(jnp.where(mine, got[WINDOW:], 0.0), axis=0, keepdims=True))

            first = span_ref[0, block]

            def put(pair):
                for v in range(8):
                    found_re[8 * half + v, at, :] = pair[0][:, v * 128:(v + 1) * 128]
                    found_im[8 * half + v, at, :] = pair[1][:, v * 128:(v + 1) * 128]

            def more(p, inner):
                pair = fetch(first + p * WINDOW)
                for v in range(8):
                    found_re[8 * half + v, at, :] += pair[0][:, v * 128:(v + 1) * 128]
                    found_im[8 * half + v, at, :] += pair[1][:, v * 128:(v + 1) * 128]
                return inner

            put(fetch(first))
            lax.fori_loop(1, span_ref[1, block], more, 0)
        return carry

    lax.fori_loop(0, 8, one, 0)
    scale = 1.0 / (GX * GY * GZ)
    home = []
    for v in range(16):
        key = key_ref[v]
        home.append(key - jnp.floor(key * (1.0 / 128.0)) * 128.0)
    _, (real, imag) = sort_rows(home, [[found_re[v] for v in range(16)], [found_im[v] for v in range(16)]])
    for v in range(16):
        here = slice(v * 8, (v + 1) * 8)
        out_ref[0, here, :] = base_ref[0, here, :] + real[v] * scale
        out_ref[1, here, :] = base_ref[1, here, :] + imag[v] * scale


def collect(span, key, recv, stick, base, far):
    vmem = pl.BlockSpec(memory_space=pltpu.VMEM)
    return pl.pallas_call(
        collect_kernel,
        in_specs=[pl.BlockSpec(memory_space=pltpu.SMEM)] + [vmem] * 6,
        out_specs=[vmem, vmem],
        out_shape=[jax.ShapeDtypeStruct((2, 128, 128), F32), jax.ShapeDtypeStruct((8, 128), F32)],
        scratch_shapes=[
            pltpu.VMEM((2, SLOT_ROWS + WINDOW, 256), BF16),
            pltpu.VMEM((16, 8, 128), F32),
            pltpu.VMEM((16, 8, 128), F32),
        ],
        compiler_params=pltpu.CompilerParams(vmem_limit_bytes=60 << 20),
        cost_estimate=pl.CostEstimate(flops=6 * 10 ** 9, bytes_accessed=4 << 20, transcendentals=0),
        name="collect",
    )(span, key, recv, stick, jnp.asarray(collect_table()), base, far)


def local(wave_coef, projector, potential, grid_slot, stick_column, proj_atom, coupling):
    stick = stick_column.reshape(PW * TILES, 128)
    sent, key, kinetic, span = spread_sticks(grid_slot.reshape(128, 128), wave_coef, projector, stick)
    recv = lax.all_to_all(sent, "pw", split_axis=0, concat_axis=0, tiled=True)
    others = [lax.ppermute(recv, "band", [(b, b ^ m) for b in range(4)]) for m in (1, 2, 3)]
    worked = apply_field(recv, potential)
    payload, becp = gram_part(recv, others, worked)
    returned = lax.all_to_all(payload, "pw", split_axis=0, concat_axis=0, tiled=True)

    becp = becp[:, 0, :].reshape(4, 2, PROJ)
    same_atom = proj_atom[:, None] == proj_atom[None, :]
    matrix = jnp.where(same_atom, 0.5 * (coupling + coupling.T), 0.0)
    coupled = jnp.sum(matrix[None] * becp[0][:, None, :], axis=2, keepdims=True)
    base = base_part(kinetic.reshape(1, COEFS), wave_coef, projector, coupled)
    line = coupled.reshape(1, 2, PROJ)
    far_re = jnp.sum(becp * line, axis=(1, 2))
    far_im = jnp.sum(becp[:, 0] * line[:, 1] - becp[:, 1] * line[:, 0], axis=1)
    far = jnp.concatenate([far_re, far_im, jnp.zeros((120,), F32)]).reshape(1, 128)
    applied, total = collect(span, key, returned, stick, base.reshape(2, 128, 128), far)
    total = total[0, :16].reshape(2, 2, 1, 4)
    band = jnp.arange(4, dtype=jnp.int32)
    here = (band[:, None] ^ band[None, :]) == lax.axis_index("band")
    total = jnp.sum(jnp.where(here, total, 0.0), axis=3, keepdims=True)
    return applied.reshape(2, 1, COEFS), total[0], total[1]


def solution(mesh):
    in_specs = (
        P(None, "band", "pw"),
        P(None, None, "pw"),
        P("pw", None, None),
        P("pw"),
        P(),
        P(),
        P(),
    )
    out_specs = (P(None, "band", "pw"), P(None, None, "band"), P(None, None, "band"))
    return jax.shard_map(local, mesh=mesh, in_specs=in_specs, out_specs=out_specs, check_vma=False)
```

```python
import functools

import jax
import jax.numpy as jnp
import ml_dtypes
import numpy as np
from jax import lax
from jax.experimental import pallas as pl
from jax.experimental.pallas import tpu as pltpu
from jax.sharding import PartitionSpec as P

GX = 256
GY = 256
GZ = 256
KIN_MAX = 2.0
PRECISE = lax.Precision.HIGHEST

PW = 32
STICKS = 384
COEFS = 16384
PROJ = 64
PLANES = GZ // PW
ROWS = 2 * PLANES
KC = 4096
STEP_BLOCKS = KC // 1024
WINDOW = 256
SLOT_ROWS = 768
TILES = STICKS // 128
GROUPS = 24
CHUNKS = 16
NQ = 4
NCH = 3
PAIR = 4
PLACE_UNROLL = 4
PICK_UNROLL = 6
GRAM_STEPS = 2
FETCH_UNROLL = 4
F32 = jnp.float32
BF16 = jnp.bfloat16
NN = (((1,), (0,)), ((), ()))
NT = (((1,), (1,)), ((), ()))


def mm(left, right, dims=NN):
    return lax.dot_general(left, right, dims, preferred_element_type=F32)


def split(value):
    high = value.astype(BF16)
    low = (value - high.astype(F32)).astype(BF16)
    return high, low


def split_table(table):
    high = table.astype(np.float32).astype(ml_dtypes.bfloat16)
    low = (table - high.astype(np.float64)).astype(np.float32).astype(ml_dtypes.bfloat16)
    return high, low


def trig():
    n = np.arange(256)
    angle = 2.0 * np.pi * (np.outer(n, n) % 256) / 256.0
    return np.cos(angle), np.sin(angle)


def folded_table():
    c, s = trig()
    return np.concatenate([c[:128], c[128:129], s[1:128]], axis=0)


def plane_tables():
    table = folded_table()
    order = [128 * part + 8 * chunk + i for chunk in range(CHUNKS) for part in range(2) for i in range(8)]
    table_x = table[order]

    def left(values):
        high, low = split_table(values)
        return jnp.asarray(np.concatenate([high, low, high], axis=1))

    def right(values):
        high, low = split_table(values)
        return jnp.asarray(np.concatenate([high, low, high], axis=0))

    return right(table), right(table.T), left(table_x.T), left(table_x)


def spread_table():
    c, s = trig()
    rows = np.concatenate(
        [np.concatenate([np.concatenate([c[z], -s[z]])[None] if part == 0 else np.concatenate([s[z], c[z]])[None]
                         for z in range(d * PLANES, (d + 1) * PLANES)])
         for d in range(PW) for part in range(2)])
    high, low = split_table(rows)
    return np.concatenate([high, low, high], axis=1)


def collect_table():
    c, s = trig()
    full = np.zeros((512, 512))
    for d in range(PW):
        zs = np.arange(d * PLANES, (d + 1) * PLANES)
        at = d * ROWS
        full[:256, at:at + PLANES] = c[:, zs]
        full[:256, at + PLANES:at + ROWS] = s[:, zs]
        full[256:, at:at + PLANES] = -s[:, zs]
        full[256:, at + PLANES:at + ROWS] = c[:, zs]
    high, low = split_table(full)
    return np.concatenate([high, low, high], axis=1)


def iota(shape, dim):
    return lax.broadcasted_iota(jnp.int32, shape, dim).astype(F32)


def sort_rows(keys, values):
    keys = list(keys)
    values = [list(each) for each in values]
    sub = lax.broadcasted_iota(jnp.int32, (8, 128), 0)
    size = 2
    while size <= 128:
        dist = size // 2
        while dist >= 1:
            if dist < 16:
                for one in range(16):
                    if one & dist:
                        continue
                    two = one | dist
                    swap = keys[one] > keys[two]
                    if size < 16:
                        if one & size:
                            swap = keys[one] < keys[two]
                    elif size < 128:
                        swap = jnp.where((sub & (size // 16)) == 0, keys[one] - keys[two], keys[two] - keys[one]) > 0.0
                    for each in [keys] + values:
                        each[one], each[two] = (jnp.where(swap, each[two], each[one]),
                                                jnp.where(swap, each[one], each[two]))
            else:
                hop = dist // 16
                low = (sub & hop) == 0
                rising = (sub & (size // 16)) == 0 if size < 128 else jnp.full((8, 128), True)
                least = jnp.where(low == rising, 1.0, -1.0)

                def other(x):
                    return jnp.where(low, pltpu.roll(x, 8 - hop, 0), pltpu.roll(x, hop, 0))

                for one in range(16):
                    swap = (keys[one] - other(keys[one])) * least > 0.0
                    for each in [keys] + values:
                        each[one] = jnp.where(swap, other(each[one]), each[one])
            dist //= 2
        size *= 2
    return keys, values


def block_row(ref, block):
    at = pl.ds(block // 2, 1)
    half = 8 * (block % 2)
    return jnp.concatenate([ref[half + v, at, :] for v in range(8)], axis=1)


def key_parts(key):
    row = jnp.floor(key * (1.0 / 16384.0))
    rest = key - row * 16384.0
    return row, jnp.floor(rest * (1.0 / 128.0))


def fold(x):
    key = jnp.where(x == 128.0, 0.0, jnp.minimum(x, 256.0 - x))
    even = jnp.where(x == 128.0, -1.0, key)
    odd = jnp.where(x == 0.0, -1.0, key)
    return key, even, odd, jnp.where(x > 128.0, -1.0, 1.0)


def rank_of(owned):
    wide = jnp.broadcast_to(owned, (128, STICKS))
    down = jnp.transpose(wide)[:, :1]

    def sort_key(column):
        return fold(jnp.floor(column * (1.0 / GY)))[0] * 65536.0 + column

    key = sort_key(owned)
    key_down = sort_key(down)
    rank_row = jnp.sum(jnp.where(key_down < key, 1.0, 0.0), axis=0, keepdims=True)
    order = jnp.where(iota((STICKS, STICKS), 0) == rank_row, 1.0, 0.0)
    rank_col = jnp.sum(jnp.where(key < key_down, 1.0, 0.0), axis=1, keepdims=True)
    ordered = jnp.sum(jnp.where(iota((STICKS, STICKS), 1) == rank_col, down, 0.0), axis=0, keepdims=True)
    return order, ordered


def centred(values, length):
    return jnp.where(values < length // 2, values, values - length)


def owned_row(stick_ref):
    first = lax.axis_index("pw") * TILES
    return jnp.concatenate([stick_ref[pl.ds(first + t, 1), :] for t in range(TILES)], axis=1).astype(F32)


def kinetic_of(z, tile, lane, owned):
    x = jnp.floor(owned * (1.0 / GY))
    y = centred(owned - x * GY, GY)
    x = centred(x, GX)
    flat = x * x + y * y
    square = jnp.zeros((128, 128), F32)
    for t in range(TILES):
        line = jnp.broadcast_to(flat[:, t * 128:(t + 1) * 128], (128, 128))
        square = jnp.where(tile == t, jnp.take_along_axis(line, lane.astype(jnp.int32), axis=1), square)
    z = centred(z, GZ)
    return (square + z * z) * (KIN_MAX / 3.0 / 16384.0)


def spread_kernel(slot_ref, tile_ref, coef_ref, proj_ref, stick_ref, table_hbm, out_ref, key_ref, kinetic_ref,
                  span_ref, parts, acc, becp, table_ref, table_sem):
    step = pl.program_id(0)
    table_copy = pltpu.make_async_copy(table_hbm, table_ref, table_sem)

    @pl.when(step == 0)
    def _():
        table_copy.start()
        slot = slot_ref[...].astype(F32)
        z = jnp.floor((slot + 0.5) * (1.0 / STICKS))
        s = slot - z * STICKS
        tile = jnp.floor(s * (1.0 / 128.0))
        lane = s - tile * 128.0
        place = (tile * 256.0 + z) * 128.0 + lane
        kinetic = kinetic_of(z, tile, lane, owned_row(stick_ref))
        kinetic_ref[...] = kinetic
        for d in range(PW):
            here = slice(d * 4, d * 4 + 4)
            out_ref[d, 52:56, :] = kinetic[here]
            out_ref[d, 56:60, :] = tile_ref[0, here, :]
            out_ref[d, 60:64, :] = tile_ref[1, here, :]
        row = iota((128, 128), 0)
        array = jnp.floor(row * 0.125)
        key = place * 128.0 + (row - array * 8.0) * 16.0 + array

        def rows(x):
            return [x[v * 8:(v + 1) * 8] for v in range(16)]

        keys, (real, imag) = sort_rows(rows(key), [rows(tile_ref[0]), rows(tile_ref[1])])
        for v in range(16):
            key_ref[v] = keys[v]
            for at, part in enumerate(key_parts(keys[v]) + split(real[v]) + split(imag[v])):
                parts[at, v] = part.astype(F32)
        for block in range(16):
            half = 8 * (block % 2)
            at = block // 2
            first = jnp.min(key_parts(keys[half][at:at + 1])[0]).astype(jnp.int32)
            last = jnp.max(key_parts(keys[half + 7][at:at + 1])[0]).astype(jnp.int32)
            first = (first >> 4) << 4
            span_ref[0, block] = first
            span_ref[1, block] = ((last - first) >> 8) + 1
        acc[...] = jnp.zeros_like(acc)
        becp[...] = jnp.zeros_like(becp)

    none = jnp.zeros((), BF16)
    lane_of = (iota((128, 1024), 0)).astype(BF16)
    row_of = (iota((WINDOW, 1024), 0) - 128.0).astype(BF16)

    def product(block, first):
        row, lane, re_hi, re_lo, im_hi, im_lo = [block_row(parts.at[at], block) for at in range(6)]
        hit = lane_of == lane.astype(BF16)
        placed = jnp.concatenate(
            [jnp.where(hit, part.astype(BF16), none) for part in (re_hi, im_hi, re_lo, im_lo)], axis=0)
        want = row - (first + 128).astype(F32)
        hot = jnp.where(row_of == want.astype(BF16), jnp.ones((), BF16), none)
        return mm(hot, placed, NT)

    def window(first):
        return pl.ds(pl.multiple_of(first, 16), WINDOW)

    blocks = [step * STEP_BLOCKS + at for at in range(STEP_BLOCKS)]
    for block in blocks:
        first = span_ref[0, block]
        acc[window(first), :] += product(block, first)

    @pl.when(sum(span_ref[1, block] for block in blocks) > STEP_BLOCKS)
    def _():
        def rest(at, carry):
            block = step * STEP_BLOCKS + at

            def more(p, inner):
                first = span_ref[0, block] + p * WINDOW
                acc[window(first), :] += product(block, first)
                return inner

            return lax.fori_loop(1, span_ref[1, block], more, carry)

        lax.fori_loop(0, STEP_BLOCKS, rest, 0)

    c_re = coef_ref[0]
    c_im = coef_ref[1]
    p_re = proj_ref[0]
    p_im = proj_ref[1]
    real = p_re * c_re + p_im * c_im
    imag = p_re * c_im - p_im * c_re
    both = jnp.concatenate([real, imag], axis=0)
    total = both[:, :128]
    for at in range(128, KC, 128):
        total = total + both[:, at:at + 128]
    becp[...] += total

    @pl.when(step == pl.num_programs(0) - 1)
    def _():
        order, ordered = rank_of(owned_row(stick_ref))
        sticks = jnp.concatenate(
            [jnp.concatenate([acc[t * 256:(t + 1) * 256, part * 128:(part + 1) * 128] for t in range(TILES)], axis=1)
             for part in range(4)], axis=0).astype(BF16)
        sticks = mm(sticks, order.astype(BF16), NT).astype(BF16)
        high = sticks[:512]
        low = sticks[512:]
        table_copy.wait()
        spread = mm(table_ref[...], jnp.concatenate([high, high, low], axis=0))
        spread = spread.reshape(PW, ROWS, STICKS)
        for t in range(TILES):
            out_ref[:, t * ROWS:(t + 1) * ROWS, :] = spread[:, :, t * 128:(t + 1) * 128]
        line = jnp.sum(jnp.transpose(becp[...]), axis=0, keepdims=True)
        extra = jnp.concatenate(
            [line] + [ordered[:, t * 128:(t + 1) * 128] for t in range(TILES)], axis=0)
        out_ref[:, TILES * ROWS:TILES * ROWS + 4, :] = jnp.broadcast_to(extra[None], (PW, 4, 128))


def spread_sticks(slot, coef, proj, stick):
    table = jnp.asarray(spread_table())
    return pl.pallas_call(
        spread_kernel,
        grid=(COEFS // KC,),
        in_specs=[
            pl.BlockSpec((128, 128), lambda i: (0, 0)),
            pl.BlockSpec((2, 128, 128), lambda i: (0, 0, 0)),
            pl.BlockSpec((2, 1, KC), lambda i: (0, 0, i)),
            pl.BlockSpec((2, PROJ, KC), lambda i: (0, 0, i)),
            pl.BlockSpec((PW * TILES, 128), lambda i: (0, 0)),
            pl.BlockSpec(memory_space=pl.ANY),
        ],
        out_specs=[
            pl.BlockSpec((PW, 64, 128), lambda i: (0, 0, 0)),
            pl.BlockSpec((16, 8, 128), lambda i: (0, 0, 0)),
            pl.BlockSpec((128, 128), lambda i: (0, 0)),
            pl.BlockSpec(memory_space=pltpu.SMEM),
        ],
        out_shape=[
            jax.ShapeDtypeStruct((PW, 64, 128), F32),
            jax.ShapeDtypeStruct((16, 8, 128), F32),
            jax.ShapeDtypeStruct((128, 128), F32),
            jax.ShapeDtypeStruct((2, 16), jnp.int32),
        ],
        scratch_shapes=[
            pltpu.VMEM((6, 16, 8, 128), F32),
            pltpu.VMEM((SLOT_ROWS + WINDOW, 512), F32),
            pltpu.VMEM((128, 128), F32),
            pltpu.VMEM((512, 1536), BF16),
            pltpu.SemaphoreType.DMA,
        ],
        compiler_params=pltpu.CompilerParams(vmem_limit_bytes=60 << 20),
        cost_estimate=pl.CostEstimate(flops=6 * 10 ** 9, bytes_accessed=12 << 20, transcendentals=0),
        name="spread_sticks",
    )(slot, coef.reshape(2, 128, 128), coef, proj, stick, table)


def swap_chunks(parts):
    parts = list(parts)
    chunk = lax.broadcasted_iota(jnp.int32, parts[0].shape, 1) // 16
    for bit in (1, 2, 4):
        here = (chunk & bit) == 0
        for a in range(8):
            if a & bit:
                continue
            one, two = parts[a], parts[a | bit]
            parts[a] = jnp.where(here, one, pltpu.roll(two, 16 * bit, 1))
            parts[a | bit] = jnp.where(here, pltpu.roll(one, 128 - 16 * bit, 1), two)
    return parts


def write_bounds(columns, bounds):
    firsts, lasts = [], []
    for column in columns:
        chunk = jnp.floor(fold(jnp.floor(column * (1.0 / GY)))[0] * 0.125)
        firsts.append(jnp.min(chunk, axis=1, keepdims=True))
        lasts.append(jnp.max(chunk, axis=1, keepdims=True))
    first = jnp.broadcast_to(jnp.concatenate(firsts, axis=0), (GROUPS, 128))
    last = jnp.broadcast_to(jnp.concatenate(lasts, axis=0), (GROUPS, 128))
    lane = iota((GROUPS, 128), 1)
    start = jnp.sum(jnp.where(last < lane, 1.0, 0.0), axis=0, keepdims=True)
    end = jnp.sum(jnp.where(first <= lane, 1.0, 0.0), axis=0, keepdims=True)
    more = jnp.zeros((128 - GROUPS, 128), F32)
    first = jnp.transpose(jnp.concatenate([first, more], axis=0))[:1]
    last = jnp.transpose(jnp.concatenate([last, more], axis=0))[:1]
    count = jnp.where(lane[:1] < CHUNKS, end - start, 0.0)
    lines = [jnp.minimum(start, GROUPS - 1.0), end - start, first, last - first + 1.0,
             jnp.broadcast_to(jnp.max(count, axis=1, keepdims=True), (1, 128)),
             jnp.broadcast_to(jnp.max(last - first + 1.0, axis=1, keepdims=True), (1, 128)), jnp.zeros((2, 128), F32)]
    bounds[...] = jnp.concatenate(lines, axis=0).astype(jnp.int32)


def field_kernel(recv_ref, field_hbm, y_in_ref, y_out_ref, x_in_ref, x_out_ref, out_ref,
                 wide, hot, keys, signs, grid, done, sticks, field_ref, bounds, range_ref, field_sem, range_sem):
    field_copy = pltpu.make_async_copy(field_hbm, field_ref, field_sem)
    field_copy.start()
    cells = []
    for g in range(4):
        mixed = swap_chunks([recv_ref[g * 8 + i, TILES * ROWS:TILES * ROWS + 8, :] for i in range(8)])
        cells.append(mixed)
    columns = [jnp.concatenate([cells[g][q % 8][1 + q // 8:2 + q // 8] for g in range(4)], axis=1)
               for q in range(GROUPS)]
    write_bounds(columns, bounds)
    range_copy = pltpu.make_async_copy(bounds, range_ref, range_sem)
    range_copy.start()
    one_hot = iota((128, 512), 0).astype(BF16)
    zero = jnp.zeros((), BF16)
    for t in range(TILES):
        mixed = [swap_chunks([recv_ref[g * 8 + i, t * ROWS:(t + 1) * ROWS, :] for i in range(8)]) for g in range(4)]
        for c in range(8):
            q = t * 8 + c
            values = jnp.concatenate([mixed[g][c] for g in range(4)], axis=1)
            high, low = split(values)
            both = jnp.concatenate([high.astype(F32), low.astype(F32)], axis=0)
            wide[q] = jnp.broadcast_to(both[:, None, :], (2 * ROWS, 16, 512)).astype(BF16)
            column = columns[q]
            x = jnp.floor(column * (1.0 / GY))
            y = column - x * GY
            _, even, odd, sign = fold(x)
            upper = iota((16, 512), 0) < 8.0
            keys[q] = jnp.where(upper, even, odd).astype(BF16)
            signs[q] = jnp.where(upper, 1.0, sign).astype(BF16)
            _, even, odd, sign = fold(y)
            hot[q, :128, :] = jnp.where(one_hot == even.astype(BF16), jnp.ones((), BF16), zero)
            hot[q, 128:, :] = jnp.where(one_hot == odd.astype(BF16), sign.astype(BF16), zero)
    for q in range(GROUPS, GROUPS + NQ):
        wide[q] = jnp.zeros((2 * ROWS, 16, 512), BF16)
        hot[q] = jnp.zeros((256, 512), BF16)
        keys[q] = jnp.full((16, 512), -1.0, BF16)
        signs[q] = jnp.zeros((16, 512), BF16)
    done[:, GX:, :] = jnp.zeros((ROWS, 16 * (NCH - 1), 512), BF16)

    step_of = iota((16, 512), 0)
    step_of = jnp.where(step_of < 8.0, step_of, step_of - 8.0)

    def place(chunk, first, groups):
        want = (step_of + (chunk * 8).astype(F32)).astype(BF16)
        masked = []
        for j in range(groups):
            mine = jnp.where(keys[first + j] == want, signs[first + j], zero)
            masked.append((wide[first + j] * mine[None]).reshape(2 * ROWS * 16, 512))
        got = mm(jnp.concatenate(masked, axis=1),
                 jnp.concatenate([hot[first + j] for j in range(groups)], axis=1), NT)
        got = got.reshape(2, ROWS, 16, 256)
        return got[0] + got[1]

    def rows_of(chunk):
        return pl.ds(pl.multiple_of(chunk * 16, 16), 16)

    def place_first(step, carry):
        chunks = [step * PLACE_UNROLL + at for at in range(PLACE_UNROLL)]
        most = functools.reduce(jnp.maximum, [range_ref[1, chunk] for chunk in chunks])

        def run(groups):
            for chunk in chunks:
                grid[:, rows_of(chunk), :] = place(chunk, range_ref[0, chunk], groups)

        pl.when(most <= NQ)(lambda: run(NQ))
        pl.when(most > NQ)(lambda: run(NQ + 1))
        return carry

    def place_rest(chunk, carry):
        def more(p, inner):
            grid[:, rows_of(chunk), :] += place(chunk, range_ref[0, chunk] + p, 1)
            return inner

        return lax.fori_loop(NQ + 1, range_ref[1, chunk], more, carry)

    range_copy.wait()
    lax.fori_loop(0, CHUNKS // PLACE_UNROLL, place_first, 0)

    @pl.when(range_ref[4, 0] > NQ + 1)
    def _():
        lax.fori_loop(0, CHUNKS, place_rest, 0)

    row = lax.broadcasted_iota(jnp.int32, (256, 256), 0)
    lane = lax.broadcasted_iota(jnp.int32, (256, 256), 1)
    even_x = ((row & 8) == 0) | (row == 8)
    even_y = lane <= 128

    def along_y(re, im, table):
        high, low = split(jnp.concatenate([re, im], axis=0))
        got = mm(jnp.concatenate([high, high, low], axis=1), table[...])
        return got[:256], got[256:]

    def along_x(re, im, table):
        high, low = split(jnp.concatenate([re, im], axis=1))
        got = mm(table[...], jnp.concatenate([high, high, low], axis=0))
        return got[:, :256], got[:, 256:]

    def plane(zz):
        re = grid[zz]
        im = grid[PLANES + zz]
        re, im = along_y(jnp.where(even_y, re, -im), jnp.where(even_y, im, re), y_in_ref)
        re, im = along_x(jnp.where(even_x, re, -im), jnp.where(even_x, im, re), x_in_ref)
        field = field_ref[zz]
        re, im = along_x(re * field, im * field, x_out_ref)
        re, im = along_y(jnp.where(even_x, re, im), jnp.where(even_x, im, -re), y_out_ref)
        high, low = split(jnp.where(even_y, re, im))
        done[zz, :GX, :256] = high
        done[zz, :GX, 256:] = low
        high, low = split(jnp.where(even_y, im, -re))
        done[PLANES + zz, :GX, :256] = high
        done[PLANES + zz, :GX, 256:] = low

    def planes(pair, carry):
        for at in range(PAIR):
            plane(pair * PAIR + at)
        return carry

    field_copy.wait()
    lax.fori_loop(0, PLANES // PAIR, planes, 0)

    def pick(q, first, chunks):
        both = jnp.concatenate([hot[q], hot[q]], axis=0)
        key = keys[q].astype(F32)
        sign = signs[q].astype(F32)
        here = pl.ds(pl.multiple_of(first * 16, 16), 16 * chunks)
        lines = done[:, here, :].reshape(ROWS * 16 * chunks, 512)
        got = mm(lines, both).reshape(ROWS, 2 * chunks, 8, 512)
        total = None
        for j in range(chunks):
            want = step_of + ((first + j) * 8).astype(F32)
            mine = jnp.where(key == want, sign, 0.0)
            part = got[:, 2 * j] * mine[None, :8] + got[:, 2 * j + 1] * mine[None, 8:]
            total = part if total is None else total + part
        return jnp.sum(total, axis=1)

    def pick_first(step, carry):
        for at in range(PICK_UNROLL):
            q = step * PICK_UNROLL + at
            sticks[q] = pick(q, range_ref[2, q], NCH)
        return carry

    def pick_rest(q, carry):
        def more(p, inner):
            sticks[q] += pick(q, range_ref[2, q] + p, 1)
            return inner

        return lax.fori_loop(NCH, range_ref[3, q], more, carry)

    lax.fori_loop(0, GROUPS // PICK_UNROLL, pick_first, 0)

    @pl.when(range_ref[5, 0] > NCH)
    def _():
        lax.fori_loop(0, GROUPS, pick_rest, 0)

    for t in range(TILES):
        for g in range(4):
            mixed = swap_chunks([sticks[t * 8 + c, :, g * 128:(g + 1) * 128] for c in range(8)])
            for i in range(8):
                out_ref[g * 8 + i, t * ROWS:(t + 1) * ROWS, :] = mixed[i]


def apply_field(recv, field):
    vmem = pl.BlockSpec(memory_space=pltpu.VMEM)
    return pl.pallas_call(
        field_kernel,
        in_specs=[vmem, pl.BlockSpec(memory_space=pl.ANY)] + [vmem] * 4,
        out_specs=vmem,
        out_shape=jax.ShapeDtypeStruct((PW, 48, 128), F32),
        scratch_shapes=[
            pltpu.VMEM((GROUPS + NQ, 2 * ROWS, 16, 512), BF16),
            pltpu.VMEM((GROUPS + NQ, 256, 512), BF16),
            pltpu.VMEM((GROUPS + NQ, 16, 512), BF16),
            pltpu.VMEM((GROUPS + NQ, 16, 512), BF16),
            pltpu.VMEM((ROWS, GX, GY), F32),
            pltpu.VMEM((ROWS, GX + 16 * (NCH - 1), 512), BF16),
            pltpu.VMEM((GROUPS, ROWS, 512), F32),
            pltpu.VMEM((PLANES, GX, GY), F32),
            pltpu.VMEM((8, 128), jnp.int32),
            pltpu.SMEM((8, 128), jnp.int32),
            pltpu.SemaphoreType.DMA,
            pltpu.SemaphoreType.DMA,
        ],
        compiler_params=pltpu.CompilerParams(vmem_limit_bytes=60 << 20),
        cost_estimate=pl.CostEstimate(flops=35 * 10 ** 9, bytes_accessed=8 << 20, transcendentals=0),
        name="apply_field",
    )(recv, field, *plane_tables())


def gram_kernel(own_ref, one_ref, two_ref, three_ref, worked_ref, out_ref, becp_ref, total, small):
    step = pl.program_id(0)

    @pl.when(step == 0)
    def _():
        total[...] = jnp.zeros_like(total)
        small[...] = jnp.zeros_like(small)
        becp_ref[...] = jnp.zeros_like(becp_ref)

    span = PW // GRAM_STEPS
    here = pl.ds(pl.multiple_of(step * span, span), span)
    worked = worked_ref[...].reshape(span * TILES, 2, PLANES, 128)
    out_ref[here, :TILES * ROWS, :] = worked_ref[...]
    w_re = worked[:, 0]
    w_im = worked[:, 1]
    upper = lax.broadcasted_iota(jnp.int32, (span * 8, 128), 0) % 8 < 4
    mine = own_ref[:, 56:, :].reshape(span * 8, 128)
    weight = own_ref[:, 48:56, :].reshape(span * 8, 128)

    def halves(x):
        return pltpu.roll(x.reshape(span, 8, 128), 4, 1).reshape(span * 8, 128)

    turned = jnp.where(upper, halves(mine), -halves(mine))
    weight = jnp.where(upper, halves(weight), weight)
    for a, ref in enumerate((own_ref, one_ref, two_ref, three_ref)):
        lines = ref[:, :TILES * ROWS, :].reshape(span * TILES, 2, PLANES, 128)
        a_re = lines[:, 0]
        a_im = lines[:, 1]
        total[a] += jnp.sum(a_re * w_re + a_im * w_im, axis=0)
        total[4 + a] += jnp.sum(a_re * w_im - a_im * w_re, axis=0)
        becp_ref[a] += jnp.sum(ref[:, 48:56, :], axis=0)
        coef = ref[:, 56:, :].reshape(span * 8, 128)
        real = coef * mine
        imag = coef * turned
        for at, value in ((a, real * weight), (4 + a, imag * weight), (8 + a, real), (12 + a, imag)):
            small[at] += jnp.sum(value.reshape(span, 8, 128), axis=0)

    @pl.when(step == pl.num_programs(0) - 1)
    def _():
        scale = 1.0 / (GX * GY * GZ)
        lines = [jnp.sum(small[at] + total[at] * scale, axis=0, keepdims=True) for at in range(8)]
        lines += [jnp.sum(small[at], axis=0, keepdims=True) for at in range(8, 16)]
        lines = jnp.concatenate(lines + [jnp.zeros((112, 128), F32)], axis=0)
        line = jnp.sum(jnp.transpose(lines), axis=0, keepdims=True)
        out_ref[:, TILES * ROWS:, :] = jnp.broadcast_to(line[None], (PW, 8, 128))


def gram_part(recv, others, worked):
    span = PW // GRAM_STEPS
    return pl.pallas_call(
        gram_kernel,
        grid=(GRAM_STEPS,),
        in_specs=[pl.BlockSpec((span, 64, 128), lambda i: (i, 0, 0))] * 4 + [
            pl.BlockSpec((span, 48, 128), lambda i: (i, 0, 0)),
        ],
        out_specs=[pl.BlockSpec((PW, 56, 128), lambda i: (0, 0, 0)), pl.BlockSpec((4, 8, 128), lambda i: (0, 0, 0))],
        out_shape=[jax.ShapeDtypeStruct((PW, 56, 128), F32), jax.ShapeDtypeStruct((4, 8, 128), F32)],
        scratch_shapes=[pltpu.VMEM((8, PLANES, 128), F32), pltpu.VMEM((16, 8, 128), F32)],
        compiler_params=pltpu.CompilerParams(vmem_limit_bytes=60 << 20),
        cost_estimate=pl.CostEstimate(flops=10 ** 7, bytes_accessed=6 << 20, transcendentals=0),
        name="gram_part",
    )(recv, *others, worked)


def base_kernel(kinetic_ref, coef_ref, proj_ref, matrix_ref, becp_ref, out_ref, far_ref, weight):
    @pl.when(pl.program_id(0) == 0)
    def _():
        matrix = matrix_ref[...]
        lines = jnp.concatenate([becp_ref[a, :1, :] for a in range(4)], axis=0)
        w_re = jnp.sum(matrix * lines[:1, :PROJ], axis=1, keepdims=True)
        w_im = jnp.sum(matrix * lines[:1, PROJ:], axis=1, keepdims=True)
        weight[0] = jnp.broadcast_to(w_re, (PROJ, 128))
        weight[1] = jnp.broadcast_to(w_im, (PROJ, 128))
        down = jnp.transpose(jnp.concatenate([lines, jnp.zeros((124, 128), F32)], axis=0))
        far_re = jnp.sum(down[:PROJ] * w_re + down[PROJ:] * w_im, axis=0, keepdims=True)
        far_im = jnp.sum(down[:PROJ] * w_im - down[PROJ:] * w_re, axis=0, keepdims=True)
        far = jnp.broadcast_to(far_re, (8, 128)) + pltpu.roll(jnp.broadcast_to(far_im, (8, 128)), 4, 1)
        far_ref[...] = far

    kinetic = kinetic_ref[...]
    p_re = proj_ref[0]
    p_im = proj_ref[1]
    w_re = weight[0][:, :1]
    w_im = weight[1][:, :1]
    far_re = jnp.sum(p_re * w_re - p_im * w_im, axis=0, keepdims=True)
    far_im = jnp.sum(p_re * w_im + p_im * w_re, axis=0, keepdims=True)
    out_ref[0] = kinetic * coef_ref[0] + far_re
    out_ref[1] = kinetic * coef_ref[1] + far_im


def base_part(kinetic, coef, proj, matrix, becp):
    return pl.pallas_call(
        base_kernel,
        grid=(COEFS // KC,),
        in_specs=[
            pl.BlockSpec((1, KC), lambda i: (0, i)),
            pl.BlockSpec((2, 1, KC), lambda i: (0, 0, i)),
            pl.BlockSpec((2, PROJ, KC), lambda i: (0, 0, i)),
            pl.BlockSpec((PROJ, PROJ), lambda i: (0, 0)),
            pl.BlockSpec((4, 8, 128), lambda i: (0, 0, 0)),
        ],
        out_specs=[pl.BlockSpec((2, 1, KC), lambda i: (0, 0, i)), pl.BlockSpec((8, 128), lambda i: (0, 0))],
        out_shape=[jax.ShapeDtypeStruct((2, 1, COEFS), F32), jax.ShapeDtypeStruct((8, 128), F32)],
        scratch_shapes=[pltpu.VMEM((2, PROJ, 128), F32)],
        compiler_params=pltpu.CompilerParams(vmem_limit_bytes=60 << 20),
        cost_estimate=pl.CostEstimate(flops=10 ** 7, bytes_accessed=10 << 20, transcendentals=0),
        name="base_part",
    )(kinetic, coef, proj, matrix, becp)


def collect_kernel(span_ref, key_ref, recv_ref, stick_ref, table_ref, base_ref, far_ref, out_ref,
                   energy_ref, overlap_ref, values, found_re, found_im):
    total = jnp.sum(recv_ref[:, TILES * ROWS:, :], axis=0) + far_ref[...]
    band = lax.axis_index("band")
    lane = lax.broadcasted_iota(jnp.int32, (8, 128), 1)
    for bit in (1, 2):
        swapped = jnp.where((lane & bit) == 0, pltpu.roll(total, 128 - bit, 1), pltpu.roll(total, bit, 1))
        total = jnp.where((band & bit) != 0, swapped, total)
    for ri in range(2):
        energy_ref[ri] = total[:1, ri * 4:ri * 4 + 4]
        overlap_ref[ri] = total[:1, 8 + ri * 4:12 + ri * 4]

    order, _ = rank_of(owned_row(stick_ref))
    order = order.astype(BF16)
    lines = jnp.concatenate(
        [recv_ref[:, t * ROWS:(t + 1) * ROWS, :].reshape(512, 128) for t in range(TILES)], axis=1)
    high, low = split(lines)
    back = mm(table_ref[...], jnp.concatenate([high, high, low], axis=0))
    for at, part in enumerate(split(back)):
        part = mm(part, order).astype(BF16)
        for ri in range(2):
            for t in range(TILES):
                values[ri, t * 256:(t + 1) * 256, at * 128:(at + 1) * 128] = part[
                    ri * 256:(ri + 1) * 256, t * 128:(t + 1) * 128]
    values[:, SLOT_ROWS:, :] = jnp.zeros((2, WINDOW, 256), BF16)

    lane_of = iota((128, 1024), 0).astype(BF16)
    row_of = iota((WINDOW, 1024), 0)

    def fetch(block, first):
        row, lane = key_parts(block_row(key_ref, block))
        hit = jnp.where(lane_of == lane.astype(BF16), jnp.ones((), BF16), jnp.zeros((), BF16))
        here = pl.ds(pl.multiple_of(first, 16), WINDOW)
        got = mm(jnp.concatenate([values[0, here, :], values[1, here, :]], axis=0), jnp.concatenate([hit, hit], axis=0))
        mine = row_of == row - first.astype(F32)
        return (jnp.sum(jnp.where(mine, got[:WINDOW], 0.0), axis=0, keepdims=True),
                jnp.sum(jnp.where(mine, got[WINDOW:], 0.0), axis=0, keepdims=True))

    def put(block, pair, old):
        at = pl.ds(block // 2, 1)
        half = 8 * (block % 2)
        for ref, line in zip((found_re, found_im), pair):
            for v in range(8):
                piece = line[:, v * 128:(v + 1) * 128]
                ref[half + v, at, :] = ref[half + v, at, :] + piece if old else piece

    def one(step, carry):
        for at in range(FETCH_UNROLL):
            block = step * FETCH_UNROLL + at
            put(block, fetch(block, span_ref[0, block]), False)
        return carry

    lax.fori_loop(0, 16 // FETCH_UNROLL, one, 0)

    @pl.when(sum(span_ref[1, block] for block in range(16)) > 16)
    def _():
        def rest(block, carry):
            def more(p, inner):
                put(block, fetch(block, span_ref[0, block] + p * WINDOW), True)
                return inner

            return lax.fori_loop(1, span_ref[1, block], more, carry)

        lax.fori_loop(0, 16, rest, 0)

    scale = 1.0 / (GX * GY * GZ)
    home = []
    for v in range(16):
        key = key_ref[v]
        home.append(key - jnp.floor(key * (1.0 / 128.0)) * 128.0)
    _, (real, imag) = sort_rows(home, [[found_re[v] for v in range(16)], [found_im[v] for v in range(16)]])
    for v in range(16):
        here = slice(v * 8, (v + 1) * 8)
        out_ref[0, here, :] = base_ref[0, here, :] + real[v] * scale
        out_ref[1, here, :] = base_ref[1, here, :] + imag[v] * scale


def collect(span, key, recv, stick, base, far):
    vmem = pl.BlockSpec(memory_space=pltpu.VMEM)
    return pl.pallas_call(
        collect_kernel,
        in_specs=[pl.BlockSpec(memory_space=pltpu.SMEM)] + [vmem] * 6,
        out_specs=[vmem, vmem, vmem],
        out_shape=[
            jax.ShapeDtypeStruct((2, 128, 128), F32),
            jax.ShapeDtypeStruct((2, 1, 4), F32),
            jax.ShapeDtypeStruct((2, 1, 4), F32),
        ],
        scratch_shapes=[
            pltpu.VMEM((2, SLOT_ROWS + WINDOW, 256), BF16),
            pltpu.VMEM((16, 8, 128), F32),
            pltpu.VMEM((16, 8, 128), F32),
        ],
        compiler_params=pltpu.CompilerParams(vmem_limit_bytes=32 << 20),
        cost_estimate=pl.CostEstimate(flops=6 * 10 ** 9, bytes_accessed=4 << 20, transcendentals=0),
        name="collect",
    )(span, key, recv, stick, jnp.asarray(collect_table()), base, far)


def local(wave_coef, projector, potential, grid_slot, stick_column, proj_atom, coupling):
    stick = stick_column.reshape(PW * TILES, 128)
    sent, key, kinetic, span = spread_sticks(grid_slot.reshape(128, 128), wave_coef, projector, stick)
    recv = lax.all_to_all(sent, "pw", split_axis=0, concat_axis=0, tiled=True)
    others = [lax.ppermute(recv, "band", [(b, b ^ m) for b in range(4)]) for m in (1, 2, 3)]
    worked = apply_field(recv, potential)
    payload, becp = gram_part(recv, others, worked)
    returned = lax.all_to_all(payload, "pw", split_axis=0, concat_axis=0, tiled=True)

    same_atom = proj_atom[:, None] == proj_atom[None, :]
    matrix = jnp.where(same_atom, 0.5 * (coupling + coupling.T), 0.0)
    base, far = base_part(kinetic.reshape(1, COEFS), wave_coef, projector, matrix, becp)
    applied, energy, overlap = collect(span, key, returned, stick, base.reshape(2, 128, 128), far)
    return applied.reshape(2, 1, COEFS), energy.transpose(0, 2, 1), overlap.transpose(0, 2, 1)


def solution(mesh):
    in_specs = (
        P(None, "band", "pw"),
        P(None, None, "pw"),
        P("pw", None, None),
        P("pw"),
        P(),
        P(),
        P(),
    )
    out_specs = (P(None, "band", "pw"), P(None, None, "band"), P(None, None, "band"))
    return jax.shard_map(local, mesh=mesh, in_specs=in_specs, out_specs=out_specs, check_vma=False)
```

```python
import functools

import jax
import jax.numpy as jnp
import ml_dtypes
import numpy as np
from jax import lax
from jax.experimental import pallas as pl
from jax.experimental.pallas import tpu as pltpu
from jax.sharding import PartitionSpec as P

GX = 256
GY = 256
GZ = 256
KIN_MAX = 2.0
PRECISE = lax.Precision.HIGHEST

PW = 32
STICKS = 384
COEFS = 16384
PROJ = 64
PLANES = GZ // PW
ROWS = 2 * PLANES
KC = 4096
STEP_BLOCKS = KC // 1024
WINDOW = 256
SLOT_ROWS = 768
TILES = STICKS // 128
GROUPS = 24
CHUNKS = 16
NQ = 4
NCH = 3
PAIR = 8
PLACE_UNROLL = 4
PICK_UNROLL = 6
GRAM_STEPS = 2
FETCH_UNROLL = 16
F32 = jnp.float32
BF16 = jnp.bfloat16
NN = (((1,), (0,)), ((), ()))
NT = (((1,), (1,)), ((), ()))


def mm(left, right, dims=NN):
    return lax.dot_general(left, right, dims, preferred_element_type=F32)


def split(value):
    high = value.astype(BF16)
    low = (value - high.astype(F32)).astype(BF16)
    return high, low


def split_table(table):
    high = table.astype(np.float32).astype(ml_dtypes.bfloat16)
    low = (table - high.astype(np.float64)).astype(np.float32).astype(ml_dtypes.bfloat16)
    return high, low


def trig():
    n = np.arange(256)
    angle = 2.0 * np.pi * (np.outer(n, n) % 256) / 256.0
    return np.cos(angle), np.sin(angle)


def folded_table():
    c, s = trig()
    return np.concatenate([c[:128], c[128:129], s[1:128]], axis=0)


def plane_tables():
    table = folded_table()
    order = [128 * part + 8 * chunk + i for chunk in range(CHUNKS) for part in range(2) for i in range(8)]
    table_x = table[order]

    def left(values):
        high, low = split_table(values)
        return jnp.asarray(np.concatenate([high, low, high], axis=1))

    def right(values):
        high, low = split_table(values)
        return jnp.asarray(np.concatenate([high, low, high], axis=0))

    return right(table), right(table.T), left(table_x.T), left(table_x)


def spread_table():
    c, s = trig()
    rows = np.concatenate(
        [np.concatenate([np.concatenate([c[z], -s[z]])[None] if part == 0 else np.concatenate([s[z], c[z]])[None]
                         for z in range(d * PLANES, (d + 1) * PLANES)])
         for d in range(PW) for part in range(2)])
    high, low = split_table(rows)
    return np.concatenate([high, low, high], axis=1)


def collect_table():
    c, s = trig()
    full = np.zeros((512, 512))
    for d in range(PW):
        zs = np.arange(d * PLANES, (d + 1) * PLANES)
        at = d * ROWS
        full[:256, at:at + PLANES] = c[:, zs]
        full[:256, at + PLANES:at + ROWS] = s[:, zs]
        full[256:, at:at + PLANES] = -s[:, zs]
        full[256:, at + PLANES:at + ROWS] = c[:, zs]
    high, low = split_table(full)
    return np.concatenate([high, low, high], axis=1)


def iota(shape, dim):
    return lax.broadcasted_iota(jnp.int32, shape, dim).astype(F32)


def sort_rows(keys, values):
    keys = list(keys)
    values = [list(each) for each in values]
    sub = lax.broadcasted_iota(jnp.int32, (8, 128), 0)
    size = 2
    while size <= 128:
        dist = size // 2
        while dist >= 1:
            if dist < 16:
                for one in range(16):
                    if one & dist:
                        continue
                    two = one | dist
                    swap = keys[one] > keys[two]
                    if size < 16:
                        if one & size:
                            swap = keys[one] < keys[two]
                    elif size < 128:
                        swap = jnp.where((sub & (size // 16)) == 0, keys[one] - keys[two], keys[two] - keys[one]) > 0.0
                    for each in [keys] + values:
                        each[one], each[two] = (jnp.where(swap, each[two], each[one]),
                                                jnp.where(swap, each[one], each[two]))
            else:
                hop = dist // 16
                low = (sub & hop) == 0
                rising = (sub & (size // 16)) == 0 if size < 128 else jnp.full((8, 128), True)
                least = jnp.where(low == rising, 1.0, -1.0)

                def other(x):
                    return jnp.where(low, pltpu.roll(x, 8 - hop, 0), pltpu.roll(x, hop, 0))

                for one in range(16):
                    swap = (keys[one] - other(keys[one])) * least > 0.0
                    for each in [keys] + values:
                        each[one] = jnp.where(swap, other(each[one]), each[one])
            dist //= 2
        size *= 2
    return keys, values


def block_row(ref, block):
    at = pl.ds(block // 2, 1)
    half = 8 * (block % 2)
    return jnp.concatenate([ref[half + v, at, :] for v in range(8)], axis=1)


def key_parts(key):
    row = jnp.floor(key * (1.0 / 16384.0))
    rest = key - row * 16384.0
    return row, jnp.floor(rest * (1.0 / 128.0))


def fold(x):
    key = jnp.where(x == 128.0, 0.0, jnp.minimum(x, 256.0 - x))
    even = jnp.where(x == 128.0, -1.0, key)
    odd = jnp.where(x == 0.0, -1.0, key)
    return key, even, odd, jnp.where(x > 128.0, -1.0, 1.0)


def rank_of(owned):
    wide = jnp.broadcast_to(owned, (128, STICKS))
    down = jnp.transpose(wide)[:, :1]

    def sort_key(column):
        return fold(jnp.floor(column * (1.0 / GY)))[0] * 65536.0 + column

    key = sort_key(owned)
    key_down = sort_key(down)
    rank_row = jnp.sum(jnp.where(key_down < key, 1.0, 0.0), axis=0, keepdims=True)
    order = jnp.where(iota((STICKS, STICKS), 0) == rank_row, 1.0, 0.0)
    rank_col = jnp.sum(jnp.where(key < key_down, 1.0, 0.0), axis=1, keepdims=True)
    ordered = jnp.sum(jnp.where(iota((STICKS, STICKS), 1) == rank_col, down, 0.0), axis=0, keepdims=True)
    return order, ordered


def centred(values, length):
    return jnp.where(values < length // 2, values, values - length)


def owned_row(stick_ref):
    first = lax.axis_index("pw") * TILES
    return jnp.concatenate([stick_ref[pl.ds(first + t, 1), :] for t in range(TILES)], axis=1).astype(F32)


def kinetic_of(z, tile, lane, owned):
    x = jnp.floor(owned * (1.0 / GY))
    y = centred(owned - x * GY, GY)
    x = centred(x, GX)
    flat = x * x + y * y
    square = jnp.zeros((128, 128), F32)
    for t in range(TILES):
        line = jnp.broadcast_to(flat[:, t * 128:(t + 1) * 128], (128, 128))
        square = jnp.where(tile == t, jnp.take_along_axis(line, lane.astype(jnp.int32), axis=1), square)
    z = centred(z, GZ)
    return (square + z * z) * (KIN_MAX / 3.0 / 16384.0)


def spread_kernel(slot_ref, tile_ref, coef_ref, proj_hbm, stick_ref, table_hbm, out_ref, key_ref, kinetic_ref,
                  span_ref, parts, acc, becp, table_ref, proj_buf, table_sem, proj_sems):
    step = pl.program_id(0)
    table_copy = pltpu.make_async_copy(table_hbm, table_ref, table_sem)

    def proj_copy(at):
        here = pl.ds(pl.multiple_of(at * KC, KC), KC)
        return pltpu.make_async_copy(proj_hbm.at[:, :, here], proj_buf.at[at], proj_sems.at[at])

    @pl.when(step == 0)
    def _():
        for at in range(COEFS // KC):
            proj_copy(at).start()
        table_copy.start()
        slot = slot_ref[...].astype(F32)
        z = jnp.floor((slot + 0.5) * (1.0 / STICKS))
        s = slot - z * STICKS
        tile = jnp.floor(s * (1.0 / 128.0))
        lane = s - tile * 128.0
        place = (tile * 256.0 + z) * 128.0 + lane
        kinetic = kinetic_of(z, tile, lane, owned_row(stick_ref))
        kinetic_ref[...] = kinetic
        for d in range(PW):
            here = slice(d * 4, d * 4 + 4)
            out_ref[d, 52:56, :] = kinetic[here]
            out_ref[d, 56:60, :] = tile_ref[0, here, :]
            out_ref[d, 60:64, :] = tile_ref[1, here, :]
        row = iota((128, 128), 0)
        array = jnp.floor(row * 0.125)
        key = place * 128.0 + (row - array * 8.0) * 16.0 + array

        def rows(x):
            return [x[v * 8:(v + 1) * 8] for v in range(16)]

        keys, (real, imag) = sort_rows(rows(key), [rows(tile_ref[0]), rows(tile_ref[1])])
        for v in range(16):
            key_ref[v] = keys[v]
            for at, part in enumerate(key_parts(keys[v]) + split(real[v]) + split(imag[v])):
                parts[at, v] = part.astype(F32)
        for block in range(16):
            half = 8 * (block % 2)
            at = block // 2
            first = jnp.min(key_parts(keys[half][at:at + 1])[0]).astype(jnp.int32)
            last = jnp.max(key_parts(keys[half + 7][at:at + 1])[0]).astype(jnp.int32)
            first = (first >> 4) << 4
            span_ref[0, block] = first
            span_ref[1, block] = ((last - first) >> 8) + 1
        acc[...] = jnp.zeros_like(acc)
        becp[...] = jnp.zeros_like(becp)

    none = jnp.zeros((), BF16)
    lane_of = (iota((128, 1024), 0)).astype(BF16)
    row_of = (iota((WINDOW, 1024), 0) - 128.0).astype(BF16)

    def product(block, first):
        row, lane, re_hi, re_lo, im_hi, im_lo = [block_row(parts.at[at], block) for at in range(6)]
        hit = lane_of == lane.astype(BF16)
        placed = jnp.concatenate(
            [jnp.where(hit, part.astype(BF16), none) for part in (re_hi, im_hi, re_lo, im_lo)], axis=0)
        want = row - (first + 128).astype(F32)
        hot = jnp.where(row_of == want.astype(BF16), jnp.ones((), BF16), none)
        return mm(hot, placed, NT)

    def window(first):
        return pl.ds(pl.multiple_of(first, 16), WINDOW)

    blocks = [step * STEP_BLOCKS + at for at in range(STEP_BLOCKS)]
    for block in blocks:
        first = span_ref[0, block]
        acc[window(first), :] += product(block, first)

    @pl.when(sum(span_ref[1, block] for block in blocks) > STEP_BLOCKS)
    def _():
        def rest(at, carry):
            block = step * STEP_BLOCKS + at

            def more(p, inner):
                first = span_ref[0, block] + p * WINDOW
                acc[window(first), :] += product(block, first)
                return inner

            return lax.fori_loop(1, span_ref[1, block], more, carry)

        lax.fori_loop(0, STEP_BLOCKS, rest, 0)

    c_re = coef_ref[0]
    c_im = coef_ref[1]
    proj_copy(step).wait()
    p_re = proj_buf[step, 0]
    p_im = proj_buf[step, 1]
    real = p_re * c_re + p_im * c_im
    imag = p_re * c_im - p_im * c_re
    both = jnp.concatenate([real, imag], axis=0)
    total = both[:, :128]
    for at in range(128, KC, 128):
        total = total + both[:, at:at + 128]
    becp[...] += total

    @pl.when(step == pl.num_programs(0) - 1)
    def _():
        order, ordered = rank_of(owned_row(stick_ref))
        sticks = jnp.concatenate(
            [jnp.concatenate([acc[t * 256:(t + 1) * 256, part * 128:(part + 1) * 128] for t in range(TILES)], axis=1)
             for part in range(4)], axis=0).astype(BF16)
        sticks = mm(sticks, order.astype(BF16), NT).astype(BF16)
        high = sticks[:512]
        low = sticks[512:]
        table_copy.wait()
        spread = mm(table_ref[...], jnp.concatenate([high, high, low], axis=0))
        spread = spread.reshape(PW, ROWS, STICKS)
        for t in range(TILES):
            out_ref[:, t * ROWS:(t + 1) * ROWS, :] = spread[:, :, t * 128:(t + 1) * 128]
        line = jnp.sum(jnp.transpose(becp[...]), axis=0, keepdims=True)
        extra = jnp.concatenate(
            [line] + [ordered[:, t * 128:(t + 1) * 128] for t in range(TILES)], axis=0)
        out_ref[:, TILES * ROWS:TILES * ROWS + 4, :] = jnp.broadcast_to(extra[None], (PW, 4, 128))


def spread_sticks(slot, coef, proj, stick):
    table = jnp.asarray(spread_table())
    return pl.pallas_call(
        spread_kernel,
        grid=(COEFS // KC,),
        in_specs=[
            pl.BlockSpec((128, 128), lambda i: (0, 0)),
            pl.BlockSpec((2, 128, 128), lambda i: (0, 0, 0)),
            pl.BlockSpec((2, 1, KC), lambda i: (0, 0, i)),
            pl.BlockSpec(memory_space=pl.ANY),
            pl.BlockSpec((PW * TILES, 128), lambda i: (0, 0)),
            pl.BlockSpec(memory_space=pl.ANY),
        ],
        out_specs=[
            pl.BlockSpec((PW, 64, 128), lambda i: (0, 0, 0)),
            pl.BlockSpec((16, 8, 128), lambda i: (0, 0, 0)),
            pl.BlockSpec((128, 128), lambda i: (0, 0)),
            pl.BlockSpec(memory_space=pltpu.SMEM),
        ],
        out_shape=[
            jax.ShapeDtypeStruct((PW, 64, 128), F32),
            jax.ShapeDtypeStruct((16, 8, 128), F32),
            jax.ShapeDtypeStruct((128, 128), F32),
            jax.ShapeDtypeStruct((2, 16), jnp.int32),
        ],
        scratch_shapes=[
            pltpu.VMEM((6, 16, 8, 128), F32),
            pltpu.VMEM((SLOT_ROWS + WINDOW, 512), F32),
            pltpu.VMEM((128, 128), F32),
            pltpu.VMEM((512, 1536), BF16),
            pltpu.VMEM((COEFS // KC, 2, PROJ, KC), F32),
            pltpu.SemaphoreType.DMA,
            pltpu.SemaphoreType.DMA((COEFS // KC,)),
        ],
        compiler_params=pltpu.CompilerParams(vmem_limit_bytes=60 << 20),
        cost_estimate=pl.CostEstimate(flops=6 * 10 ** 9, bytes_accessed=12 << 20, transcendentals=0),
        name="spread_sticks",
    )(slot, coef.reshape(2, 128, 128), coef, proj, stick, table)


def swap_chunks(parts):
    parts = list(parts)
    chunk = lax.broadcasted_iota(jnp.int32, parts[0].shape, 1) // 16
    for bit in (1, 2, 4):
        here = (chunk & bit) == 0
        for a in range(8):
            if a & bit:
                continue
            one, two = parts[a], parts[a | bit]
            parts[a] = jnp.where(here, one, pltpu.roll(two, 16 * bit, 1))
            parts[a | bit] = jnp.where(here, pltpu.roll(one, 128 - 16 * bit, 1), two)
    return parts


def write_bounds(columns, bounds):
    chunk = jnp.floor(fold(jnp.floor(jnp.concatenate(columns, axis=0) * (1.0 / GY)))[0] * 0.125)
    first = jnp.broadcast_to(jnp.min(chunk, axis=1, keepdims=True), (GROUPS, 128))
    last = jnp.broadcast_to(jnp.max(chunk, axis=1, keepdims=True), (GROUPS, 128))
    lane = iota((GROUPS, 128), 1)
    start = jnp.sum(jnp.where(last < lane, 1.0, 0.0), axis=0, keepdims=True)
    end = jnp.sum(jnp.where(first <= lane, 1.0, 0.0), axis=0, keepdims=True)
    more = jnp.zeros((128 - GROUPS, 128), F32)
    first = jnp.transpose(jnp.concatenate([first, more], axis=0))[:1]
    last = jnp.transpose(jnp.concatenate([last, more], axis=0))[:1]
    count = jnp.where(lane[:1] < CHUNKS, end - start, 0.0)
    lines = [jnp.minimum(start, GROUPS - 1.0), end - start, first, last - first + 1.0,
             jnp.broadcast_to(jnp.max(count, axis=1, keepdims=True), (1, 128)),
             jnp.broadcast_to(jnp.max(last - first + 1.0, axis=1, keepdims=True), (1, 128)), jnp.zeros((2, 128), F32)]
    bounds[...] = jnp.concatenate(lines, axis=0).astype(jnp.int32)


def field_kernel(recv_ref, field_hbm, y_in_hbm, y_out_hbm, x_in_hbm, x_out_hbm, out_ref,
                 wide, hot, keys, signs, grid, done, sticks, field_ref, y_in_ref, y_out_ref, x_in_ref, x_out_ref,
                 bounds, range_ref, sems, range_sem):
    copies = [pltpu.make_async_copy(source, target, sems.at[at]) for at, (source, target) in enumerate((
        (field_hbm, field_ref), (y_in_hbm, y_in_ref), (y_out_hbm, y_out_ref),
        (x_in_hbm, x_in_ref), (x_out_hbm, x_out_ref)))]
    for copy in copies:
        copy.start()
    cells = []
    for g in range(4):
        mixed = swap_chunks([recv_ref[g * 8 + i, TILES * ROWS:TILES * ROWS + 8, :] for i in range(8)])
        cells.append(mixed)
    columns = [jnp.concatenate([cells[g][q % 8][1 + q // 8:2 + q // 8] for g in range(4)], axis=1)
               for q in range(GROUPS)]
    write_bounds(columns, bounds)
    range_copy = pltpu.make_async_copy(bounds, range_ref, range_sem)
    range_copy.start()
    one_hot = iota((128, 512), 0).astype(BF16)
    zero = jnp.zeros((), BF16)
    for t in range(TILES):
        mixed = [swap_chunks([recv_ref[g * 8 + i, t * ROWS:(t + 1) * ROWS, :] for i in range(8)]) for g in range(4)]
        for c in range(8):
            q = t * 8 + c
            values = jnp.concatenate([mixed[g][c] for g in range(4)], axis=1)
            high, low = split(values)
            both = jnp.concatenate([high.astype(F32), low.astype(F32)], axis=0)
            wide[q] = jnp.broadcast_to(both[:, None, :], (2 * ROWS, 16, 512)).astype(BF16)
            column = columns[q]
            x = jnp.floor(column * (1.0 / GY))
            y = column - x * GY
            _, even, odd, sign = fold(x)
            upper = iota((16, 512), 0) < 8.0
            keys[q] = jnp.where(upper, even, odd).astype(BF16)
            signs[q] = jnp.where(upper, 1.0, sign).astype(BF16)
            _, even, odd, sign = fold(y)
            hot[q, :128, :] = jnp.where(one_hot == even.astype(BF16), jnp.ones((), BF16), zero)
            hot[q, 128:, :] = jnp.where(one_hot == odd.astype(BF16), sign.astype(BF16), zero)
    for q in range(GROUPS, GROUPS + NQ):
        wide[q] = jnp.zeros((2 * ROWS, 16, 512), BF16)
        hot[q] = jnp.zeros((256, 512), BF16)
        keys[q] = jnp.full((16, 512), -1.0, BF16)
        signs[q] = jnp.zeros((16, 512), BF16)
    done[:, GX:, :] = jnp.zeros((ROWS, 16 * (NCH - 1), 512), BF16)

    step_of = iota((16, 512), 0)
    step_of = jnp.where(step_of < 8.0, step_of, step_of - 8.0)

    def place(chunk, first, groups):
        want = (step_of + (chunk * 8).astype(F32)).astype(BF16)
        masked = []
        for j in range(groups):
            mine = jnp.where(keys[first + j] == want, signs[first + j], zero)
            masked.append((wide[first + j] * mine[None]).reshape(2 * ROWS * 16, 512))
        got = mm(jnp.concatenate(masked, axis=1),
                 jnp.concatenate([hot[first + j] for j in range(groups)], axis=1), NT)
        got = got.reshape(2, ROWS, 16, 256)
        return got[0] + got[1]

    def rows_of(chunk):
        return pl.ds(pl.multiple_of(chunk * 16, 16), 16)

    def place_first(step, carry):
        chunks = [step * PLACE_UNROLL + at for at in range(PLACE_UNROLL)]
        most = functools.reduce(jnp.maximum, [range_ref[1, chunk] for chunk in chunks])

        def run(groups):
            for chunk in chunks:
                grid[:, rows_of(chunk), :] = place(chunk, range_ref[0, chunk], groups)

        pl.when(most <= NQ)(lambda: run(NQ))
        pl.when(most > NQ)(lambda: run(NQ + 1))
        return carry

    def place_rest(chunk, carry):
        def more(p, inner):
            grid[:, rows_of(chunk), :] += place(chunk, range_ref[0, chunk] + p, 1)
            return inner

        return lax.fori_loop(NQ + 1, range_ref[1, chunk], more, carry)

    range_copy.wait()
    lax.fori_loop(0, CHUNKS // PLACE_UNROLL, place_first, 0)

    @pl.when(range_ref[4, 0] > NQ + 1)
    def _():
        lax.fori_loop(0, CHUNKS, place_rest, 0)

    row = lax.broadcasted_iota(jnp.int32, (256, 256), 0)
    lane = lax.broadcasted_iota(jnp.int32, (256, 256), 1)
    even_x = ((row & 8) == 0) | (row == 8)
    even_y = lane <= 128

    def along_y(re, im, table):
        high, low = split(jnp.concatenate([re, im], axis=0))
        got = mm(jnp.concatenate([high, high, low], axis=1), table[...])
        return got[:256], got[256:]

    def along_x(re, im, table):
        high, low = split(jnp.concatenate([re, im], axis=1))
        got = mm(table[...], jnp.concatenate([high, high, low], axis=0))
        return got[:, :256], got[:, 256:]

    def plane(zz):
        re = grid[zz]
        im = grid[PLANES + zz]
        re, im = along_y(jnp.where(even_y, re, -im), jnp.where(even_y, im, re), y_in_ref)
        re, im = along_x(jnp.where(even_x, re, -im), jnp.where(even_x, im, re), x_in_ref)
        field = field_ref[zz]
        re, im = along_x(re * field, im * field, x_out_ref)
        re, im = along_y(jnp.where(even_x, re, im), jnp.where(even_x, im, -re), y_out_ref)
        high, low = split(jnp.where(even_y, re, im))
        done[zz, :GX, :256] = high
        done[zz, :GX, 256:] = low
        high, low = split(jnp.where(even_y, im, -re))
        done[PLANES + zz, :GX, :256] = high
        done[PLANES + zz, :GX, 256:] = low

    def planes(pair, carry):
        for at in range(PAIR):
            plane(pair * PAIR + at)
        return carry

    for copy in copies:
        copy.wait()
    lax.fori_loop(0, PLANES // PAIR, planes, 0)

    def pick(q, first, chunks):
        both = jnp.concatenate([hot[q], hot[q]], axis=0)
        key = keys[q].astype(F32)
        sign = signs[q].astype(F32)
        here = pl.ds(pl.multiple_of(first * 16, 16), 16 * chunks)
        lines = done[:, here, :].reshape(ROWS * 16 * chunks, 512)
        got = mm(lines, both).reshape(ROWS, 2 * chunks, 8, 512)
        total = None
        for j in range(chunks):
            want = step_of + ((first + j) * 8).astype(F32)
            mine = jnp.where(key == want, sign, 0.0)
            part = got[:, 2 * j] * mine[None, :8] + got[:, 2 * j + 1] * mine[None, 8:]
            total = part if total is None else total + part
        return jnp.sum(total, axis=1)

    def pick_first(step, carry):
        for at in range(PICK_UNROLL):
            q = step * PICK_UNROLL + at
            sticks[q] = pick(q, range_ref[2, q], NCH)
        return carry

    def pick_rest(q, carry):
        def more(p, inner):
            sticks[q] += pick(q, range_ref[2, q] + p, 1)
            return inner

        return lax.fori_loop(NCH, range_ref[3, q], more, carry)

    lax.fori_loop(0, GROUPS // PICK_UNROLL, pick_first, 0)

    @pl.when(range_ref[5, 0] > NCH)
    def _():
        lax.fori_loop(0, GROUPS, pick_rest, 0)

    for t in range(TILES):
        for g in range(4):
            mixed = swap_chunks([sticks[t * 8 + c, :, g * 128:(g + 1) * 128] for c in range(8)])
            for i in range(8):
                out_ref[g * 8 + i, t * ROWS:(t + 1) * ROWS, :] = mixed[i]


def apply_field(recv, field):
    vmem = pl.BlockSpec(memory_space=pltpu.VMEM)
    return pl.pallas_call(
        field_kernel,
        in_specs=[vmem] + [pl.BlockSpec(memory_space=pl.ANY)] * 5,
        out_specs=vmem,
        out_shape=jax.ShapeDtypeStruct((PW, 48, 128), F32),
        scratch_shapes=[
            pltpu.VMEM((GROUPS + NQ, 2 * ROWS, 16, 512), BF16),
            pltpu.VMEM((GROUPS + NQ, 256, 512), BF16),
            pltpu.VMEM((GROUPS + NQ, 16, 512), BF16),
            pltpu.VMEM((GROUPS + NQ, 16, 512), BF16),
            pltpu.VMEM((ROWS, GX, GY), F32),
            pltpu.VMEM((ROWS, GX + 16 * (NCH - 1), 512), BF16),
            pltpu.VMEM((GROUPS, ROWS, 512), F32),
            pltpu.VMEM((PLANES, GX, GY), F32),
            pltpu.VMEM((768, 256), BF16),
            pltpu.VMEM((768, 256), BF16),
            pltpu.VMEM((256, 768), BF16),
            pltpu.VMEM((256, 768), BF16),
            pltpu.VMEM((8, 128), jnp.int32),
            pltpu.SMEM((8, 128), jnp.int32),
            pltpu.SemaphoreType.DMA((5,)),
            pltpu.SemaphoreType.DMA,
        ],
        compiler_params=pltpu.CompilerParams(vmem_limit_bytes=48 << 20),
        cost_estimate=pl.CostEstimate(flops=35 * 10 ** 9, bytes_accessed=8 << 20, transcendentals=0),
        name="apply_field",
    )(recv, field, *plane_tables())


def gram_kernel(own_ref, one_ref, two_ref, three_ref, worked_ref, out_ref, becp_ref, total, small):
    step = pl.program_id(0)

    @pl.when(step == 0)
    def _():
        total[...] = jnp.zeros_like(total)
        small[...] = jnp.zeros_like(small)
        becp_ref[...] = jnp.zeros_like(becp_ref)

    span = PW // GRAM_STEPS
    here = pl.ds(pl.multiple_of(step * span, span), span)
    worked = worked_ref[...].reshape(span * TILES, 2, PLANES, 128)
    out_ref[here, :TILES * ROWS, :] = worked_ref[...]
    w_re = worked[:, 0]
    w_im = worked[:, 1]
    upper = lax.broadcasted_iota(jnp.int32, (span * 8, 128), 0) % 8 < 4
    mine = own_ref[:, 56:, :].reshape(span * 8, 128)
    weight = own_ref[:, 48:56, :].reshape(span * 8, 128)

    def halves(x):
        return pltpu.roll(x.reshape(span, 8, 128), 4, 1).reshape(span * 8, 128)

    turned = jnp.where(upper, halves(mine), -halves(mine))
    weight = jnp.where(upper, halves(weight), weight)
    for a, ref in enumerate((own_ref, one_ref, two_ref, three_ref)):
        lines = ref[:, :TILES * ROWS, :].reshape(span * TILES, 2, PLANES, 128)
        a_re = lines[:, 0]
        a_im = lines[:, 1]
        total[a] += jnp.sum(a_re * w_re + a_im * w_im, axis=0)
        total[4 + a] += jnp.sum(a_re * w_im - a_im * w_re, axis=0)
        becp_ref[a] += jnp.sum(ref[:, 48:56, :], axis=0)
        coef = ref[:, 56:, :].reshape(span * 8, 128)
        real = coef * mine
        imag = coef * turned
        for at, value in ((a, real * weight), (4 + a, imag * weight), (8 + a, real), (12 + a, imag)):
            small[at] += jnp.sum(value.reshape(span, 8, 128), axis=0)

    @pl.when(step == pl.num_programs(0) - 1)
    def _():
        scale = 1.0 / (GX * GY * GZ)
        lines = [jnp.sum(small[at] + total[at] * scale, axis=0, keepdims=True) for at in range(8)]
        lines += [jnp.sum(small[at], axis=0, keepdims=True) for at in range(8, 16)]
        lines = jnp.concatenate(lines + [jnp.zeros((112, 128), F32)], axis=0)
        line = jnp.sum(jnp.transpose(lines), axis=0, keepdims=True)
        out_ref[:, TILES * ROWS:, :] = jnp.broadcast_to(line[None], (PW, 8, 128))


def gram_part(recv, others, worked):
    span = PW // GRAM_STEPS
    return pl.pallas_call(
        gram_kernel,
        grid=(GRAM_STEPS,),
        in_specs=[pl.BlockSpec((span, 64, 128), lambda i: (i, 0, 0))] * 4 + [
            pl.BlockSpec((span, 48, 128), lambda i: (i, 0, 0)),
        ],
        out_specs=[pl.BlockSpec((PW, 56, 128), lambda i: (0, 0, 0)), pl.BlockSpec((4, 8, 128), lambda i: (0, 0, 0))],
        out_shape=[jax.ShapeDtypeStruct((PW, 56, 128), F32), jax.ShapeDtypeStruct((4, 8, 128), F32)],
        scratch_shapes=[pltpu.VMEM((8, PLANES, 128), F32), pltpu.VMEM((16, 8, 128), F32)],
        compiler_params=pltpu.CompilerParams(vmem_limit_bytes=16 << 20),
        cost_estimate=pl.CostEstimate(flops=10 ** 7, bytes_accessed=6 << 20, transcendentals=0),
        name="gram_part",
    )(recv, *others, worked)


def base_kernel(kinetic_ref, coef_ref, proj_ref, matrix_ref, becp_ref, out_ref, far_ref, weight):
    @pl.when(pl.program_id(0) == 0)
    def _():
        matrix = matrix_ref[...]
        lines = jnp.concatenate([becp_ref[a, :1, :] for a in range(4)], axis=0)
        w_re = jnp.sum(matrix * lines[:1, :PROJ], axis=1, keepdims=True)
        w_im = jnp.sum(matrix * lines[:1, PROJ:], axis=1, keepdims=True)
        weight[0] = jnp.broadcast_to(w_re, (PROJ, 128))
        weight[1] = jnp.broadcast_to(w_im, (PROJ, 128))
        down = jnp.transpose(jnp.concatenate([lines, jnp.zeros((124, 128), F32)], axis=0))
        far_re = jnp.sum(down[:PROJ] * w_re + down[PROJ:] * w_im, axis=0, keepdims=True)
        far_im = jnp.sum(down[:PROJ] * w_im - down[PROJ:] * w_re, axis=0, keepdims=True)
        far = jnp.broadcast_to(far_re, (8, 128)) + pltpu.roll(jnp.broadcast_to(far_im, (8, 128)), 4, 1)
        far_ref[...] = far

    kinetic = kinetic_ref[...]
    p_re = proj_ref[0]
    p_im = proj_ref[1]
    w_re = weight[0][:, :1]
    w_im = weight[1][:, :1]
    far_re = jnp.sum(p_re * w_re - p_im * w_im, axis=0, keepdims=True)
    far_im = jnp.sum(p_re * w_im + p_im * w_re, axis=0, keepdims=True)
    out_ref[0] = kinetic * coef_ref[0] + far_re
    out_ref[1] = kinetic * coef_ref[1] + far_im


def base_part(kinetic, coef, proj, matrix, becp):
    return pl.pallas_call(
        base_kernel,
        grid=(COEFS // KC,),
        in_specs=[
            pl.BlockSpec((1, KC), lambda i: (0, i)),
            pl.BlockSpec((2, 1, KC), lambda i: (0, 0, i)),
            pl.BlockSpec((2, PROJ, KC), lambda i: (0, 0, i)),
            pl.BlockSpec((PROJ, PROJ), lambda i: (0, 0)),
            pl.BlockSpec((4, 8, 128), lambda i: (0, 0, 0)),
        ],
        out_specs=[pl.BlockSpec((2, 1, KC), lambda i: (0, 0, i)), pl.BlockSpec((8, 128), lambda i: (0, 0))],
        out_shape=[jax.ShapeDtypeStruct((2, 1, COEFS), F32), jax.ShapeDtypeStruct((8, 128), F32)],
        scratch_shapes=[pltpu.VMEM((2, PROJ, 128), F32)],
        compiler_params=pltpu.CompilerParams(vmem_limit_bytes=16 << 20),
        cost_estimate=pl.CostEstimate(flops=10 ** 7, bytes_accessed=10 << 20, transcendentals=0),
        name="base_part",
    )(kinetic, coef, proj, matrix, becp)


def collect_kernel(span_ref, key_ref, recv_ref, stick_ref, table_ref, base_ref, far_ref, out_ref,
                   energy_ref, overlap_ref, values, found_re, found_im):
    total = jnp.sum(recv_ref[:, TILES * ROWS:, :], axis=0) + far_ref[...]
    band = lax.axis_index("band")
    lane = lax.broadcasted_iota(jnp.int32, (8, 128), 1)
    for bit in (1, 2):
        swapped = jnp.where((lane & bit) == 0, pltpu.roll(total, 128 - bit, 1), pltpu.roll(total, bit, 1))
        total = jnp.where((band & bit) != 0, swapped, total)
    for ri in range(2):
        energy_ref[ri] = total[:1, ri * 4:ri * 4 + 4]
        overlap_ref[ri] = total[:1, 8 + ri * 4:12 + ri * 4]

    order, _ = rank_of(owned_row(stick_ref))
    order = order.astype(BF16)
    lines = jnp.concatenate(
        [recv_ref[:, t * ROWS:(t + 1) * ROWS, :].reshape(512, 128) for t in range(TILES)], axis=1)
    high, low = split(lines)
    back = mm(table_ref[...], jnp.concatenate([high, high, low], axis=0))
    for at, part in enumerate(split(back)):
        part = mm(part, order).astype(BF16)
        for ri in range(2):
            for t in range(TILES):
                values[ri, t * 256:(t + 1) * 256, at * 128:(at + 1) * 128] = part[
                    ri * 256:(ri + 1) * 256, t * 128:(t + 1) * 128]
    values[:, SLOT_ROWS:, :] = jnp.zeros((2, WINDOW, 256), BF16)

    lane_of = iota((128, 1024), 0).astype(BF16)
    row_of = iota((WINDOW, 1024), 0)

    def fetch(block, first):
        row, lane = key_parts(block_row(key_ref, block))
        hit = jnp.where(lane_of == lane.astype(BF16), jnp.ones((), BF16), jnp.zeros((), BF16))
        here = pl.ds(pl.multiple_of(first, 16), WINDOW)
        got = mm(jnp.concatenate([values[0, here, :], values[1, here, :]], axis=0), jnp.concatenate([hit, hit], axis=0))
        mine = row_of == row - first.astype(F32)
        return (jnp.sum(jnp.where(mine, got[:WINDOW], 0.0), axis=0, keepdims=True),
                jnp.sum(jnp.where(mine, got[WINDOW:], 0.0), axis=0, keepdims=True))

    def put(block, pair, old):
        at = pl.ds(block // 2, 1)
        half = 8 * (block % 2)
        for ref, line in zip((found_re, found_im), pair):
            for v in range(8):
                piece = line[:, v * 128:(v + 1) * 128]
                ref[half + v, at, :] = ref[half + v, at, :] + piece if old else piece

    def one(step, carry):
        for at in range(FETCH_UNROLL):
            block = step * FETCH_UNROLL + at
            put(block, fetch(block, span_ref[0, block]), False)
        return carry

    lax.fori_loop(0, 16 // FETCH_UNROLL, one, 0)

    @pl.when(sum(span_ref[1, block] for block in range(16)) > 16)
    def _():
        def rest(block, carry):
            def more(p, inner):
                put(block, fetch(block, span_ref[0, block] + p * WINDOW), True)
                return inner

            return lax.fori_loop(1, span_ref[1, block], more, carry)

        lax.fori_loop(0, 16, rest, 0)

    scale = 1.0 / (GX * GY * GZ)
    home = []
    for v in range(16):
        key = key_ref[v]
        home.append(key - jnp.floor(key * (1.0 / 128.0)) * 128.0)
    _, (real, imag) = sort_rows(home, [[found_re[v] for v in range(16)], [found_im[v] for v in range(16)]])
    for v in range(16):
        here = slice(v * 8, (v + 1) * 8)
        out_ref[0, here, :] = base_ref[0, here, :] + real[v] * scale
        out_ref[1, here, :] = base_ref[1, here, :] + imag[v] * scale


def collect(span, key, recv, stick, base, far):
    vmem = pl.BlockSpec(memory_space=pltpu.VMEM)
    return pl.pallas_call(
        collect_kernel,
        in_specs=[pl.BlockSpec(memory_space=pltpu.SMEM)] + [vmem] * 6,
        out_specs=[vmem, vmem, vmem],
        out_shape=[
            jax.ShapeDtypeStruct((2, 128, 128), F32),
            jax.ShapeDtypeStruct((2, 1, 4), F32),
            jax.ShapeDtypeStruct((2, 1, 4), F32),
        ],
        scratch_shapes=[
            pltpu.VMEM((2, SLOT_ROWS + WINDOW, 256), BF16),
            pltpu.VMEM((16, 8, 128), F32),
            pltpu.VMEM((16, 8, 128), F32),
        ],
        compiler_params=pltpu.CompilerParams(vmem_limit_bytes=32 << 20),
        cost_estimate=pl.CostEstimate(flops=6 * 10 ** 9, bytes_accessed=4 << 20, transcendentals=0),
        name="collect",
    )(span, key, recv, stick, jnp.asarray(collect_table()), base, far)


def local(wave_coef, projector, potential, grid_slot, stick_column, proj_atom, coupling):
    stick = stick_column.reshape(PW * TILES, 128)
    sent, key, kinetic, span = spread_sticks(grid_slot.reshape(128, 128), wave_coef, projector, stick)
    recv = lax.all_to_all(sent, "pw", split_axis=0, concat_axis=0, tiled=True)
    others = [lax.ppermute(recv, "band", [(b, b ^ m) for b in range(4)]) for m in (1, 2, 3)]
    worked = apply_field(recv, potential)
    payload, becp = gram_part(recv, others, worked)
    returned = lax.all_to_all(payload, "pw", split_axis=0, concat_axis=0, tiled=True)

    same_atom = proj_atom[:, None] == proj_atom[None, :]
    matrix = jnp.where(same_atom, 0.5 * (coupling + coupling.T), 0.0)
    base, far = base_part(kinetic.reshape(1, COEFS), wave_coef, projector, matrix, becp)
    applied, energy, overlap = collect(span, key, returned, stick, base.reshape(2, 128, 128), far)
    return applied.reshape(2, 1, COEFS), energy.transpose(0, 2, 1), overlap.transpose(0, 2, 1)


def solution(mesh):
    in_specs = (
        P(None, "band", "pw"),
        P(None, None, "pw"),
        P("pw", None, None),
        P("pw"),
        P(),
        P(),
        P(),
    )
    out_specs = (P(None, "band", "pw"), P(None, None, "band"), P(None, None, "band"))
    return jax.shard_map(local, mesh=mesh, in_specs=in_specs, out_specs=out_specs, check_vma=False)
```

```python
import functools

import jax
import jax.numpy as jnp
import ml_dtypes
import numpy as np
from jax import lax
from jax.experimental import pallas as pl
from jax.experimental.pallas import tpu as pltpu
from jax.sharding import PartitionSpec as P

GX = 256
GY = 256
GZ = 256
KIN_MAX = 2.0
PRECISE = lax.Precision.HIGHEST

PW = 32
STICKS = 384
COEFS = 16384
PROJ = 64
PLANES = GZ // PW
ROWS = 2 * PLANES
KC = 4096
STEP_BLOCKS = KC // 1024
WINDOW = 320
SLOT_ROWS = 768
TILES = STICKS // 128
GROUPS = 24
CHUNKS = 16
NQ = 4
NCH = 3
PAIR = 8
PLACE_UNROLL = 4
PICK_UNROLL = 6
GRAM_STEPS = 2
FETCH_UNROLL = 16
F32 = jnp.float32
BF16 = jnp.bfloat16
NN = (((1,), (0,)), ((), ()))
NT = (((1,), (1,)), ((), ()))


def mm(left, right, dims=NN):
    return lax.dot_general(left, right, dims, preferred_element_type=F32)


def split(value):
    high = value.astype(BF16)
    low = (value - high.astype(F32)).astype(BF16)
    return high, low


def split_table(table):
    high = table.astype(np.float32).astype(ml_dtypes.bfloat16)
    low = (table - high.astype(np.float64)).astype(np.float32).astype(ml_dtypes.bfloat16)
    return high, low


def trig():
    n = np.arange(256)
    angle = 2.0 * np.pi * (np.outer(n, n) % 256) / 256.0
    return np.cos(angle), np.sin(angle)


def folded_table():
    c, s = trig()
    return np.concatenate([c[:128], c[128:129], s[1:128]], axis=0)


def plane_tables():
    table = folded_table()
    order = [128 * part + 8 * chunk + i for chunk in range(CHUNKS) for part in range(2) for i in range(8)]
    table_x = table[order]

    def left(values):
        high, low = split_table(values)
        return jnp.asarray(np.concatenate([high, low, high], axis=1))

    def right(values):
        high, low = split_table(values)
        return jnp.asarray(np.concatenate([high, low, high], axis=0))

    return right(table), right(table.T), left(table_x.T), left(table_x)


def spread_table():
    c, s = trig()
    rows = np.concatenate(
        [np.concatenate([np.concatenate([c[z], -s[z]])[None] if part == 0 else np.concatenate([s[z], c[z]])[None]
                         for z in range(d * PLANES, (d + 1) * PLANES)])
         for d in range(PW) for part in range(2)])
    high, low = split_table(rows)
    return np.concatenate([high, low, high], axis=1)


def collect_table():
    c, s = trig()
    full = np.zeros((512, 512))
    for d in range(PW):
        zs = np.arange(d * PLANES, (d + 1) * PLANES)
        at = d * ROWS
        full[:256, at:at + PLANES] = c[:, zs]
        full[:256, at + PLANES:at + ROWS] = s[:, zs]
        full[256:, at:at + PLANES] = -s[:, zs]
        full[256:, at + PLANES:at + ROWS] = c[:, zs]
    high, low = split_table(full)
    return np.concatenate([high, low, high], axis=1)


def iota(shape, dim):
    return lax.broadcasted_iota(jnp.int32, shape, dim).astype(F32)


def sort_rows(keys, values):
    keys = list(keys)
    values = [list(each) for each in values]
    sub = lax.broadcasted_iota(jnp.int32, (8, 128), 0)
    size = 2
    while size <= 128:
        dist = size // 2
        while dist >= 1:
            if dist < 16:
                for one in range(16):
                    if one & dist:
                        continue
                    two = one | dist
                    swap = keys[one] > keys[two]
                    if size < 16:
                        if one & size:
                            swap = keys[one] < keys[two]
                    elif size < 128:
                        swap = jnp.where((sub & (size // 16)) == 0, keys[one] - keys[two], keys[two] - keys[one]) > 0.0
                    for each in [keys] + values:
                        each[one], each[two] = (jnp.where(swap, each[two], each[one]),
                                                jnp.where(swap, each[one], each[two]))
            else:
                hop = dist // 16
                low = (sub & hop) == 0
                rising = (sub & (size // 16)) == 0 if size < 128 else jnp.full((8, 128), True)
                least = jnp.where(low == rising, 1.0, -1.0)

                def other(x):
                    return jnp.where(low, pltpu.roll(x, 8 - hop, 0), pltpu.roll(x, hop, 0))

                for one in range(16):
                    swap = (keys[one] - other(keys[one])) * least > 0.0
                    for each in [keys] + values:
                        each[one] = jnp.where(swap, other(each[one]), each[one])
            dist //= 2
        size *= 2
    return keys, values


def block_row(ref, block):
    at = pl.ds(block // 2, 1)
    half = 8 * (block % 2)
    return jnp.concatenate([ref[half + v, at, :] for v in range(8)], axis=1)


def key_parts(key):
    row = jnp.floor(key * (1.0 / 16384.0))
    rest = key - row * 16384.0
    return row, jnp.floor(rest * (1.0 / 128.0))


def fold(x):
    key = jnp.where(x == 128.0, 0.0, jnp.minimum(x, 256.0 - x))
    even = jnp.where(x == 128.0, -1.0, key)
    odd = jnp.where(x == 0.0, -1.0, key)
    return key, even, odd, jnp.where(x > 128.0, -1.0, 1.0)


def rank_of(owned):
    wide = jnp.broadcast_to(owned, (128, STICKS))
    down = jnp.transpose(wide)[:, :1]

    def sort_key(column):
        return fold(jnp.floor(column * (1.0 / GY)))[0] * 65536.0 + column

    key = sort_key(owned)
    key_down = sort_key(down)
    rank_row = jnp.sum(jnp.where(key_down < key, 1.0, 0.0), axis=0, keepdims=True)
    order = jnp.where(iota((STICKS, STICKS), 0) == rank_row, 1.0, 0.0)
    rank_col = jnp.sum(jnp.where(key < key_down, 1.0, 0.0), axis=1, keepdims=True)
    ordered = jnp.sum(jnp.where(iota((STICKS, STICKS), 1) == rank_col, down, 0.0), axis=0, keepdims=True)
    return order, ordered


def centred(values, length):
    return jnp.where(values < length // 2, values, values - length)


def owned_row(stick_ref):
    first = lax.axis_index("pw") * TILES
    return jnp.concatenate([stick_ref[pl.ds(first + t, 1), :] for t in range(TILES)], axis=1).astype(F32)


def kinetic_of(z, tile, lane, owned):
    x = jnp.floor(owned * (1.0 / GY))
    y = centred(owned - x * GY, GY)
    x = centred(x, GX)
    flat = x * x + y * y
    square = jnp.zeros((128, 128), F32)
    for t in range(TILES):
        line = jnp.broadcast_to(flat[:, t * 128:(t + 1) * 128], (128, 128))
        square = jnp.where(tile == t, jnp.take_along_axis(line, lane.astype(jnp.int32), axis=1), square)
    z = centred(z, GZ)
    return (square + z * z) * (KIN_MAX / 3.0 / 16384.0)


def spread_kernel(slot_ref, tile_ref, coef_ref, proj_hbm, stick_ref, table_hbm, out_ref, key_ref, kinetic_ref,
                  span_ref, parts, acc, becp, table_ref, proj_buf, table_sem, proj_sems):
    step = pl.program_id(0)
    table_copy = pltpu.make_async_copy(table_hbm, table_ref, table_sem)

    def proj_copy(at):
        here = pl.ds(pl.multiple_of(at * KC, KC), KC)
        return pltpu.make_async_copy(proj_hbm.at[:, :, here], proj_buf.at[at], proj_sems.at[at])

    @pl.when(step == 0)
    def _():
        for at in range(COEFS // KC):
            proj_copy(at).start()
        table_copy.start()
        slot = slot_ref[...].astype(F32)
        z = jnp.floor((slot + 0.5) * (1.0 / STICKS))
        s = slot - z * STICKS
        tile = jnp.floor(s * (1.0 / 128.0))
        lane = s - tile * 128.0
        place = (tile * 256.0 + z) * 128.0 + lane
        kinetic = kinetic_of(z, tile, lane, owned_row(stick_ref))
        kinetic_ref[...] = kinetic
        for d in range(PW):
            here = slice(d * 4, d * 4 + 4)
            out_ref[d, 52:56, :] = kinetic[here]
            out_ref[d, 56:60, :] = tile_ref[0, here, :]
            out_ref[d, 60:64, :] = tile_ref[1, here, :]
        row = iota((128, 128), 0)
        array = jnp.floor(row * 0.125)
        key = place * 128.0 + (row - array * 8.0) * 16.0 + array

        def rows(x):
            return [x[v * 8:(v + 1) * 8] for v in range(16)]

        keys, (real, imag) = sort_rows(rows(key), [rows(tile_ref[0]), rows(tile_ref[1])])
        for v in range(16):
            key_ref[v] = keys[v]
            for at, part in enumerate(key_parts(keys[v]) + split(real[v]) + split(imag[v])):
                parts[at, v] = part.astype(F32)
        for block in range(16):
            half = 8 * (block % 2)
            at = block // 2
            first = jnp.min(key_parts(keys[half][at:at + 1])[0]).astype(jnp.int32)
            last = jnp.max(key_parts(keys[half + 7][at:at + 1])[0]).astype(jnp.int32)
            first = (first >> 4) << 4
            span_ref[0, block] = first
            span_ref[1, block] = lax.div(last - first, WINDOW) + 1
        acc[...] = jnp.zeros_like(acc)
        becp[...] = jnp.zeros_like(becp)

    none = jnp.zeros((), BF16)
    lane_of = (iota((128, 1024), 0)).astype(BF16)
    row_of = (iota((WINDOW, 1024), 0) - 128.0).astype(BF16)

    def product(block, first):
        row, lane, re_hi, re_lo, im_hi, im_lo = [block_row(parts.at[at], block) for at in range(6)]
        hit = lane_of == lane.astype(BF16)
        placed = jnp.concatenate(
            [jnp.where(hit, part.astype(BF16), none) for part in (re_hi, im_hi, re_lo, im_lo)], axis=0)
        want = row - (first + 128).astype(F32)
        hot = jnp.where(row_of == want.astype(BF16), jnp.ones((), BF16), none)
        return mm(hot, placed, NT)

    def window(first):
        return pl.ds(pl.multiple_of(first, 16), WINDOW)

    blocks = [step * STEP_BLOCKS + at for at in range(STEP_BLOCKS)]
    for block in blocks:
        first = span_ref[0, block]
        acc[window(first), :] += product(block, first)

    @pl.when(sum(span_ref[1, block] for block in blocks) > STEP_BLOCKS)
    def _():
        def rest(at, carry):
            block = step * STEP_BLOCKS + at

            def more(p, inner):
                first = span_ref[0, block] + p * WINDOW
                acc[window(first), :] += product(block, first)
                return inner

            return lax.fori_loop(1, span_ref[1, block], more, carry)

        lax.fori_loop(0, STEP_BLOCKS, rest, 0)

    c_re = coef_ref[0]
    c_im = coef_ref[1]
    proj_copy(step).wait()
    p_re = proj_buf[step, 0]
    p_im = proj_buf[step, 1]
    real = p_re * c_re + p_im * c_im
    imag = p_re * c_im - p_im * c_re
    both = jnp.concatenate([real, imag], axis=0)
    total = both[:, :128]
    for at in range(128, KC, 128):
        total = total + both[:, at:at + 128]
    becp[...] += total

    @pl.when(step == pl.num_programs(0) - 1)
    def _():
        order, ordered = rank_of(owned_row(stick_ref))
        sticks = jnp.concatenate(
            [jnp.concatenate([acc[t * 256:(t + 1) * 256, part * 128:(part + 1) * 128] for t in range(TILES)], axis=1)
             for part in range(4)], axis=0).astype(BF16)
        sticks = mm(sticks, order.astype(BF16), NT).astype(BF16)
        high = sticks[:512]
        low = sticks[512:]
        table_copy.wait()
        spread = mm(table_ref[...], jnp.concatenate([high, high, low], axis=0))
        spread = spread.reshape(PW, ROWS, STICKS)
        for t in range(TILES):
            out_ref[:, t * ROWS:(t + 1) * ROWS, :] = spread[:, :, t * 128:(t + 1) * 128]
        line = jnp.sum(jnp.transpose(becp[...]), axis=0, keepdims=True)
        extra = jnp.concatenate(
            [line] + [ordered[:, t * 128:(t + 1) * 128] for t in range(TILES)], axis=0)
        out_ref[:, TILES * ROWS:TILES * ROWS + 4, :] = jnp.broadcast_to(extra[None], (PW, 4, 128))


def spread_sticks(slot, coef, proj, stick):
    table = jnp.asarray(spread_table())
    return pl.pallas_call(
        spread_kernel,
        grid=(COEFS // KC,),
        in_specs=[
            pl.BlockSpec((128, 128), lambda i: (0, 0)),
            pl.BlockSpec((2, 128, 128), lambda i: (0, 0, 0)),
            pl.BlockSpec((2, 1, KC), lambda i: (0, 0, i)),
            pl.BlockSpec(memory_space=pl.ANY),
            pl.BlockSpec((PW * TILES, 128), lambda i: (0, 0)),
            pl.BlockSpec(memory_space=pl.ANY),
        ],
        out_specs=[
            pl.BlockSpec((PW, 64, 128), lambda i: (0, 0, 0)),
            pl.BlockSpec((16, 8, 128), lambda i: (0, 0, 0)),
            pl.BlockSpec((128, 128), lambda i: (0, 0)),
            pl.BlockSpec(memory_space=pltpu.SMEM),
        ],
        out_shape=[
            jax.ShapeDtypeStruct((PW, 64, 128), F32),
            jax.ShapeDtypeStruct((16, 8, 128), F32),
            jax.ShapeDtypeStruct((128, 128), F32),
            jax.ShapeDtypeStruct((2, 16), jnp.int32),
        ],
        scratch_shapes=[
            pltpu.VMEM((6, 16, 8, 128), F32),
            pltpu.VMEM((SLOT_ROWS + WINDOW, 512), F32),
            pltpu.VMEM((128, 128), F32),
            pltpu.VMEM((512, 1536), BF16),
            pltpu.VMEM((COEFS // KC, 2, PROJ, KC), F32),
            pltpu.SemaphoreType.DMA,
            pltpu.SemaphoreType.DMA((COEFS // KC,)),
        ],
        compiler_params=pltpu.CompilerParams(vmem_limit_bytes=60 << 20),
        cost_estimate=pl.CostEstimate(flops=6 * 10 ** 9, bytes_accessed=12 << 20, transcendentals=0),
        name="spread_sticks",
    )(slot, coef.reshape(2, 128, 128), coef, proj, stick, table)


def swap_chunks(parts):
    parts = list(parts)
    chunk = lax.broadcasted_iota(jnp.int32, parts[0].shape, 1) // 16
    for bit in (1, 2, 4):
        here = (chunk & bit) == 0
        for a in range(8):
            if a & bit:
                continue
            one, two = parts[a], parts[a | bit]
            parts[a] = jnp.where(here, one, pltpu.roll(two, 16 * bit, 1))
            parts[a | bit] = jnp.where(here, pltpu.roll(one, 128 - 16 * bit, 1), two)
    return parts


def write_bounds(columns, bounds):
    chunk = jnp.floor(fold(jnp.floor(jnp.concatenate(columns, axis=0) * (1.0 / GY)))[0] * 0.125)
    first = jnp.broadcast_to(jnp.min(chunk, axis=1, keepdims=True), (GROUPS, 128))
    last = jnp.broadcast_to(jnp.max(chunk, axis=1, keepdims=True), (GROUPS, 128))
    lane = iota((GROUPS, 128), 1)
    start = jnp.sum(jnp.where(last < lane, 1.0, 0.0), axis=0, keepdims=True)
    end = jnp.sum(jnp.where(first <= lane, 1.0, 0.0), axis=0, keepdims=True)
    more = jnp.zeros((128 - GROUPS, 128), F32)
    first = jnp.transpose(jnp.concatenate([first, more], axis=0))[:1]
    last = jnp.transpose(jnp.concatenate([last, more], axis=0))[:1]
    count = jnp.where(lane[:1] < CHUNKS, end - start, 0.0)
    lines = [jnp.minimum(start, GROUPS - 1.0), end - start, first, last - first + 1.0,
             jnp.broadcast_to(jnp.max(count, axis=1, keepdims=True), (1, 128)),
             jnp.broadcast_to(jnp.max(last - first + 1.0, axis=1, keepdims=True), (1, 128)), jnp.zeros((2, 128), F32)]
    bounds[...] = jnp.concatenate(lines, axis=0).astype(jnp.int32)


def field_kernel(recv_ref, field_hbm, y_in_hbm, y_out_hbm, x_in_hbm, x_out_hbm, out_ref,
                 wide, hot, keys, signs, grid, done, sticks, field_ref, y_in_ref, y_out_ref, x_in_ref, x_out_ref,
                 bounds, range_ref, sems, range_sem):
    copies = [pltpu.make_async_copy(source, target, sems.at[at]) for at, (source, target) in enumerate((
        (field_hbm, field_ref), (y_in_hbm, y_in_ref), (y_out_hbm, y_out_ref),
        (x_in_hbm, x_in_ref), (x_out_hbm, x_out_ref)))]
    for copy in copies:
        copy.start()
    cells = []
    for g in range(4):
        mixed = swap_chunks([recv_ref[g * 8 + i, TILES * ROWS:TILES * ROWS + 8, :] for i in range(8)])
        cells.append(mixed)
    columns = [jnp.concatenate([cells[g][q % 8][1 + q // 8:2 + q // 8] for g in range(4)], axis=1)
               for q in range(GROUPS)]
    write_bounds(columns, bounds)
    range_copy = pltpu.make_async_copy(bounds, range_ref, range_sem)
    range_copy.start()
    one_hot = iota((128, 512), 0).astype(BF16)
    zero = jnp.zeros((), BF16)
    for t in range(TILES):
        mixed = [swap_chunks([recv_ref[g * 8 + i, t * ROWS:(t + 1) * ROWS, :] for i in range(8)]) for g in range(4)]
        for c in range(8):
            q = t * 8 + c
            values = jnp.concatenate([mixed[g][c] for g in range(4)], axis=1)
            high, low = split(values)
            both = jnp.concatenate([high.astype(F32), low.astype(F32)], axis=0)
            wide[q] = jnp.broadcast_to(both[:, None, :], (2 * ROWS, 16, 512)).astype(BF16)
            column = columns[q]
            x = jnp.floor(column * (1.0 / GY))
            y = column - x * GY
            _, even, odd, sign = fold(x)
            upper = iota((16, 512), 0) < 8.0
            keys[q] = jnp.where(upper, even, odd).astype(BF16)
            signs[q] = jnp.where(upper, 1.0, sign).astype(BF16)
            _, even, odd, sign = fold(y)
            hot[q, :128, :] = jnp.where(one_hot == even.astype(BF16), jnp.ones((), BF16), zero)
            hot[q, 128:, :] = jnp.where(one_hot == odd.astype(BF16), sign.astype(BF16), zero)
    for q in range(GROUPS, GROUPS + NQ):
        wide[q] = jnp.zeros((2 * ROWS, 16, 512), BF16)
        hot[q] = jnp.zeros((256, 512), BF16)
        keys[q] = jnp.full((16, 512), -1.0, BF16)
        signs[q] = jnp.zeros((16, 512), BF16)
    done[:, GX:, :] = jnp.zeros((ROWS, 16 * (NCH - 1), 512), BF16)

    step_of = iota((16, 512), 0)
    step_of = jnp.where(step_of < 8.0, step_of, step_of - 8.0)

    def place(chunk, first, groups):
        want = (step_of + (chunk * 8).astype(F32)).astype(BF16)
        masked = []
        for j in range(groups):
            mine = jnp.where(keys[first + j] == want, signs[first + j], zero)
            masked.append((wide[first + j] * mine[None]).reshape(2 * ROWS * 16, 512))
        got = mm(jnp.concatenate(masked, axis=1),
                 jnp.concatenate([hot[first + j] for j in range(groups)], axis=1), NT)
        got = got.reshape(2, ROWS, 16, 256)
        return got[0] + got[1]

    def rows_of(chunk):
        return pl.ds(pl.multiple_of(chunk * 16, 16), 16)

    def place_first(step, carry):
        chunks = [step * PLACE_UNROLL + at for at in range(PLACE_UNROLL)]
        most = functools.reduce(jnp.maximum, [range_ref[1, chunk] for chunk in chunks])

        def run(groups):
            for chunk in chunks:
                grid[:, rows_of(chunk), :] = place(chunk, range_ref[0, chunk], groups)

        pl.when(most <= NQ)(lambda: run(NQ))
        pl.when(most > NQ)(lambda: run(NQ + 1))
        return carry

    def place_rest(chunk, carry):
        def more(p, inner):
            grid[:, rows_of(chunk), :] += place(chunk, range_ref[0, chunk] + p, 1)
            return inner

        return lax.fori_loop(NQ + 1, range_ref[1, chunk], more, carry)

    range_copy.wait()
    lax.fori_loop(0, CHUNKS // PLACE_UNROLL, place_first, 0)

    @pl.when(range_ref[4, 0] > NQ + 1)
    def _():
        lax.fori_loop(0, CHUNKS, place_rest, 0)

    row = lax.broadcasted_iota(jnp.int32, (256, 256), 0)
    lane = lax.broadcasted_iota(jnp.int32, (256, 256), 1)
    even_x = ((row & 8) == 0) | (row == 8)
    even_y = lane <= 128

    def along_y(re, im, table):
        high, low = split(jnp.concatenate([re, im], axis=0))
        got = mm(jnp.concatenate([high, high, low], axis=1), table[...])
        return got[:256], got[256:]

    def along_x(re, im, table):
        high, low = split(jnp.concatenate([re, im], axis=1))
        got = mm(table[...], jnp.concatenate([high, high, low], axis=0))
        return got[:, :256], got[:, 256:]

    def plane(zz):
        re = grid[zz]
        im = grid[PLANES + zz]
        re, im = along_y(jnp.where(even_y, re, -im), jnp.where(even_y, im, re), y_in_ref)
        re, im = along_x(jnp.where(even_x, re, -im), jnp.where(even_x, im, re), x_in_ref)
        field = field_ref[zz]
        re, im = along_x(re * field, im * field, x_out_ref)
        re, im = along_y(jnp.where(even_x, re, im), jnp.where(even_x, im, -re), y_out_ref)
        high, low = split(jnp.where(even_y, re, im))
        done[zz, :GX, :256] = high
        done[zz, :GX, 256:] = low
        high, low = split(jnp.where(even_y, im, -re))
        done[PLANES + zz, :GX, :256] = high
        done[PLANES + zz, :GX, 256:] = low

    def planes(pair, carry):
        for at in range(PAIR):
            plane(pair * PAIR + at)
        return carry

    for copy in copies:
        copy.wait()
    lax.fori_loop(0, PLANES // PAIR, planes, 0)

    def pick(q, first, chunks):
        both = jnp.concatenate([hot[q], hot[q]], axis=0)
        key = keys[q].astype(F32)
        sign = signs[q].astype(F32)
        here = pl.ds(pl.multiple_of(first * 16, 16), 16 * chunks)
        lines = done[:, here, :].reshape(ROWS * 16 * chunks, 512)
        got = mm(lines, both).reshape(ROWS, 2 * chunks, 8, 512)
        total = None
        for j in range(chunks):
            want = step_of + ((first + j) * 8).astype(F32)
            mine = jnp.where(key == want, sign, 0.0)
            part = got[:, 2 * j] * mine[None, :8] + got[:, 2 * j + 1] * mine[None, 8:]
            total = part if total is None else total + part
        return jnp.sum(total, axis=1)

    def pick_first(step, carry):
        for at in range(PICK_UNROLL):
            q = step * PICK_UNROLL + at
            sticks[q] = pick(q, range_ref[2, q], NCH)
        return carry

    def pick_rest(q, carry):
        def more(p, inner):
            sticks[q] += pick(q, range_ref[2, q] + p, 1)
            return inner

        return lax.fori_loop(NCH, range_ref[3, q], more, carry)

    lax.fori_loop(0, GROUPS // PICK_UNROLL, pick_first, 0)

    @pl.when(range_ref[5, 0] > NCH)
    def _():
        lax.fori_loop(0, GROUPS, pick_rest, 0)

    for t in range(TILES):
        for g in range(4):
            mixed = swap_chunks([sticks[t * 8 + c, :, g * 128:(g + 1) * 128] for c in range(8)])
            for i in range(8):
                out_ref[g * 8 + i, t * ROWS:(t + 1) * ROWS, :] = mixed[i]


def apply_field(recv, field):
    vmem = pl.BlockSpec(memory_space=pltpu.VMEM)
    return pl.pallas_call(
        field_kernel,
        in_specs=[vmem] + [pl.BlockSpec(memory_space=pl.ANY)] * 5,
        out_specs=vmem,
        out_shape=jax.ShapeDtypeStruct((PW, 48, 128), F32),
        scratch_shapes=[
            pltpu.VMEM((GROUPS + NQ, 2 * ROWS, 16, 512), BF16),
            pltpu.VMEM((GROUPS + NQ, 256, 512), BF16),
            pltpu.VMEM((GROUPS + NQ, 16, 512), BF16),
            pltpu.VMEM((GROUPS + NQ, 16, 512), BF16),
            pltpu.VMEM((ROWS, GX, GY), F32),
            pltpu.VMEM((ROWS, GX + 16 * (NCH - 1), 512), BF16),
            pltpu.VMEM((GROUPS, ROWS, 512), F32),
            pltpu.VMEM((PLANES, GX, GY), F32),
            pltpu.VMEM((768, 256), BF16),
            pltpu.VMEM((768, 256), BF16),
            pltpu.VMEM((256, 768), BF16),
            pltpu.VMEM((256, 768), BF16),
            pltpu.VMEM((8, 128), jnp.int32),
            pltpu.SMEM((8, 128), jnp.int32),
            pltpu.SemaphoreType.DMA((5,)),
            pltpu.SemaphoreType.DMA,
        ],
        compiler_params=pltpu.CompilerParams(vmem_limit_bytes=48 << 20),
        cost_estimate=pl.CostEstimate(flops=35 * 10 ** 9, bytes_accessed=8 << 20, transcendentals=0),
        name="apply_field",
    )(recv, field, *plane_tables())


def add_pairs(span, own_ref, refs, worked_ref, total, small, becp_ref):
    worked = worked_ref[...].reshape(span * TILES, 2, PLANES, 128)
    w_re = worked[:, 0]
    w_im = worked[:, 1]
    upper = lax.broadcasted_iota(jnp.int32, (span * 8, 128), 0) % 8 < 4
    mine = own_ref[:, 56:, :].reshape(span * 8, 128)
    weight = own_ref[:, 48:56, :].reshape(span * 8, 128)

    def halves(x):
        return pltpu.roll(x.reshape(span, 8, 128), 4, 1).reshape(span * 8, 128)

    turned = jnp.where(upper, halves(mine), -halves(mine))
    weight = jnp.where(upper, halves(weight), weight)
    for a, ref in refs.items():
        lines = ref[:, :TILES * ROWS, :].reshape(span * TILES, 2, PLANES, 128)
        a_re = lines[:, 0]
        a_im = lines[:, 1]
        total[a] += jnp.sum(a_re * w_re + a_im * w_im, axis=0)
        total[4 + a] += jnp.sum(a_re * w_im - a_im * w_re, axis=0)
        becp_ref[a] += jnp.sum(ref[:, 48:56, :], axis=0)
        coef = ref[:, 56:, :].reshape(span * 8, 128)
        real = coef * mine
        imag = coef * turned
        for at, value in ((a, real * weight), (4 + a, imag * weight), (8 + a, real), (12 + a, imag)):
            small[at] += jnp.sum(value.reshape(span, 8, 128), axis=0)


def first_kernel(own_ref, one_ref, two_ref, worked_ref, total, small, becp_ref):
    @pl.when(pl.program_id(0) == 0)
    def _():
        total[...] = jnp.zeros_like(total)
        small[...] = jnp.zeros_like(small)
        becp_ref[...] = jnp.zeros_like(becp_ref)

    add_pairs(PW // GRAM_STEPS, own_ref, {0: own_ref, 1: one_ref, 2: two_ref}, worked_ref, total, small, becp_ref)


def last_kernel(total_ref, small_ref, sums_ref, own_ref, three_ref, worked_ref, out_ref, becp_ref, total, small):
    step = pl.program_id(0)

    @pl.when(step == 0)
    def _():
        total[...] = total_ref[...]
        small[...] = small_ref[...]
        becp_ref[...] = sums_ref[...]

    span = PW // GRAM_STEPS
    here = pl.ds(pl.multiple_of(step * span, span), span)
    out_ref[here, :TILES * ROWS, :] = worked_ref[...]
    add_pairs(span, own_ref, {3: three_ref}, worked_ref, total, small, becp_ref)

    @pl.when(step == pl.num_programs(0) - 1)
    def _():
        scale = 1.0 / (GX * GY * GZ)
        lines = [jnp.sum(small[at] + total[at] * scale, axis=0, keepdims=True) for at in range(8)]
        lines += [jnp.sum(small[at], axis=0, keepdims=True) for at in range(8, 16)]
        lines = jnp.concatenate(lines + [jnp.zeros((112, 128), F32)], axis=0)
        line = jnp.sum(jnp.transpose(lines), axis=0, keepdims=True)
        out_ref[:, TILES * ROWS:, :] = jnp.broadcast_to(line[None], (PW, 8, 128))


SUM_SHAPES = ((8, PLANES, 128), (16, 8, 128), (4, 8, 128))


def gram_first(sticks, worked):
    span = PW // GRAM_STEPS
    return pl.pallas_call(
        first_kernel,
        grid=(GRAM_STEPS,),
        in_specs=[pl.BlockSpec((span, 64, 128), lambda i: (i, 0, 0))] * 3 + [
            pl.BlockSpec((span, 48, 128), lambda i: (i, 0, 0)),
        ],
        out_specs=[pl.BlockSpec(shape, lambda i: (0, 0, 0)) for shape in SUM_SHAPES],
        out_shape=[jax.ShapeDtypeStruct(shape, F32) for shape in SUM_SHAPES],
        compiler_params=pltpu.CompilerParams(vmem_limit_bytes=16 << 20),
        cost_estimate=pl.CostEstimate(flops=10 ** 7, bytes_accessed=5 << 20, transcendentals=0),
        name="gram_first",
    )(*sticks, worked)


def gram_last(sums, recv, three, worked):
    span = PW // GRAM_STEPS
    return pl.pallas_call(
        last_kernel,
        grid=(GRAM_STEPS,),
        in_specs=[pl.BlockSpec(shape, lambda i: (0, 0, 0)) for shape in SUM_SHAPES]
        + [pl.BlockSpec((span, 64, 128), lambda i: (i, 0, 0))] * 2
        + [pl.BlockSpec((span, 48, 128), lambda i: (i, 0, 0))],
        out_specs=[pl.BlockSpec((PW, 56, 128), lambda i: (0, 0, 0)), pl.BlockSpec((4, 8, 128), lambda i: (0, 0, 0))],
        out_shape=[jax.ShapeDtypeStruct((PW, 56, 128), F32), jax.ShapeDtypeStruct((4, 8, 128), F32)],
        scratch_shapes=[pltpu.VMEM((8, PLANES, 128), F32), pltpu.VMEM((16, 8, 128), F32)],
        compiler_params=pltpu.CompilerParams(vmem_limit_bytes=16 << 20),
        cost_estimate=pl.CostEstimate(flops=10 ** 7, bytes_accessed=4 << 20, transcendentals=0),
        name="gram_last",
    )(*sums, recv, three, worked)


def base_kernel(kinetic_ref, coef_ref, proj_ref, matrix_ref, becp_ref, out_ref, far_ref, weight):
    @pl.when(pl.program_id(0) == 0)
    def _():
        matrix = matrix_ref[...]
        lines = jnp.concatenate([becp_ref[a, :1, :] for a in range(4)], axis=0)
        w_re = jnp.sum(matrix * lines[:1, :PROJ], axis=1, keepdims=True)
        w_im = jnp.sum(matrix * lines[:1, PROJ:], axis=1, keepdims=True)
        weight[0] = jnp.broadcast_to(w_re, (PROJ, 128))
        weight[1] = jnp.broadcast_to(w_im, (PROJ, 128))
        down = jnp.transpose(jnp.concatenate([lines, jnp.zeros((124, 128), F32)], axis=0))
        far_re = jnp.sum(down[:PROJ] * w_re + down[PROJ:] * w_im, axis=0, keepdims=True)
        far_im = jnp.sum(down[:PROJ] * w_im - down[PROJ:] * w_re, axis=0, keepdims=True)
        far = jnp.broadcast_to(far_re, (8, 128)) + pltpu.roll(jnp.broadcast_to(far_im, (8, 128)), 4, 1)
        far_ref[...] = far

    kinetic = kinetic_ref[...]
    p_re = proj_ref[0]
    p_im = proj_ref[1]
    w_re = weight[0][:, :1]
    w_im = weight[1][:, :1]
    far_re = jnp.sum(p_re * w_re - p_im * w_im, axis=0, keepdims=True)
    far_im = jnp.sum(p_re * w_im + p_im * w_re, axis=0, keepdims=True)
    out_ref[0] = kinetic * coef_ref[0] + far_re
    out_ref[1] = kinetic * coef_ref[1] + far_im


def base_part(kinetic, coef, proj, matrix, becp):
    return pl.pallas_call(
        base_kernel,
        grid=(COEFS // KC,),
        in_specs=[
            pl.BlockSpec((1, KC), lambda i: (0, i)),
            pl.BlockSpec((2, 1, KC), lambda i: (0, 0, i)),
            pl.BlockSpec((2, PROJ, KC), lambda i: (0, 0, i)),
            pl.BlockSpec((PROJ, PROJ), lambda i: (0, 0)),
            pl.BlockSpec((4, 8, 128), lambda i: (0, 0, 0)),
        ],
        out_specs=[pl.BlockSpec((2, 1, KC), lambda i: (0, 0, i)), pl.BlockSpec((8, 128), lambda i: (0, 0))],
        out_shape=[jax.ShapeDtypeStruct((2, 1, COEFS), F32), jax.ShapeDtypeStruct((8, 128), F32)],
        scratch_shapes=[pltpu.VMEM((2, PROJ, 128), F32)],
        compiler_params=pltpu.CompilerParams(vmem_limit_bytes=16 << 20),
        cost_estimate=pl.CostEstimate(flops=10 ** 7, bytes_accessed=10 << 20, transcendentals=0),
        name="base_part",
    )(kinetic, coef, proj, matrix, becp)


def collect_kernel(span_ref, key_ref, recv_ref, stick_ref, table_ref, base_ref, far_ref, out_ref,
                   energy_ref, overlap_ref, values, found_re, found_im):
    total = jnp.sum(recv_ref[:, TILES * ROWS:, :], axis=0) + far_ref[...]
    band = lax.axis_index("band")
    lane = lax.broadcasted_iota(jnp.int32, (8, 128), 1)
    for bit in (1, 2):
        swapped = jnp.where((lane & bit) == 0, pltpu.roll(total, 128 - bit, 1), pltpu.roll(total, bit, 1))
        total = jnp.where((band & bit) != 0, swapped, total)
    for ri in range(2):
        energy_ref[ri] = total[:1, ri * 4:ri * 4 + 4]
        overlap_ref[ri] = total[:1, 8 + ri * 4:12 + ri * 4]

    order, _ = rank_of(owned_row(stick_ref))
    order = order.astype(BF16)
    lines = jnp.concatenate(
        [recv_ref[:, t * ROWS:(t + 1) * ROWS, :].reshape(512, 128) for t in range(TILES)], axis=1)
    high, low = split(lines)
    back = mm(table_ref[...], jnp.concatenate([high, high, low], axis=0))
    for at, part in enumerate(split(back)):
        part = mm(part, order).astype(BF16)
        for ri in range(2):
            for t in range(TILES):
                values[ri, t * 256:(t + 1) * 256, at * 128:(at + 1) * 128] = part[
                    ri * 256:(ri + 1) * 256, t * 128:(t + 1) * 128]
    values[:, SLOT_ROWS:, :] = jnp.zeros((2, WINDOW, 256), BF16)

    lane_of = iota((128, 1024), 0).astype(BF16)
    row_of = iota((WINDOW, 1024), 0)

    def fetch(block, first):
        row, lane = key_parts(block_row(key_ref, block))
        hit = jnp.where(lane_of == lane.astype(BF16), jnp.ones((), BF16), jnp.zeros((), BF16))
        here = pl.ds(pl.multiple_of(first, 16), WINDOW)
        got = mm(jnp.concatenate([values[0, here, :], values[1, here, :]], axis=0), jnp.concatenate([hit, hit], axis=0))
        mine = row_of == row - first.astype(F32)
        return (jnp.sum(jnp.where(mine, got[:WINDOW], 0.0), axis=0, keepdims=True),
                jnp.sum(jnp.where(mine, got[WINDOW:], 0.0), axis=0, keepdims=True))

    def put(block, pair, old):
        at = pl.ds(block // 2, 1)
        half = 8 * (block % 2)
        for ref, line in zip((found_re, found_im), pair):
            for v in range(8):
                piece = line[:, v * 128:(v + 1) * 128]
                ref[half + v, at, :] = ref[half + v, at, :] + piece if old else piece

    def one(step, carry):
        for at in range(FETCH_UNROLL):
            block = step * FETCH_UNROLL + at
            put(block, fetch(block, span_ref[0, block]), False)
        return carry

    lax.fori_loop(0, 16 // FETCH_UNROLL, one, 0)

    @pl.when(sum(span_ref[1, block] for block in range(16)) > 16)
    def _():
        def rest(block, carry):
            def more(p, inner):
                put(block, fetch(block, span_ref[0, block] + p * WINDOW), True)
                return inner

            return lax.fori_loop(1, span_ref[1, block], more, carry)

        lax.fori_loop(0, 16, rest, 0)

    scale = 1.0 / (GX * GY * GZ)
    home = []
    for v in range(16):
        key = key_ref[v]
        home.append(key - jnp.floor(key * (1.0 / 128.0)) * 128.0)
    _, (real, imag) = sort_rows(home, [[found_re[v] for v in range(16)], [found_im[v] for v in range(16)]])
    for v in range(16):
        here = slice(v * 8, (v + 1) * 8)
        out_ref[0, here, :] = base_ref[0, here, :] + real[v] * scale
        out_ref[1, here, :] = base_ref[1, here, :] + imag[v] * scale


def collect(span, key, recv, stick, base, far):
    vmem = pl.BlockSpec(memory_space=pltpu.VMEM)
    return pl.pallas_call(
        collect_kernel,
        in_specs=[pl.BlockSpec(memory_space=pltpu.SMEM)] + [vmem] * 6,
        out_specs=[vmem, vmem, vmem],
        out_shape=[
            jax.ShapeDtypeStruct((2, 128, 128), F32),
            jax.ShapeDtypeStruct((2, 1, 4), F32),
            jax.ShapeDtypeStruct((2, 1, 4), F32),
        ],
        scratch_shapes=[
            pltpu.VMEM((2, SLOT_ROWS + WINDOW, 256), BF16),
            pltpu.VMEM((16, 8, 128), F32),
            pltpu.VMEM((16, 8, 128), F32),
        ],
        compiler_params=pltpu.CompilerParams(vmem_limit_bytes=32 << 20),
        cost_estimate=pl.CostEstimate(flops=6 * 10 ** 9, bytes_accessed=4 << 20, transcendentals=0),
        name="collect",
    )(span, key, recv, stick, jnp.asarray(collect_table()), base, far)


def local(wave_coef, projector, potential, grid_slot, stick_column, proj_atom, coupling):
    stick = stick_column.reshape(PW * TILES, 128)
    sent, key, kinetic, span = spread_sticks(grid_slot.reshape(128, 128), wave_coef, projector, stick)
    recv = lax.all_to_all(sent, "pw", split_axis=0, concat_axis=0, tiled=True)
    one = lax.ppermute(recv, "band", [(b, b ^ 1) for b in range(4)])
    two = lax.ppermute(recv, "band", [(b, b ^ 2) for b in range(4)])
    worked = apply_field(recv, potential)
    late, _ = lax.optimization_barrier((two, worked))
    three = lax.ppermute(late, "band", [(b, b ^ 1) for b in range(4)])
    payload, becp = gram_last(gram_first((recv, one, two), worked), recv, three, worked)
    returned = lax.all_to_all(payload, "pw", split_axis=0, concat_axis=0, tiled=True)

    same_atom = proj_atom[:, None] == proj_atom[None, :]
    matrix = jnp.where(same_atom, 0.5 * (coupling + coupling.T), 0.0)
    base, far = base_part(kinetic.reshape(1, COEFS), wave_coef, projector, matrix, becp)
    applied, energy, overlap = collect(span, key, returned, stick, base.reshape(2, 128, 128), far)
    return applied.reshape(2, 1, COEFS), energy.transpose(0, 2, 1), overlap.transpose(0, 2, 1)


def solution(mesh):
    in_specs = (
        P(None, "band", "pw"),
        P(None, None, "pw"),
        P("pw", None, None),
        P("pw"),
        P(),
        P(),
        P(),
    )
    out_specs = (P(None, "band", "pw"), P(None, None, "band"), P(None, None, "band"))
    return jax.shard_map(local, mesh=mesh, in_specs=in_specs, out_specs=out_specs, check_vma=False)
```

```python
import functools

import jax
import jax.numpy as jnp
import ml_dtypes
import numpy as np
from jax import lax
from jax.experimental import pallas as pl
from jax.experimental.pallas import tpu as pltpu
from jax.sharding import PartitionSpec as P

GX = 256
GY = 256
GZ = 256
KIN_MAX = 2.0
PRECISE = lax.Precision.HIGHEST

PW = 32
STICKS = 384
COEFS = 16384
PROJ = 64
PLANES = GZ // PW
ROWS = 2 * PLANES
KC = 4096
STEP_BLOCKS = KC // 1024
WINDOW = 320
WINDOWS = (208, 256, 272, 288, 304, 320, 320, 320, 320, 320, 320, 304, 288, 272, 256, 208)
SLOT_ROWS = 768
TILES = STICKS // 128
GROUPS = 24
CHUNKS = 16
NQ = 4
NCH = 3
PAIR = 8
PLACE_UNROLL = 4
PICK_UNROLL = 6
GRAM_STEPS = 2
F32 = jnp.float32
BF16 = jnp.bfloat16
NN = (((1,), (0,)), ((), ()))
NT = (((1,), (1,)), ((), ()))


def mm(left, right, dims=NN):
    return lax.dot_general(left, right, dims, preferred_element_type=F32)


def split(value):
    high = value.astype(BF16)
    low = (value - high.astype(F32)).astype(BF16)
    return high, low


def split_table(table):
    high = table.astype(np.float32).astype(ml_dtypes.bfloat16)
    low = (table - high.astype(np.float64)).astype(np.float32).astype(ml_dtypes.bfloat16)
    return high, low


def trig():
    n = np.arange(256)
    angle = 2.0 * np.pi * (np.outer(n, n) % 256) / 256.0
    return np.cos(angle), np.sin(angle)


def folded_table():
    c, s = trig()
    return np.concatenate([c[:128], c[128:129], s[1:128]], axis=0)


def plane_tables():
    table = folded_table()
    order = [128 * part + 8 * chunk + i for chunk in range(CHUNKS) for part in range(2) for i in range(8)]
    table_x = table[order]

    def left(values):
        high, low = split_table(values)
        return jnp.asarray(np.concatenate([high, low, high], axis=1))

    def right(values):
        high, low = split_table(values)
        return jnp.asarray(np.concatenate([high, low, high], axis=0))

    return right(table), right(table.T), left(table_x.T), left(table_x)


def spread_table():
    c, s = trig()
    rows = np.concatenate(
        [np.concatenate([np.concatenate([c[z], -s[z]])[None] if part == 0 else np.concatenate([s[z], c[z]])[None]
                         for z in range(d * PLANES, (d + 1) * PLANES)])
         for d in range(PW) for part in range(2)])
    high, low = split_table(rows)
    return np.concatenate([high, low, high], axis=1)


def collect_table():
    c, s = trig()
    full = np.zeros((512, 512))
    for d in range(PW):
        zs = np.arange(d * PLANES, (d + 1) * PLANES)
        at = d * ROWS
        full[:256, at:at + PLANES] = c[:, zs]
        full[:256, at + PLANES:at + ROWS] = s[:, zs]
        full[256:, at:at + PLANES] = -s[:, zs]
        full[256:, at + PLANES:at + ROWS] = c[:, zs]
    high, low = split_table(full)
    return np.concatenate([high, low, high], axis=1)


def iota(shape, dim):
    return lax.broadcasted_iota(jnp.int32, shape, dim).astype(F32)


def sort_rows(keys, values):
    keys = list(keys)
    values = [list(each) for each in values]
    sub = lax.broadcasted_iota(jnp.int32, (8, 128), 0)
    size = 2
    while size <= 128:
        dist = size // 2
        while dist >= 1:
            if dist < 16:
                for one in range(16):
                    if one & dist:
                        continue
                    two = one | dist
                    swap = keys[one] > keys[two]
                    if size < 16:
                        if one & size:
                            swap = keys[one] < keys[two]
                    elif size < 128:
                        swap = jnp.where((sub & (size // 16)) == 0, keys[one] - keys[two], keys[two] - keys[one]) > 0.0
                    for each in [keys] + values:
                        each[one], each[two] = (jnp.where(swap, each[two], each[one]),
                                                jnp.where(swap, each[one], each[two]))
            else:
                hop = dist // 16
                low = (sub & hop) == 0
                rising = (sub & (size // 16)) == 0 if size < 128 else jnp.full((8, 128), True)
                least = jnp.where(low == rising, 1.0, -1.0)

                def other(x):
                    return jnp.where(low, pltpu.roll(x, 8 - hop, 0), pltpu.roll(x, hop, 0))

                for one in range(16):
                    swap = (keys[one] - other(keys[one])) * least > 0.0
                    for each in [keys] + values:
                        each[one] = jnp.where(swap, other(each[one]), each[one])
            dist //= 2
        size *= 2
    return keys, values


def block_row(ref, block):
    at = pl.ds(block // 2, 1)
    half = 8 * (block % 2)
    return jnp.concatenate([ref[half + v, at, :] for v in range(8)], axis=1)


def key_parts(key):
    row = jnp.floor(key * (1.0 / 16384.0))
    rest = key - row * 16384.0
    return row, jnp.floor(rest * (1.0 / 128.0))


def fold(x):
    key = jnp.where(x == 128.0, 0.0, jnp.minimum(x, 256.0 - x))
    even = jnp.where(x == 128.0, -1.0, key)
    odd = jnp.where(x == 0.0, -1.0, key)
    return key, even, odd, jnp.where(x > 128.0, -1.0, 1.0)


def rank_of(owned):
    wide = jnp.broadcast_to(owned, (128, STICKS))
    down = jnp.transpose(wide)[:, :1]

    def sort_key(column):
        return fold(jnp.floor(column * (1.0 / GY)))[0] * 65536.0 + column

    key = sort_key(owned)
    key_down = sort_key(down)
    rank_row = jnp.sum(jnp.where(key_down < key, 1.0, 0.0), axis=0, keepdims=True)
    order = jnp.where(iota((STICKS, STICKS), 0) == rank_row, 1.0, 0.0)
    rank_col = jnp.sum(jnp.where(key < key_down, 1.0, 0.0), axis=1, keepdims=True)
    ordered = jnp.sum(jnp.where(iota((STICKS, STICKS), 1) == rank_col, down, 0.0), axis=0, keepdims=True)
    return order, ordered


def centred(values, length):
    return jnp.where(values < length // 2, values, values - length)


def owned_row(stick_ref):
    first = lax.axis_index("pw") * TILES
    return jnp.concatenate([stick_ref[pl.ds(first + t, 1), :] for t in range(TILES)], axis=1).astype(F32)


def kinetic_of(z, tile, lane, owned):
    x = jnp.floor(owned * (1.0 / GY))
    y = centred(owned - x * GY, GY)
    x = centred(x, GX)
    flat = x * x + y * y
    square = jnp.zeros((128, 128), F32)
    for t in range(TILES):
        line = jnp.broadcast_to(flat[:, t * 128:(t + 1) * 128], (128, 128))
        square = jnp.where(tile == t, jnp.take_along_axis(line, lane.astype(jnp.int32), axis=1), square)
    z = centred(z, GZ)
    return (square + z * z) * (KIN_MAX / 3.0 / 16384.0)


def spread_kernel(slot_ref, tile_ref, coef_ref, proj_hbm, stick_ref, table_hbm, out_ref, key_ref, kinetic_ref,
                  span_ref, order_ref, parts, acc, becp, table_ref, proj_buf, table_sem, proj_sems):
    step = pl.program_id(0)
    table_copy = pltpu.make_async_copy(table_hbm, table_ref, table_sem)

    def proj_copy(at):
        here = pl.ds(pl.multiple_of(at * KC, KC), KC)
        return pltpu.make_async_copy(proj_hbm.at[:, :, here], proj_buf.at[at], proj_sems.at[at])

    @pl.when(step == 0)
    def _():
        for at in range(COEFS // KC):
            proj_copy(at).start()
        table_copy.start()
        slot = slot_ref[...].astype(F32)
        z = jnp.floor((slot + 0.5) * (1.0 / STICKS))
        s = slot - z * STICKS
        tile = jnp.floor(s * (1.0 / 128.0))
        lane = s - tile * 128.0
        place = (tile * 256.0 + z) * 128.0 + lane
        kinetic = kinetic_of(z, tile, lane, owned_row(stick_ref))
        kinetic_ref[...] = kinetic
        for d in range(PW):
            here = slice(d * 4, d * 4 + 4)
            out_ref[d, 52:56, :] = kinetic[here]
            out_ref[d, 56:60, :] = tile_ref[0, here, :]
            out_ref[d, 60:64, :] = tile_ref[1, here, :]
        row = iota((128, 128), 0)
        array = jnp.floor(row * 0.125)
        key = place * 128.0 + (row - array * 8.0) * 16.0 + array

        def rows(x):
            return [x[v * 8:(v + 1) * 8] for v in range(16)]

        keys, (real, imag) = sort_rows(rows(key), [rows(tile_ref[0]), rows(tile_ref[1])])
        for v in range(16):
            key_ref[v] = keys[v]
            for at, part in enumerate(key_parts(keys[v]) + split(real[v]) + split(imag[v])):
                parts[at, v] = part.astype(F32)
        for block in range(16):
            half = 8 * (block % 2)
            at = block // 2
            first = jnp.min(key_parts(keys[half][at:at + 1])[0]).astype(jnp.int32)
            last = jnp.max(key_parts(keys[half + 7][at:at + 1])[0]).astype(jnp.int32)
            first = (first >> 4) << 4
            span_ref[0, block] = first
            span_ref[1, block] = lax.div(last - first, WINDOW) + 1
            span_ref[2, block] = WINDOWS[block]
            span_ref[3, block] = jnp.maximum(lax.div(last - first - WINDOWS[block] + WINDOW, WINDOW), 0)
        acc[...] = jnp.zeros_like(acc)
        becp[...] = jnp.zeros_like(becp)

    none = jnp.zeros((), BF16)
    lane_of = (iota((128, 1024), 0)).astype(BF16)
    row_of = (iota((WINDOW, 1024), 0) - 128.0).astype(BF16)

    def product(block, first):
        row, lane, re_hi, re_lo, im_hi, im_lo = [block_row(parts.at[at], block) for at in range(6)]
        hit = lane_of == lane.astype(BF16)
        placed = jnp.concatenate(
            [jnp.where(hit, part.astype(BF16), none) for part in (re_hi, im_hi, re_lo, im_lo)], axis=0)
        want = row - (first + 128).astype(F32)
        hot = jnp.where(row_of == want.astype(BF16), jnp.ones((), BF16), none)
        return mm(hot, placed, NT)

    def window(first):
        return pl.ds(pl.multiple_of(first, 16), WINDOW)

    blocks = [step * STEP_BLOCKS + at for at in range(STEP_BLOCKS)]
    for block in blocks:
        first = span_ref[0, block]
        acc[window(first), :] += product(block, first)

    @pl.when(sum(span_ref[1, block] for block in blocks) > STEP_BLOCKS)
    def _():
        def rest(at, carry):
            block = step * STEP_BLOCKS + at

            def more(p, inner):
                first = span_ref[0, block] + p * WINDOW
                acc[window(first), :] += product(block, first)
                return inner

            return lax.fori_loop(1, span_ref[1, block], more, carry)

        lax.fori_loop(0, STEP_BLOCKS, rest, 0)

    c_re = coef_ref[0]
    c_im = coef_ref[1]
    proj_copy(step).wait()
    p_re = proj_buf[step, 0]
    p_im = proj_buf[step, 1]
    real = p_re * c_re + p_im * c_im
    imag = p_re * c_im - p_im * c_re
    both = jnp.concatenate([real, imag], axis=0)
    total = both[:, :128]
    for at in range(128, KC, 128):
        total = total + both[:, at:at + 128]
    becp[...] += total

    @pl.when(step == pl.num_programs(0) - 1)
    def _():
        order, ordered = rank_of(owned_row(stick_ref))
        order_ref[...] = order.astype(BF16)
        sticks = jnp.concatenate(
            [jnp.concatenate([acc[t * 256:(t + 1) * 256, part * 128:(part + 1) * 128] for t in range(TILES)], axis=1)
             for part in range(4)], axis=0).astype(BF16)
        sticks = mm(sticks, order.astype(BF16), NT).astype(BF16)
        high = sticks[:512]
        low = sticks[512:]
        table_copy.wait()
        spread = mm(table_ref[...], jnp.concatenate([high, high, low], axis=0))
        spread = spread.reshape(PW, ROWS, STICKS)
        for t in range(TILES):
            out_ref[:, t * ROWS:(t + 1) * ROWS, :] = spread[:, :, t * 128:(t + 1) * 128]
        line = jnp.sum(jnp.transpose(becp[...]), axis=0, keepdims=True)
        extra = jnp.concatenate(
            [line] + [ordered[:, t * 128:(t + 1) * 128] for t in range(TILES)], axis=0)
        out_ref[:, TILES * ROWS:TILES * ROWS + 4, :] = jnp.broadcast_to(extra[None], (PW, 4, 128))


def spread_sticks(slot, coef, proj, stick):
    table = jnp.asarray(spread_table())
    return pl.pallas_call(
        spread_kernel,
        grid=(COEFS // KC,),
        in_specs=[
            pl.BlockSpec((128, 128), lambda i: (0, 0)),
            pl.BlockSpec((2, 128, 128), lambda i: (0, 0, 0)),
            pl.BlockSpec((2, 1, KC), lambda i: (0, 0, i)),
            pl.BlockSpec(memory_space=pl.ANY),
            pl.BlockSpec((PW * TILES, 128), lambda i: (0, 0)),
            pl.BlockSpec(memory_space=pl.ANY),
        ],
        out_specs=[
            pl.BlockSpec((PW, 64, 128), lambda i: (0, 0, 0)),
            pl.BlockSpec((16, 8, 128), lambda i: (0, 0, 0)),
            pl.BlockSpec((128, 128), lambda i: (0, 0)),
            pl.BlockSpec(memory_space=pltpu.SMEM),
            pl.BlockSpec((STICKS, STICKS), lambda i: (0, 0)),
        ],
        out_shape=[
            jax.ShapeDtypeStruct((PW, 64, 128), F32),
            jax.ShapeDtypeStruct((16, 8, 128), F32),
            jax.ShapeDtypeStruct((128, 128), F32),
            jax.ShapeDtypeStruct((4, 16), jnp.int32),
            jax.ShapeDtypeStruct((STICKS, STICKS), BF16),
        ],
        scratch_shapes=[
            pltpu.VMEM((6, 16, 8, 128), F32),
            pltpu.VMEM((SLOT_ROWS + WINDOW, 512), F32),
            pltpu.VMEM((128, 128), F32),
            pltpu.VMEM((512, 1536), BF16),
            pltpu.VMEM((COEFS // KC, 2, PROJ, KC), F32),
            pltpu.SemaphoreType.DMA,
            pltpu.SemaphoreType.DMA((COEFS // KC,)),
        ],
        compiler_params=pltpu.CompilerParams(vmem_limit_bytes=60 << 20),
        cost_estimate=pl.CostEstimate(flops=6 * 10 ** 9, bytes_accessed=12 << 20, transcendentals=0),
        name="spread_sticks",
    )(slot, coef.reshape(2, 128, 128), coef, proj, stick, table)


def swap_chunks(parts):
    parts = list(parts)
    chunk = lax.broadcasted_iota(jnp.int32, parts[0].shape, 1) // 16
    for bit in (1, 2, 4):
        here = (chunk & bit) == 0
        for a in range(8):
            if a & bit:
                continue
            one, two = parts[a], parts[a | bit]
            parts[a] = jnp.where(here, one, pltpu.roll(two, 16 * bit, 1))
            parts[a | bit] = jnp.where(here, pltpu.roll(one, 128 - 16 * bit, 1), two)
    return parts


def write_bounds(columns, bounds):
    chunk = jnp.floor(fold(jnp.floor(jnp.concatenate(columns, axis=0) * (1.0 / GY)))[0] * 0.125)
    first = jnp.broadcast_to(jnp.min(chunk, axis=1, keepdims=True), (GROUPS, 128))
    last = jnp.broadcast_to(jnp.max(chunk, axis=1, keepdims=True), (GROUPS, 128))
    lane = iota((GROUPS, 128), 1)
    start = jnp.sum(jnp.where(last < lane, 1.0, 0.0), axis=0, keepdims=True)
    end = jnp.sum(jnp.where(first <= lane, 1.0, 0.0), axis=0, keepdims=True)
    more = jnp.zeros((128 - GROUPS, 128), F32)
    first = jnp.transpose(jnp.concatenate([first, more], axis=0))[:1]
    last = jnp.transpose(jnp.concatenate([last, more], axis=0))[:1]
    count = jnp.where(lane[:1] < CHUNKS, end - start, 0.0)
    lines = [jnp.minimum(start, GROUPS - 1.0), end - start, first, last - first + 1.0,
             jnp.broadcast_to(jnp.max(count, axis=1, keepdims=True), (1, 128)),
             jnp.broadcast_to(jnp.max(last - first + 1.0, axis=1, keepdims=True), (1, 128)), jnp.zeros((2, 128), F32)]
    bounds[...] = jnp.concatenate(lines, axis=0).astype(jnp.int32)


def field_kernel(recv_ref, field_hbm, y_in_hbm, y_out_hbm, x_in_hbm, x_out_hbm, out_ref,
                 wide, hot, keys, signs, grid, done, sticks, field_ref, y_in_ref, y_out_ref, x_in_ref, x_out_ref,
                 bounds, range_ref, sems, range_sem):
    copies = [pltpu.make_async_copy(source, target, sems.at[at]) for at, (source, target) in enumerate((
        (field_hbm, field_ref), (y_in_hbm, y_in_ref), (y_out_hbm, y_out_ref),
        (x_in_hbm, x_in_ref), (x_out_hbm, x_out_ref)))]
    for copy in copies:
        copy.start()
    cells = []
    for g in range(4):
        mixed = swap_chunks([recv_ref[g * 8 + i, TILES * ROWS:TILES * ROWS + 8, :] for i in range(8)])
        cells.append(mixed)
    columns = [jnp.concatenate([cells[g][q % 8][1 + q // 8:2 + q // 8] for g in range(4)], axis=1)
               for q in range(GROUPS)]
    write_bounds(columns, bounds)
    range_copy = pltpu.make_async_copy(bounds, range_ref, range_sem)
    range_copy.start()
    one_hot = iota((128, 512), 0).astype(BF16)
    zero = jnp.zeros((), BF16)
    for t in range(TILES):
        mixed = [swap_chunks([recv_ref[g * 8 + i, t * ROWS:(t + 1) * ROWS, :] for i in range(8)]) for g in range(4)]
        for c in range(8):
            q = t * 8 + c
            values = jnp.concatenate([mixed[g][c] for g in range(4)], axis=1)
            high, low = split(values)
            both = jnp.concatenate([high.astype(F32), low.astype(F32)], axis=0)
            wide[q] = jnp.broadcast_to(both[:, None, :], (2 * ROWS, 16, 512)).astype(BF16)
            column = columns[q]
            x = jnp.floor(column * (1.0 / GY))
            y = column - x * GY
            _, even, odd, sign = fold(x)
            upper = iota((16, 512), 0) < 8.0
            keys[q] = jnp.where(upper, even, odd).astype(BF16)
            signs[q] = jnp.where(upper, 1.0, sign).astype(BF16)
            _, even, odd, sign = fold(y)
            hot[q, :128, :] = jnp.where(one_hot == even.astype(BF16), jnp.ones((), BF16), zero)
            hot[q, 128:, :] = jnp.where(one_hot == odd.astype(BF16), sign.astype(BF16), zero)
    for q in range(GROUPS, GROUPS + NQ):
        wide[q] = jnp.zeros((2 * ROWS, 16, 512), BF16)
        hot[q] = jnp.zeros((256, 512), BF16)
        keys[q] = jnp.full((16, 512), -1.0, BF16)
        signs[q] = jnp.zeros((16, 512), BF16)
    done[:, GX:, :] = jnp.zeros((ROWS, 16 * (NCH - 1), 512), BF16)

    step_of = iota((16, 512), 0)
    step_of = jnp.where(step_of < 8.0, step_of, step_of - 8.0)

    def place(chunk, first, groups):
        want = (step_of + (chunk * 8).astype(F32)).astype(BF16)
        masked = []
        for j in range(groups):
            mine = jnp.where(keys[first + j] == want, signs[first + j], zero)
            masked.append((wide[first + j] * mine[None]).reshape(2 * ROWS * 16, 512))
        got = mm(jnp.concatenate(masked, axis=1),
                 jnp.concatenate([hot[first + j] for j in range(groups)], axis=1), NT)
        got = got.reshape(2, ROWS, 16, 256)
        return got[0] + got[1]

    def rows_of(chunk):
        return pl.ds(pl.multiple_of(chunk * 16, 16), 16)

    def place_first(step, carry):
        chunks = [step * PLACE_UNROLL + at for at in range(PLACE_UNROLL)]
        most = functools.reduce(jnp.maximum, [range_ref[1, chunk] for chunk in chunks])

        def run(groups):
            for chunk in chunks:
                grid[:, rows_of(chunk), :] = place(chunk, range_ref[0, chunk], groups)

        pl.when(most <= NQ)(lambda: run(NQ))
        pl.when(most > NQ)(lambda: run(NQ + 1))
        return carry

    def place_rest(chunk, carry):
        def more(p, inner):
            grid[:, rows_of(chunk), :] += place(chunk, range_ref[0, chunk] + p, 1)
            return inner

        return lax.fori_loop(NQ + 1, range_ref[1, chunk], more, carry)

    range_copy.wait()
    lax.fori_loop(0, CHUNKS // PLACE_UNROLL, place_first, 0)

    @pl.when(range_ref[4, 0] > NQ + 1)
    def _():
        lax.fori_loop(0, CHUNKS, place_rest, 0)

    row = lax.broadcasted_iota(jnp.int32, (256, 256), 0)
    lane = lax.broadcasted_iota(jnp.int32, (256, 256), 1)
    even_x = ((row & 8) == 0) | (row == 8)
    even_y = lane <= 128

    def along_y(re, im, table):
        high, low = split(jnp.concatenate([re, im], axis=0))
        got = mm(jnp.concatenate([high, high, low], axis=1), table[...])
        return got[:256], got[256:]

    def along_x(re, im, table):
        high, low = split(jnp.concatenate([re, im], axis=1))
        got = mm(table[...], jnp.concatenate([high, high, low], axis=0))
        return got[:, :256], got[:, 256:]

    def plane(zz):
        re = grid[zz]
        im = grid[PLANES + zz]
        re, im = along_y(jnp.where(even_y, re, -im), jnp.where(even_y, im, re), y_in_ref)
        re, im = along_x(jnp.where(even_x, re, -im), jnp.where(even_x, im, re), x_in_ref)
        field = field_ref[zz]
        re, im = along_x(re * field, im * field, x_out_ref)
        re, im = along_y(jnp.where(even_x, re, im), jnp.where(even_x, im, -re), y_out_ref)
        high, low = split(jnp.where(even_y, re, im))
        done[zz, :GX, :256] = high
        done[zz, :GX, 256:] = low
        high, low = split(jnp.where(even_y, im, -re))
        done[PLANES + zz, :GX, :256] = high
        done[PLANES + zz, :GX, 256:] = low

    def planes(pair, carry):
        for at in range(PAIR):
            plane(pair * PAIR + at)
        return carry

    for copy in copies:
        copy.wait()
    lax.fori_loop(0, PLANES // PAIR, planes, 0)

    def pick(q, first, chunks):
        both = jnp.concatenate([hot[q], hot[q]], axis=0)
        key = keys[q].astype(F32)
        sign = signs[q].astype(F32)
        here = pl.ds(pl.multiple_of(first * 16, 16), 16 * chunks)
        lines = done[:, here, :].reshape(ROWS * 16 * chunks, 512)
        got = mm(lines, both).reshape(ROWS, 2 * chunks, 8, 512)
        total = None
        for j in range(chunks):
            want = step_of + ((first + j) * 8).astype(F32)
            mine = jnp.where(key == want, sign, 0.0)
            part = got[:, 2 * j] * mine[None, :8] + got[:, 2 * j + 1] * mine[None, 8:]
            total = part if total is None else total + part
        return jnp.sum(total, axis=1)

    def pick_first(step, carry):
        for at in range(PICK_UNROLL):
            q = step * PICK_UNROLL + at
            sticks[q] = pick(q, range_ref[2, q], NCH)
        return carry

    def pick_rest(q, carry):
        def more(p, inner):
            sticks[q] += pick(q, range_ref[2, q] + p, 1)
            return inner

        return lax.fori_loop(NCH, range_ref[3, q], more, carry)

    lax.fori_loop(0, GROUPS // PICK_UNROLL, pick_first, 0)

    @pl.when(range_ref[5, 0] > NCH)
    def _():
        lax.fori_loop(0, GROUPS, pick_rest, 0)

    for t in range(TILES):
        for g in range(4):
            mixed = swap_chunks([sticks[t * 8 + c, :, g * 128:(g + 1) * 128] for c in range(8)])
            for i in range(8):
                out_ref[g * 8 + i, t * ROWS:(t + 1) * ROWS, :] = mixed[i]


def apply_field(recv, field):
    vmem = pl.BlockSpec(memory_space=pltpu.VMEM)
    return pl.pallas_call(
        field_kernel,
        in_specs=[vmem] + [pl.BlockSpec(memory_space=pl.ANY)] * 5,
        out_specs=vmem,
        out_shape=jax.ShapeDtypeStruct((PW, 48, 128), F32),
        scratch_shapes=[
            pltpu.VMEM((GROUPS + NQ, 2 * ROWS, 16, 512), BF16),
            pltpu.VMEM((GROUPS + NQ, 256, 512), BF16),
            pltpu.VMEM((GROUPS + NQ, 16, 512), BF16),
            pltpu.VMEM((GROUPS + NQ, 16, 512), BF16),
            pltpu.VMEM((ROWS, GX, GY), F32),
            pltpu.VMEM((ROWS, GX + 16 * (NCH - 1), 512), BF16),
            pltpu.VMEM((GROUPS, ROWS, 512), F32),
            pltpu.VMEM((PLANES, GX, GY), F32),
            pltpu.VMEM((768, 256), BF16),
            pltpu.VMEM((768, 256), BF16),
            pltpu.VMEM((256, 768), BF16),
            pltpu.VMEM((256, 768), BF16),
            pltpu.VMEM((8, 128), jnp.int32),
            pltpu.SMEM((8, 128), jnp.int32),
            pltpu.SemaphoreType.DMA((5,)),
            pltpu.SemaphoreType.DMA,
        ],
        compiler_params=pltpu.CompilerParams(vmem_limit_bytes=48 << 20),
        cost_estimate=pl.CostEstimate(flops=35 * 10 ** 9, bytes_accessed=8 << 20, transcendentals=0),
        name="apply_field",
    )(recv, field, *plane_tables())


def add_pairs(span, own_ref, refs, worked_ref, total, small, becp_ref):
    worked = worked_ref[...].reshape(span * TILES, 2, PLANES, 128)
    w_re = worked[:, 0]
    w_im = worked[:, 1]
    upper = lax.broadcasted_iota(jnp.int32, (span * 8, 128), 0) % 8 < 4
    mine = own_ref[:, 56:, :].reshape(span * 8, 128)
    weight = own_ref[:, 48:56, :].reshape(span * 8, 128)

    def halves(x):
        return pltpu.roll(x.reshape(span, 8, 128), 4, 1).reshape(span * 8, 128)

    turned = jnp.where(upper, halves(mine), -halves(mine))
    weight = jnp.where(upper, halves(weight), weight)
    for a, ref in refs.items():
        lines = ref[:, :TILES * ROWS, :].reshape(span * TILES, 2, PLANES, 128)
        a_re = lines[:, 0]
        a_im = lines[:, 1]
        total[a] += jnp.sum(a_re * w_re + a_im * w_im, axis=0)
        total[4 + a] += jnp.sum(a_re * w_im - a_im * w_re, axis=0)
        becp_ref[a] += jnp.sum(ref[:, 48:56, :], axis=0)
        coef = ref[:, 56:, :].reshape(span * 8, 128)
        real = coef * mine
        imag = coef * turned
        for at, value in ((a, real * weight), (4 + a, imag * weight), (8 + a, real), (12 + a, imag)):
            small[at] += jnp.sum(value.reshape(span, 8, 128), axis=0)


def first_kernel(own_ref, one_ref, two_ref, worked_ref, total, small, becp_ref):
    @pl.when(pl.program_id(0) == 0)
    def _():
        total[...] = jnp.zeros_like(total)
        small[...] = jnp.zeros_like(small)
        becp_ref[...] = jnp.zeros_like(becp_ref)

    add_pairs(PW // GRAM_STEPS, own_ref, {0: own_ref, 1: one_ref, 2: two_ref}, worked_ref, total, small, becp_ref)


def last_kernel(total_ref, small_ref, sums_ref, own_ref, three_ref, worked_ref, out_ref, becp_ref, total, small):
    step = pl.program_id(0)

    @pl.when(step == 0)
    def _():
        total[...] = total_ref[...]
        small[...] = small_ref[...]
        becp_ref[...] = sums_ref[...]

    span = PW // GRAM_STEPS
    here = pl.ds(pl.multiple_of(step * span, span), span)
    out_ref[here, :TILES * ROWS, :] = worked_ref[...]
    add_pairs(span, own_ref, {3: three_ref}, worked_ref, total, small, becp_ref)

    @pl.when(step == pl.num_programs(0) - 1)
    def _():
        scale = 1.0 / (GX * GY * GZ)
        lines = [jnp.sum(small[at] + total[at] * scale, axis=0, keepdims=True) for at in range(8)]
        lines += [jnp.sum(small[at], axis=0, keepdims=True) for at in range(8, 16)]
        lines = jnp.concatenate(lines + [jnp.zeros((112, 128), F32)], axis=0)
        line = jnp.sum(jnp.transpose(lines), axis=0, keepdims=True)
        out_ref[:, TILES * ROWS:, :] = jnp.broadcast_to(line[None], (PW, 8, 128))


SUM_SHAPES = ((8, PLANES, 128), (16, 8, 128), (4, 8, 128))


def gram_first(sticks, worked):
    span = PW // GRAM_STEPS
    return pl.pallas_call(
        first_kernel,
        grid=(GRAM_STEPS,),
        in_specs=[pl.BlockSpec((span, 64, 128), lambda i: (i, 0, 0))] * 3 + [
            pl.BlockSpec((span, 48, 128), lambda i: (i, 0, 0)),
        ],
        out_specs=[pl.BlockSpec(shape, lambda i: (0, 0, 0)) for shape in SUM_SHAPES],
        out_shape=[jax.ShapeDtypeStruct(shape, F32) for shape in SUM_SHAPES],
        compiler_params=pltpu.CompilerParams(vmem_limit_bytes=16 << 20),
        cost_estimate=pl.CostEstimate(flops=10 ** 7, bytes_accessed=5 << 20, transcendentals=0),
        name="gram_first",
    )(*sticks, worked)


def gram_last(sums, recv, three, worked):
    span = PW // GRAM_STEPS
    return pl.pallas_call(
        last_kernel,
        grid=(GRAM_STEPS,),
        in_specs=[pl.BlockSpec(shape, lambda i: (0, 0, 0)) for shape in SUM_SHAPES]
        + [pl.BlockSpec((span, 64, 128), lambda i: (i, 0, 0))] * 2
        + [pl.BlockSpec((span, 48, 128), lambda i: (i, 0, 0))],
        out_specs=[pl.BlockSpec((PW, 56, 128), lambda i: (0, 0, 0)), pl.BlockSpec((4, 8, 128), lambda i: (0, 0, 0))],
        out_shape=[jax.ShapeDtypeStruct((PW, 56, 128), F32), jax.ShapeDtypeStruct((4, 8, 128), F32)],
        scratch_shapes=[pltpu.VMEM((8, PLANES, 128), F32), pltpu.VMEM((16, 8, 128), F32)],
        compiler_params=pltpu.CompilerParams(vmem_limit_bytes=16 << 20),
        cost_estimate=pl.CostEstimate(flops=10 ** 7, bytes_accessed=4 << 20, transcendentals=0),
        name="gram_last",
    )(*sums, recv, three, worked)


def base_kernel(kinetic_ref, coef_ref, proj_ref, matrix_ref, becp_ref, out_ref, far_ref, weight):
    @pl.when(pl.program_id(0) == 0)
    def _():
        matrix = matrix_ref[...]
        lines = jnp.concatenate([becp_ref[a, :1, :] for a in range(4)], axis=0)
        w_re = jnp.sum(matrix * lines[:1, :PROJ], axis=1, keepdims=True)
        w_im = jnp.sum(matrix * lines[:1, PROJ:], axis=1, keepdims=True)
        weight[0] = jnp.broadcast_to(w_re, (PROJ, 128))
        weight[1] = jnp.broadcast_to(w_im, (PROJ, 128))
        down = jnp.transpose(jnp.concatenate([lines, jnp.zeros((124, 128), F32)], axis=0))
        far_re = jnp.sum(down[:PROJ] * w_re + down[PROJ:] * w_im, axis=0, keepdims=True)
        far_im = jnp.sum(down[:PROJ] * w_im - down[PROJ:] * w_re, axis=0, keepdims=True)
        far = jnp.broadcast_to(far_re, (8, 128)) + pltpu.roll(jnp.broadcast_to(far_im, (8, 128)), 4, 1)
        far_ref[...] = far

    kinetic = kinetic_ref[...]
    p_re = proj_ref[0]
    p_im = proj_ref[1]
    w_re = weight[0][:, :1]
    w_im = weight[1][:, :1]
    far_re = jnp.sum(p_re * w_re - p_im * w_im, axis=0, keepdims=True)
    far_im = jnp.sum(p_re * w_im + p_im * w_re, axis=0, keepdims=True)
    out_ref[0] = kinetic * coef_ref[0] + far_re
    out_ref[1] = kinetic * coef_ref[1] + far_im


def base_part(kinetic, coef, proj, matrix, becp):
    return pl.pallas_call(
        base_kernel,
        grid=(COEFS // KC,),
        in_specs=[
            pl.BlockSpec((1, KC), lambda i: (0, i)),
            pl.BlockSpec((2, 1, KC), lambda i: (0, 0, i)),
            pl.BlockSpec((2, PROJ, KC), lambda i: (0, 0, i)),
            pl.BlockSpec((PROJ, PROJ), lambda i: (0, 0)),
            pl.BlockSpec((4, 8, 128), lambda i: (0, 0, 0)),
        ],
        out_specs=[pl.BlockSpec((2, 1, KC), lambda i: (0, 0, i)), pl.BlockSpec((8, 128), lambda i: (0, 0))],
        out_shape=[jax.ShapeDtypeStruct((2, 1, COEFS), F32), jax.ShapeDtypeStruct((8, 128), F32)],
        scratch_shapes=[pltpu.VMEM((2, PROJ, 128), F32)],
        compiler_params=pltpu.CompilerParams(vmem_limit_bytes=16 << 20),
        cost_estimate=pl.CostEstimate(flops=10 ** 7, bytes_accessed=10 << 20, transcendentals=0),
        name="base_part",
    )(kinetic, coef, proj, matrix, becp)


def collect_kernel(span_ref, key_ref, recv_ref, order_ref, table_ref, base_ref, far_ref, out_ref,
                   energy_ref, overlap_ref, values, found_re, found_im):
    total = jnp.sum(recv_ref[:, TILES * ROWS:, :], axis=0) + far_ref[...]
    band = lax.axis_index("band")
    lane = lax.broadcasted_iota(jnp.int32, (8, 128), 1)
    for bit in (1, 2):
        swapped = jnp.where((lane & bit) == 0, pltpu.roll(total, 128 - bit, 1), pltpu.roll(total, bit, 1))
        total = jnp.where((band & bit) != 0, swapped, total)
    for ri in range(2):
        energy_ref[ri] = total[:1, ri * 4:ri * 4 + 4]
        overlap_ref[ri] = total[:1, 8 + ri * 4:12 + ri * 4]

    order = order_ref[...]
    lines = jnp.concatenate(
        [recv_ref[:, t * ROWS:(t + 1) * ROWS, :].reshape(512, 128) for t in range(TILES)], axis=1)
    high, low = split(lines)
    back = mm(table_ref[...], jnp.concatenate([high, high, low], axis=0))
    for at, part in enumerate(split(back)):
        part = mm(part, order).astype(BF16)
        for ri in range(2):
            for t in range(TILES):
                values[ri, t * 256:(t + 1) * 256, at * 128:(at + 1) * 128] = part[
                    ri * 256:(ri + 1) * 256, t * 128:(t + 1) * 128]
    values[:, SLOT_ROWS:, :] = jnp.zeros((2, WINDOW, 256), BF16)

    lane_of = iota((128, 1024), 0).astype(BF16)
    def fetch(block, first, wide):
        row, lane = key_parts(block_row(key_ref, block))
        hit = jnp.where(lane_of == lane.astype(BF16), jnp.ones((), BF16), jnp.zeros((), BF16))
        here = pl.ds(pl.multiple_of(first, 16), wide)
        got = mm(jnp.concatenate([values[0, here, :], values[1, here, :]], axis=0), jnp.concatenate([hit, hit], axis=0))
        mine = iota((wide, 1024), 0) == row - first.astype(F32)
        return (jnp.sum(jnp.where(mine, got[:wide], 0.0), axis=0, keepdims=True),
                jnp.sum(jnp.where(mine, got[wide:], 0.0), axis=0, keepdims=True))

    def put(block, pair, old):
        at = pl.ds(block // 2, 1)
        half = 8 * (block % 2)
        for ref, line in zip((found_re, found_im), pair):
            for v in range(8):
                piece = line[:, v * 128:(v + 1) * 128]
                ref[half + v, at, :] = ref[half + v, at, :] + piece if old else piece

    for block in range(16):
        put(block, fetch(block, span_ref[0, block], WINDOWS[block]), False)

    @pl.when(sum(span_ref[3, block] for block in range(16)) > 0)
    def _():
        def rest(block, carry):
            def more(p, inner):
                first = span_ref[0, block] + span_ref[2, block] + p * WINDOW
                put(block, fetch(block, first, WINDOW), True)
                return inner

            return lax.fori_loop(0, span_ref[3, block], more, carry)

        lax.fori_loop(0, 16, rest, 0)

    scale = 1.0 / (GX * GY * GZ)
    home = []
    for v in range(16):
        key = key_ref[v]
        home.append(key - jnp.floor(key * (1.0 / 128.0)) * 128.0)
    _, (real, imag) = sort_rows(home, [[found_re[v] for v in range(16)], [found_im[v] for v in range(16)]])
    for v in range(16):
        here = slice(v * 8, (v + 1) * 8)
        out_ref[0, here, :] = base_ref[0, here, :] + real[v] * scale
        out_ref[1, here, :] = base_ref[1, here, :] + imag[v] * scale


def collect(span, key, recv, order, base, far):
    vmem = pl.BlockSpec(memory_space=pltpu.VMEM)
    return pl.pallas_call(
        collect_kernel,
        in_specs=[pl.BlockSpec(memory_space=pltpu.SMEM)] + [vmem] * 6,
        out_specs=[vmem, vmem, vmem],
        out_shape=[
            jax.ShapeDtypeStruct((2, 128, 128), F32),
            jax.ShapeDtypeStruct((2, 1, 4), F32),
            jax.ShapeDtypeStruct((2, 1, 4), F32),
        ],
        scratch_shapes=[
            pltpu.VMEM((2, SLOT_ROWS + WINDOW, 256), BF16),
            pltpu.VMEM((16, 8, 128), F32),
            pltpu.VMEM((16, 8, 128), F32),
        ],
        compiler_params=pltpu.CompilerParams(vmem_limit_bytes=32 << 20),
        cost_estimate=pl.CostEstimate(flops=6 * 10 ** 9, bytes_accessed=4 << 20, transcendentals=0),
        name="collect",
    )(span, key, recv, order, jnp.asarray(collect_table()), base, far)


def local(wave_coef, projector, potential, grid_slot, stick_column, proj_atom, coupling):
    stick = stick_column.reshape(PW * TILES, 128)
    sent, key, kinetic, span, order = spread_sticks(grid_slot.reshape(128, 128), wave_coef, projector, stick)
    recv = lax.all_to_all(sent, "pw", split_axis=0, concat_axis=0, tiled=True)
    one = lax.ppermute(recv, "band", [(b, b ^ 1) for b in range(4)])
    two = lax.ppermute(recv, "band", [(b, b ^ 2) for b in range(4)])
    worked = apply_field(recv, potential)
    late, _ = lax.optimization_barrier((two, worked))
    three = lax.ppermute(late, "band", [(b, b ^ 1) for b in range(4)])
    payload, becp = gram_last(gram_first((recv, one, two), worked), recv, three, worked)
    returned = lax.all_to_all(payload, "pw", split_axis=0, concat_axis=0, tiled=True)

    same_atom = proj_atom[:, None] == proj_atom[None, :]
    matrix = jnp.where(same_atom, 0.5 * (coupling + coupling.T), 0.0)
    base, far = base_part(kinetic.reshape(1, COEFS), wave_coef, projector, matrix, becp)
    applied, energy, overlap = collect(span, key, returned, order, base.reshape(2, 128, 128), far)
    return applied.reshape(2, 1, COEFS), energy.transpose(0, 2, 1), overlap.transpose(0, 2, 1)


def solution(mesh):
    in_specs = (
        P(None, "band", "pw"),
        P(None, None, "pw"),
        P("pw", None, None),
        P("pw"),
        P(),
        P(),
        P(),
    )
    out_specs = (P(None, "band", "pw"), P(None, None, "band"), P(None, None, "band"))
    return jax.shard_map(local, mesh=mesh, in_specs=in_specs, out_specs=out_specs, check_vma=False)
```
